512 devices in a mesh: ctx: 16 (over z_lo, x), sample: 32 (over z_hi, y, core).
Axes of the slice: x: 4, y: 4, z: 16 (z_hi: 4, z_lo: 4; z = z_hi * 4 + z_lo), core: 2. Of those that a mesh axis runs over, the one named last changes fastest.
Arguments:
- prompt_latent: bfloat16 [2, 4096, 576], P(None, ('ctx', 'sample')), may hold values from -8 to 8
- suffix_latent: bfloat16 [32, 256, 576], P('sample', 'ctx'), may hold values from -6 to 6
- queries: bfloat16 [32, 5, 128, 192], P(None, None, 'sample'), may hold values from -700 to 700
- key_up: bfloat16 [128, 128, 512], P('sample'), may hold values from -0.5 to 0.5
- value_up: bfloat16 [128, 512, 128], P('sample'), may hold values from -0.25 to 0.25
- out_grad: bfloat16 [32, 5, 128, 128], P(None, None, 'sample'), may hold values from -6 to 6
- fork_prompt: int32 [32], replicated, may hold values from 0 to 1, as said below
- suffix_length: int32 [32], replicated, may hold values from 5 to 256, as said below
Outputs:
- prompt_grad: float32 [2, 4096, 576], P(None, ('ctx', 'sample'))
- suffix_grad: float32 [32, 256, 576], P('sample', 'ctx')
- query_grad: float32 [32, 5, 128, 192], P(None, None, 'sample')
- key_up_grad: float32 [128, 128, 512], P('sample')
- value_up_grad: float32 [128, 512, 128], P('sample')
The draws below stay inside these ranges and needn't reach their ends.
Inputs may be any that keep to these rules, and one draw needn't show every extreme that they name: `fork_prompt`: each prompt has exactly 16 forks. `suffix_length`: the largest suffix length is 256 in every draw.
All inputs are finite; a program needn't handle non-finite values.
Results may differ from the reference program's by a relative error of at most 0.03.
Values may be sent and summed in bfloat16 or wider, within the bound.
A program may use at most 128 MiB of HBM per device.

```python
import jax
import jax.numpy as jnp
from jax import lax

LATENT = 512
ROPE = 64
NOPE = 128
VHEAD = 128
HEADS = 128
PROMPTS = 2
FORKS = 32
RECOMP = 5
PLEN = 4096
SUF = 256


def rope_base(key):
    return jnp.clip(jax.random.normal(key, (PROMPTS, PLEN, ROPE), jnp.float32), -6.0, 6.0)


def draw_prompt_latent(key, part):
    base = rope_base(key)
    key = jax.random.fold_in(key, 11)
    latent = jnp.clip(jax.random.normal(key, (PROMPTS, PLEN, LATENT), jnp.float32), -6.0, 6.0)
    return jnp.concatenate([latent, base], -1).astype(jnp.bfloat16)


def draw_queries(key, part):
    key = jax.random.fold_in(key, 23)
    split_keys = jax.random.split(key, 1)
    shape = (FORKS, RECOMP, HEADS, NOPE + ROPE)
    values = jnp.clip(jax.random.normal(split_keys[0], shape, jnp.float32), -6.0, 6.0)
    return values.astype(jnp.bfloat16)


def draw_fork_prompt(key, part):
    key = jax.random.fold_in(key, 5)
    return (jax.random.permutation(key, FORKS) % PROMPTS).astype(jnp.int32)


def draw_suffix_length(key, part):
    key = jax.random.fold_in(key, 7)
    split_keys = jax.random.split(key, 2)
    drawn = jax.random.randint(split_keys[0], (FORKS,), RECOMP, SUF + 1)
    chosen = jax.random.randint(split_keys[1], (), 0, FORKS)
    return jnp.where(jnp.arange(FORKS) == chosen, SUF, drawn).astype(jnp.int32)


def block_levels(own_key, shape, shards, smallest, high):
    def one(position, shards_of):
        heights = jax.random.uniform(jax.random.fold_in(jax.random.fold_in(own_key, 6), position), (shards_of,), jnp.float32, smallest / len(shards), high / len(shards))
        return jnp.repeat(jnp.exp(heights), shape[position] // shards_of).reshape((-1,) + (1,) * (len(shape) - position - 1))

    factor_of = one(*shards[0])
    for cut in shards[1:]:
        factor_of = factor_of * one(*cut)
    return factor_of


def bell_draw(stream_key, dims, scale, most, cuts=(), kind=jnp.bfloat16):
    gain = block_levels(stream_key, dims, cuts, -0.22, 0.18) if cuts else 1.0
    values = jax.random.normal(stream_key, dims, jnp.float32) * scale * gain
    return jnp.minimum(jnp.maximum(values, -most), most).astype(kind)


def setup_inputs(seed: int = 0) -> dict:
    seeds = jax.random.split(jax.random.key(seed), 9)
    return {
        "prompt_latent": draw_prompt_latent(jax.random.fold_in(seeds[8], 71), 0),
        "suffix_latent": bell_draw(seeds[1], (FORKS, SUF, LATENT + ROPE), 1.0, 6.0, ((0, 32), (1, 16))),
        "queries": draw_queries(jax.random.fold_in(seeds[8], 71), 0),
        "key_up": bell_draw(seeds[3], (HEADS, NOPE, LATENT), NOPE ** -0.5, 0.5, ((0, 32),)),
        "value_up": bell_draw(seeds[4], (HEADS, LATENT, VHEAD), LATENT ** -0.5, 0.25, ((0, 32),)),
        "out_grad": bell_draw(seeds[5], (FORKS, RECOMP, HEADS, VHEAD), 1.0, 6.0, ((2, 32),)),
        "fork_prompt": draw_fork_prompt(jax.random.fold_in(seeds[8], 71), 0),
        "suffix_length": draw_suffix_length(jax.random.fold_in(seeds[8], 71), 0),
    }


NEG_FILL = -1.0e30


def reference(prompt_latent, suffix_latent, queries, key_up, value_up, out_grad, fork_prompt, suffix_length):
    score_scale = (NOPE + ROPE) ** -0.5
    head_count = queries.shape[2]
    row_count = RECOMP * head_count
    full_width = LATENT + ROPE
    total_keys = PLEN + SUF
    highest = lax.Precision.HIGHEST
    query_lat = jnp.einsum("frhn,hnl->frhl", queries[..., :NOPE].astype(jnp.float32), key_up.astype(jnp.float32)).astype(jnp.bfloat16)
    absorbed = jnp.concatenate([query_lat, queries[..., NOPE:]], -1)
    latent_grad = jnp.einsum("frhv,hlv->frhl", out_grad.astype(jnp.float32), value_up.astype(jnp.float32)).astype(jnp.bfloat16)
    key_up32 = key_up.astype(jnp.float32)
    key_pos = jnp.arange(total_keys, dtype=jnp.int32)
    row_step = jnp.arange(row_count, dtype=jnp.int32) // head_count

    def per_fork(carry, inputs):
        prompt_acc, key_up_acc, value_up_acc = carry
        fork_query, fork_lgrad, fork_out, fork_nope, fork_suffix, prompt_id, length = inputs
        prompt_rows = lax.dynamic_index_in_dim(prompt_latent, prompt_id, 0, keepdims=False)
        key_rows = jnp.concatenate([prompt_rows, fork_suffix], 0)
        flat_query = fork_query.reshape(row_count, full_width)
        scores = jnp.dot(flat_query, key_rows.T, preferred_element_type=jnp.float32) * score_scale
        visible = (key_pos[None, :] < PLEN) | (key_pos[None, :] - PLEN <= length - RECOMP + row_step[:, None])
        scores = jnp.where(visible, scores, NEG_FILL)
        peak_val = jnp.max(scores, -1, keepdims=True)
        log_sum = peak_val + jnp.log(jnp.sum(jnp.exp(scores - peak_val), -1, keepdims=True))
        probs = jnp.where(visible, jnp.exp(scores - log_sum), 0.0)
        values32 = key_rows[:, :LATENT].astype(jnp.float32)
        latent_out = jnp.dot(probs, values32, precision=highest)
        flat_lgrad = fork_lgrad.reshape(row_count, LATENT)
        prob_grad = jnp.dot(flat_lgrad, key_rows[:, :LATENT].T, preferred_element_type=jnp.float32)
        row_delta = jnp.sum(flat_lgrad.astype(jnp.float32) * latent_out, -1, keepdims=True)
        score_grad = (probs * (prob_grad - row_delta) * score_scale).astype(jnp.bfloat16)
        absorbed_grad = jnp.dot(score_grad, key_rows, preferred_element_type=jnp.float32)
        key_grad = jnp.dot(score_grad.T, flat_query, preferred_element_type=jnp.float32)
        value_grad = jnp.dot(probs.astype(jnp.bfloat16).T, flat_lgrad, preferred_element_type=jnp.float32)
        key_grad = jnp.concatenate([key_grad[:, :LATENT] + value_grad, key_grad[:, LATENT:]], -1)
        current = lax.dynamic_index_in_dim(prompt_acc, prompt_id, 0, keepdims=False)
        prompt_acc = lax.dynamic_update_index_in_dim(prompt_acc, current + key_grad[:PLEN], prompt_id, 0)
        grad_shaped = absorbed_grad.reshape(RECOMP, head_count, full_width)
        grad_nope = jnp.einsum("rhl,hnl->rhn", grad_shaped[..., :LATENT], key_up32, precision=highest)
        fork_qgrad = jnp.concatenate([grad_nope, grad_shaped[..., LATENT:]], -1)
        key_up_acc = key_up_acc + jnp.einsum("rhn,rhl->hnl", fork_nope.astype(jnp.float32), grad_shaped[..., :LATENT], precision=highest)
        value_up_acc = value_up_acc + jnp.einsum("rhl,rhv->hlv", latent_out.reshape(RECOMP, head_count, LATENT), fork_out.astype(jnp.float32), precision=highest)
        return (prompt_acc, key_up_acc, value_up_acc), (key_grad[PLEN:], fork_qgrad)

    start = (jnp.zeros((PROMPTS, PLEN, full_width), jnp.float32),
             jnp.zeros((head_count, NOPE, LATENT), jnp.float32),
             jnp.zeros((head_count, LATENT, VHEAD), jnp.float32))
    inputs = (absorbed, latent_grad, out_grad, queries[..., :NOPE], suffix_latent,
              fork_prompt.astype(jnp.int32), suffix_length.astype(jnp.int32))
    (prompt_grad, key_up_grad, value_up_grad), (suffix_grad, query_grad) = lax.scan(per_fork, start, inputs)
    return prompt_grad, suffix_grad, query_grad, key_up_grad, value_up_grad
```

```python
import functools

import jax
import jax.numpy as jnp
from jax import lax
from jax.experimental import pallas as pl
from jax.experimental.pallas import tpu as pltpu
from jax.sharding import PartitionSpec as P

MESH = pl.DeviceIdType.MESH
F32 = jnp.float32
BF16 = jnp.bfloat16
HIDDEN = -1e30

ZL, X, ZH, Y, CORE = 4, 4, 4, 4, 2
FORKS, RECOMP, HEADS = 32, 5, 4
NOPE, ROPE, LATENT, VHEAD = 128, 64, 512, 128
WIDTH = LATENT + ROPE
QUERY = NOPE + ROPE
ROWS = FORKS * RECOMP * HEADS
TILE = 128
TILES = ROWS // TILE
PKEYS, SKEYS = 8, 16
BLOCK = 2 * PKEYS + SKEYS
KEYS = CORE * ZH * BLOCK
SCALE = QUERY**-0.5
W1 = HEADS * LATENT // 16
W2 = 192
GRAY = (0, 1, 3, 2)


def dot(a, b):
    return jnp.dot(a, b, preferred_element_type=F32)


def dot_nt(a, b):
    return lax.dot_general(a, b, (((1,), (1,)), ((), ())), preferred_element_type=F32)


class Sems:
    def __init__(self, send, recv):
        self.send, self.recv, self.used, self.started = send, recv, 0, []

    def copy(self, src, dst, device):
        k = self.used
        self.used += 1
        made = pltpu.make_async_remote_copy(
            src_ref=src,
            dst_ref=dst,
            send_sem=self.send.at[k],
            recv_sem=self.recv.at[k],
            device_id=device,
            device_id_type=MESH,
        )
        made.start()
        self.started.append(made)
        return made


def kernel(
    prompt_ref, suffix_ref, q_ref, ku_ref, vu_ref, og_ref, fork_ref, length_ref,
    prompt_out, suffix_out, query_out, key_up_out, value_up_out,
    keys, keys_t, qry, qry_t, lgr, lgr_t, og_exp, qn_exp_t, bias, score, pgrad,
    acc_t, abs_t, sgrad_b, prob_b, kgrad, stat, stat_all,
    c1s, c1r, c2s, c2r, c3s, c3r,
    w1f, w1b, w1x, w1m, w1z, w1a, w2f, w2b, w2x, w2m, w2z, w2a,
    send_sem, recv_sem,
):
    ctx, sample = lax.axis_index("ctx"), lax.axis_index("sample")
    zl, x = ctx // X, ctx % X
    zh, y, core = sample // (Y * CORE), (sample // CORE) % Y, sample % CORE

    def at(zl_=zl, x_=x, zh_=zh, y_=y, core_=core):
        return (zl_ * X + x_, zh_ * (Y * CORE) + y_ * CORE + core_)

    sibling = at(core_=1 - core)

    def zh_by(d):
        return (zh + d + ZH) % ZH

    def y_by(d):
        return (y + d + Y) % Y

    def x_by(d):
        return (x + d + X) % X

    def zl_by(d):
        return (zl + d + ZL) % ZL

    sems = Sems(send_sem, recv_sem)

    partners = [sibling]
    partners += [at(zh_=zh_by(d)) for d in range(1, ZH)]
    partners += [at(y_=y_by(d)) for d in range(1, Y)]
    partners += [at(zl_=zl_by(a), x_=x_by(b)) for a in range(ZL) for b in range(X) if a + b]
    barrier = pltpu.get_barrier_semaphore()
    for device in partners:
        pl.semaphore_signal(barrier, inc=1, device_id=device, device_id_type=MESH)
    own = jnp.concatenate(
        [prompt_ref[0].astype(F32), prompt_ref[1].astype(F32), suffix_ref[0].astype(F32)], 0
    ).astype(BF16)
    keys[y, core, zh] = own
    pl.semaphore_wait(barrier, len(partners))

    from_zh = {}
    from_y = {}
    for d in (2, 1, 3):
        block = keys.at[y, core, zh]
        from_zh[d] = sems.copy(block, block, at(zh_=zh_by(d)))

    def spread_y(dz):
        block = keys.at[y, core, zh_by(-dz)]
        for d in (2, 1, 3):
            from_y[d, dz] = sems.copy(block, block, at(y_=y_by(d)))

    spread_y(0)

    lane = lax.broadcasted_iota(jnp.int32, (1, ROWS), 1)
    row_fork = (lane * 3277) >> 16
    row_step = (lane - row_fork * (RECOMP * HEADS)) >> 2

    def project(t, carry):
        rows = pl.ds(pl.multiple_of(t * TILE, TILE), TILE)
        q = q_ref[rows, :]
        og = og_ref[rows, :]
        head = lax.broadcasted_iota(jnp.int32, (TILE, NOPE), 0) & (HEADS - 1)
        q_nope = q[:, :NOPE]
        zero = jnp.zeros_like(q_nope)
        q_exp = jnp.concatenate([jnp.where(head == h, q_nope, zero) for h in range(HEADS)], 1)
        o_exp = jnp.concatenate([jnp.where(head == h, og, zero) for h in range(HEADS)], 1)
        og_exp[rows, :] = o_exp
        q_t = q_nope.T
        head_t = lax.broadcasted_iota(jnp.int32, (NOPE, TILE), 1) & (HEADS - 1)
        qn_exp_t[:, rows] = jnp.concatenate(
            [jnp.where(head_t == h, q_t, zero) for h in range(HEADS)], 0
        )
        whole = jnp.concatenate([dot(q_exp, ku_ref[...]).astype(BF16), q[:, NOPE:]], 1)
        qry[rows, :] = whole
        qry_t[:, rows] = whole.T
        grad = dot_nt(o_exp[:, :VHEAD], vu_ref[pl.ds(0, LATENT), :])
        for h in range(1, HEADS):
            grad += dot_nt(
                o_exp[:, h * VHEAD : (h + 1) * VHEAD], vu_ref[pl.ds(h * LATENT, LATENT), :]
            )
        grad = grad.astype(BF16)
        lgr[rows, :] = grad
        lgr_t[:, rows] = grad.T
        return carry

    lax.fori_loop(0, TILES, project, 0)

    for dz in (1, 3):
        from_zh[dz].wait_recv()
        spread_y(dz)

    def gather_rows(f, carry):
        limit, prompt = carry
        mine = row_fork == f
        return jnp.where(mine, length_ref[f], limit), jnp.where(mine, fork_ref[f], prompt)

    none = jnp.zeros((1, ROWS), jnp.int32)
    row_limit, row_prompt = lax.fori_loop(0, FORKS, gather_rows, (none, none))
    row_limit = row_limit - RECOMP + row_step
    first = jnp.broadcast_to(jnp.where(row_prompt == 0, 0.0, HIDDEN), (PKEYS, ROWS))
    second = jnp.broadcast_to(jnp.where(row_prompt == 1, 0.0, HIDDEN), (PKEYS, ROWS))
    position = ctx * SKEYS + lax.broadcasted_iota(jnp.int32, (SKEYS, ROWS), 0)

    def make_bias(b, carry):
        by, bc, bz = b // (CORE * ZH), (b // ZH) % CORE, b % ZH
        fork = bz * (Y * CORE) + by * CORE + bc
        last = jnp.where(row_fork == fork, row_limit, -1)
        seen = jnp.where(position <= last, 0.0, HIDDEN)
        bias[by, pl.ds(pl.multiple_of((bc * ZH + bz) * BLOCK, BLOCK), BLOCK), :] = (
            jnp.concatenate([first, second, seen], 0)
        )
        return carry

    lax.fori_loop(0, Y * CORE * ZH, make_bias, 0)

    from_zh[2].wait_recv()
    spread_y(2)

    from_core = {}

    def to_core(dy):
        part = keys.at[y_by(-dy), core]
        from_core[dy] = sems.copy(part, part, sibling)

    to_core(0)
    peak = jnp.full((1, ROWS), HIDDEN, F32)
    for i in range(Y):
        if i + 1 < Y:
            for dz in range(ZH):
                from_y[GRAY[i + 1], dz].wait_recv()
            to_core(GRAY[i + 1])
        from_core[GRAY[i]].wait_recv()
        part = y_by(-GRAY[i])
        tile = keys[part].reshape(KEYS, WIDTH)
        s = dot(tile, qry_t[...]) + bias[part]
        score[part] = s
        peak = jnp.maximum(peak, jnp.max(s, 0, keepdims=True))
        pgrad[part] = dot(tile[:, :LATENT], lgr_t[...])
        keys_t[part] = tile.T

    def exponents(part, carry):
        total, delta = carry
        p = jnp.exp((score[part] - peak) * SCALE)
        score[part] = p
        total = total + jnp.sum(p, 0, keepdims=True)
        delta = delta + jnp.sum(p * pgrad[part], 0, keepdims=True)
        return total, delta

    zeros = jnp.zeros((1, ROWS), F32)
    total, delta = lax.fori_loop(0, Y, exponents, (zeros, zeros))

    for t in range(TILES):
        cols = slice(t * TILE, (t + 1) * TILE)
        stat[t : t + 1, :] = peak[:, cols]
        stat[TILES + t : TILES + t + 1, :] = total[:, cols]
        stat[2 * TILES + t : 2 * TILES + t + 1, :] = delta[:, cols]
    stat[3 * TILES : 3 * TILES + 1, :] = jnp.zeros((1, TILE), F32)
    stat_copies = []
    for a in range(ZL):
        for b in range(X):
            if a + b:
                stat_copies.append(
                    sems.copy(stat, stat_all.at[ctx], at(zl_=zl_by(a), x_=x_by(b)))
                )
    stat_all[ctx] = stat[...]

    acc_t[...] = jnp.zeros_like(acc_t)

    def weigh(part, carry):
        acc_t[...] += dot(keys_t[part, :LATENT, :], score[part].astype(BF16))
        return carry

    lax.fori_loop(0, Y, weigh, 0)

    for made in stat_copies:
        made.wait_recv()
    all_peak = stat_all[:, 0:TILES, :]
    top = jnp.max(all_peak, 0)
    shrink = jnp.exp((all_peak - top[None]) * SCALE)
    whole_total = jnp.sum(stat_all[:, TILES : 2 * TILES, :] * shrink, 0)
    whole_delta = jnp.sum(stat_all[:, 2 * TILES : 3 * TILES, :] * shrink, 0)
    inverse = 1.0 / whole_total
    weight = jnp.exp((stat[0:TILES, :] - top) * SCALE) * inverse
    row_delta = whole_delta * inverse

    def as_row(v):
        return jnp.concatenate([v[t : t + 1, :] for t in range(TILES)], 1)

    weight, row_delta = as_row(weight), as_row(row_delta)

    def send_x(src, dst):
        return [
            sems.copy(src.at[x_by(d)], dst.at[d - 1], at(x_=x_by(d))) for d in (2, 1, 3)
        ]

    scaled = (acc_t[...] * weight).astype(BF16)
    for h in range(HEADS):
        cols = slice(h * VHEAD, (h + 1) * VHEAD)
        part = dot(scaled, og_exp[:, cols]).reshape(ZL, W1, TILE)
        w1f[h] = part
        w1b[h] = part.astype(BF16)
    w1_x = send_x(w1b, w1x)

    abs_t[...] = jnp.zeros_like(abs_t)

    def grads(part, carry):
        p = score[part] * weight
        prob_b[part] = p.astype(BF16)
        sg = (p * (pgrad[part] - row_delta) * SCALE).astype(BF16)
        sgrad_b[part] = sg
        abs_t[...] += dot(keys_t[part], sg)
        return carry

    lax.fori_loop(0, Y, grads, 0)

    lat = abs_t[:LATENT, :].astype(BF16)
    kup = dot_nt(qn_exp_t[...], lat)
    for b in range(LATENT // TILE):
        w2f[b * 512 : (b + 1) * 512, :] = kup[:, b * TILE : (b + 1) * TILE]
    spread = dot(ku_ref[...], lat)
    head_of = lane & (HEADS - 1)
    nope = jnp.zeros((NOPE, ROWS), F32)
    for h in range(HEADS):
        nope = jnp.where(head_of == h, spread[h * NOPE : (h + 1) * NOPE, :], nope)
    for t in range(TILES):
        cols = slice(t * TILE, (t + 1) * TILE)
        base = 2048 + t * QUERY
        w2f[base : base + NOPE, :] = nope[:, cols]
        w2f[base + NOPE : base + QUERY, :] = abs_t[LATENT:WIDTH, cols]
    w2f[2048 + TILES * QUERY : 3072, :] = jnp.zeros((64, TILE), F32)
    w2b[...] = w2f[...].reshape(X, ZL, W2, TILE).astype(BF16)
    w2_x = send_x(w2b, w2x)

    from_core2 = {}
    for i in (1, 2, 3, 0):
        part = y_by(i)
        grad = dot(sgrad_b[part], qry[...])
        value = dot(prob_b[part], lgr[...])
        kgrad[part, :, :, :LATENT] = (grad[:, :LATENT] + value).reshape(
            CORE, ZH * BLOCK, LATENT
        )
        kgrad[part, :, :, LATENT:] = grad[:, LATENT:].reshape(CORE, ZH * BLOCK, ROPE)
        c1s[part] = kgrad[part, 1 - core].astype(BF16)
        from_core2[i] = sems.copy(c1s.at[part], c1r.at[part], sibling)

    def sum_x(made, full, came, middle):
        for m in made:
            m.wait_recv()
        add = full + came[0].astype(F32) + came[1].astype(F32) + came[2].astype(F32)
        middle[...] = add.astype(BF16)

    def send_zl(middle, dst):
        return [
            sems.copy(middle.at[zl_by(d)], dst.at[d - 1], at(zl_=zl_by(d))) for d in (2, 1, 3)
        ]

    sum_x(w1_x, w1f[x], w1x, w1m)
    w1_z = send_zl(w1m, w1z)

    from_y2 = []
    for i in (1, 2, 3):
        part = y_by(i)
        from_core2[i].wait_recv()
        c2s[i - 1] = (kgrad[part, core] + c1r[part].astype(F32)).astype(BF16)
        from_y2.append(sems.copy(c2s.at[i - 1], c2r.at[i - 1], at(y_=part)))

    own_rows = pl.ds(pl.multiple_of(x * (ZL * W2), W2), ZL * W2)
    sum_x(w2_x, w2f[own_rows, :].reshape(ZL, W2, TILE), w2x, w2m)
    w2_z = send_zl(w2m, w2z)

    from_core2[0].wait_recv()
    for made in from_y2:
        made.wait_recv()
    mine = kgrad[y, core] + c1r[y].astype(F32)
    for i in range(Y - 1):
        mine += c2r[i].astype(F32)
    kgrad[y, core] = mine
    c3s[...] = mine.reshape(ZH, BLOCK, WIDTH).astype(BF16)
    from_zh2 = [sems.copy(c3s.at[zh_by(d)], c3r.at[d - 1], at(zh_=zh_by(d))) for d in (2, 1, 3)]

    def sum_zl(made, middle, came, whole):
        for m in made:
            m.wait_recv()
        add = middle[zl].astype(F32)
        for i in range(ZL - 1):
            add += came[i].astype(F32)
        whole[x, zl] = add.astype(BF16)
        block = whole.at[x, zl]
        return [sems.copy(block, block, at(zl_=zl_by(d))) for d in (2, 1, 3)]

    def gather_x(made, whole):
        for m in made:
            m.wait_recv()
        block = whole.at[x]
        return [sems.copy(block, block, at(x_=x_by(d))) for d in (2, 1, 3)]

    w1_z = sum_zl(w1_z, w1m, w1z, w1a)
    w2_z = sum_zl(w2_z, w2m, w2z, w2a)
    w1_x = gather_x(w1_z, w1a)
    w2_x = gather_x(w2_z, w2a)

    for made in from_zh2:
        made.wait_recv()
    final = kgrad[y, core, pl.ds(pl.multiple_of(zh * BLOCK, BLOCK), BLOCK), :]
    for i in range(ZH - 1):
        final += c3r[i].astype(F32)
    prompt_out[0] = final[:PKEYS]
    prompt_out[1] = final[PKEYS : 2 * PKEYS]
    suffix_out[0] = final[2 * PKEYS :]

    for made in w1_x:
        made.wait_recv()
    value_up_out[...] = w1a[...].reshape(HEADS * LATENT, VHEAD).astype(F32)
    for made in w2_x:
        made.wait_recv()
    w2f[...] = w2a[...].reshape(3072, TILE).astype(F32)
    for b in range(LATENT // TILE):
        key_up_out[:, b * TILE : (b + 1) * TILE] = w2f[b * 512 : (b + 1) * 512, :]
    for t in range(TILES):
        base = 2048 + t * QUERY
        query_out[t * TILE : (t + 1) * TILE, :] = w2f[base : base + QUERY, :].T
    for made in sems.started:
        made.wait_send()


def shards(prompt, suffix, queries, key_up, value_up, out_grad, fork_prompt, suffix_length):
    vmem = pl.BlockSpec(memory_space=pltpu.VMEM)
    smem = pl.BlockSpec(memory_space=pltpu.SMEM)
    copies = 96
    outs = pl.pallas_call(
        kernel,
        out_shape=(
            jax.ShapeDtypeStruct((2, PKEYS, WIDTH), F32),
            jax.ShapeDtypeStruct((1, SKEYS, WIDTH), F32),
            jax.ShapeDtypeStruct((ROWS, QUERY), F32),
            jax.ShapeDtypeStruct((HEADS * NOPE, LATENT), F32),
            jax.ShapeDtypeStruct((HEADS * LATENT, VHEAD), F32),
        ),
        in_specs=[vmem] * 6 + [smem] * 2,
        out_specs=(vmem,) * 5,
        scratch_shapes=[
            pltpu.VMEM((Y, CORE, ZH, BLOCK, WIDTH), BF16),
            pltpu.VMEM((Y, WIDTH, KEYS), BF16),
            pltpu.VMEM((ROWS, WIDTH), BF16),
            pltpu.VMEM((WIDTH, ROWS), BF16),
            pltpu.VMEM((ROWS, LATENT), BF16),
            pltpu.VMEM((LATENT, ROWS), BF16),
            pltpu.VMEM((ROWS, HEADS * VHEAD), BF16),
            pltpu.VMEM((HEADS * NOPE, ROWS), BF16),
            pltpu.VMEM((Y, KEYS, ROWS), F32),
            pltpu.VMEM((Y, KEYS, ROWS), F32),
            pltpu.VMEM((Y, KEYS, ROWS), F32),
            pltpu.VMEM((LATENT, ROWS), F32),
            pltpu.VMEM((WIDTH, ROWS), F32),
            pltpu.VMEM((Y, KEYS, ROWS), BF16),
            pltpu.VMEM((Y, KEYS, ROWS), BF16),
            pltpu.VMEM((Y, CORE, ZH * BLOCK, WIDTH), F32),
            pltpu.VMEM((16, TILE), F32),
            pltpu.VMEM((ZL * X, 16, TILE), F32),
            pltpu.VMEM((Y, ZH * BLOCK, WIDTH), BF16),
            pltpu.VMEM((Y, ZH * BLOCK, WIDTH), BF16),
            pltpu.VMEM((Y - 1, ZH * BLOCK, WIDTH), BF16),
            pltpu.VMEM((Y - 1, ZH * BLOCK, WIDTH), BF16),
            pltpu.VMEM((ZH, BLOCK, WIDTH), BF16),
            pltpu.VMEM((ZH - 1, BLOCK, WIDTH), BF16),
            pltpu.VMEM((X, ZL, W1, TILE), F32),
            pltpu.VMEM((X, ZL, W1, TILE), BF16),
            pltpu.VMEM((X - 1, ZL, W1, TILE), BF16),
            pltpu.VMEM((ZL, W1, TILE), BF16),
            pltpu.VMEM((ZL - 1, W1, TILE), BF16),
            pltpu.VMEM((X, ZL, W1, TILE), BF16),
            pltpu.VMEM((X * ZL * W2, TILE), F32),
            pltpu.VMEM((X, ZL, W2, TILE), BF16),
            pltpu.VMEM((X - 1, ZL, W2, TILE), BF16),
            pltpu.VMEM((ZL, W2, TILE), BF16),
            pltpu.VMEM((ZL - 1, W2, TILE), BF16),
            pltpu.VMEM((X, ZL, W2, TILE), BF16),
            pltpu.SemaphoreType.DMA((copies,)),
            pltpu.SemaphoreType.DMA((copies,)),
        ],
        compiler_params=pltpu.CompilerParams(
            collective_id=0, has_side_effects=True, vmem_limit_bytes=52 << 20
        ),
        cost_estimate=pl.CostEstimate(
            flops=8_000_000_000, bytes_accessed=6_000_000, transcendentals=700_000
        ),
        name="latent_backward",
    )(
        prompt,
        suffix,
        queries.reshape(ROWS, QUERY),
        key_up.reshape(HEADS * NOPE, LATENT),
        value_up.reshape(HEADS * LATENT, VHEAD),
        out_grad.reshape(ROWS, VHEAD),
        fork_prompt,
        suffix_length,
    )
    prompt_grad, suffix_grad, query_grad, key_up_grad, value_up_grad = outs
    return (
        prompt_grad,
        suffix_grad,
        query_grad.reshape(FORKS, RECOMP, HEADS, QUERY),
        key_up_grad.reshape(HEADS, NOPE, LATENT),
        value_up_grad.reshape(HEADS, LATENT, VHEAD),
    )


def solution(mesh):
    return jax.shard_map(
        shards,
        mesh=mesh,
        in_specs=(
            P(None, ("ctx", "sample"), None),
            P("sample", "ctx", None),
            P(None, None, "sample", None),
            P("sample", None, None),
            P("sample", None, None),
            P(None, None, "sample", None),
            P(),
            P(),
        ),
        out_specs=(
            P(None, ("ctx", "sample"), None),
            P("sample", "ctx", None),
            P(None, None, "sample", None),
            P("sample", None, None),
            P("sample", None, None),
        ),
        check_vma=False,
    )
```

```python
import functools

import jax
import jax.numpy as jnp
from jax import lax
from jax.experimental import pallas as pl
from jax.experimental.pallas import tpu as pltpu
from jax.sharding import PartitionSpec as P

MESH = pl.DeviceIdType.MESH
F32 = jnp.float32
BF16 = jnp.bfloat16
HIDDEN = -1e30

ZL, X, ZH, Y, CORE = 4, 4, 4, 4, 2
FORKS, RECOMP, HEADS = 32, 5, 4
NOPE, ROPE, LATENT, VHEAD = 128, 64, 512, 128
WIDTH = LATENT + ROPE
QUERY = NOPE + ROPE
ROWS = FORKS * RECOMP * HEADS
TILE = 128
TILES = ROWS // TILE
PKEYS, SKEYS = 8, 16
BLOCK = 2 * PKEYS + SKEYS
KEYS = CORE * Y * BLOCK
SCALE = QUERY**-0.5
W1 = HEADS * LATENT // 16
W2 = 192


def dot(a, b):
    return jnp.dot(a, b, preferred_element_type=F32)


def dot_nt(a, b):
    return lax.dot_general(a, b, (((1,), (1,)), ((), ())), preferred_element_type=F32)


class Sems:
    def __init__(self, send, recv):
        self.send, self.recv, self.used, self.started = send, recv, 0, []

    def copy(self, src, dst, device):
        k = self.used
        self.used += 1
        made = pltpu.make_async_remote_copy(
            src_ref=src,
            dst_ref=dst,
            send_sem=self.send.at[k],
            recv_sem=self.recv.at[k],
            device_id=device,
            device_id_type=MESH,
        )
        made.start()
        self.started.append(made)
        return made


def kernel(
    prompt_ref, suffix_ref, q_ref, ku_ref, vu_ref, og_ref, fork_ref, length_ref,
    prompt_out, suffix_out, query_out, key_up_out, value_up_out,
    keys, qry, qry_t, lgr, lgr_t, og_exp, qn_exp_t, bias, score, pgrad, peaks,
    acc_t, dif_t, kgrad, stat, stat_all, c1s, c1r, c2s, c2r, c3s, c3r,
    w1f, w1b, w1x, w1m, w1z, w1a, w2f, w2b, w2x, w2m, w2z, w2a,
    send_sem, recv_sem,
):
    ctx, sample = lax.axis_index("ctx"), lax.axis_index("sample")
    zl, x = ctx // X, ctx % X
    zh, y, core = sample // (Y * CORE), (sample // CORE) % Y, sample % CORE

    def at(zl_=zl, x_=x, zh_=zh, y_=y, core_=core):
        return (zl_ * X + x_, zh_ * (Y * CORE) + y_ * CORE + core_)

    sibling = at(core_=1 - core)

    def zh_by(d):
        return (zh + d + ZH) % ZH

    def y_by(d):
        return (y + d + Y) % Y

    def x_by(d):
        return (x + d + X) % X

    def zl_by(d):
        return (zl + d + ZL) % ZL

    sems = Sems(send_sem, recv_sem)

    partners = [sibling]
    partners += [at(zh_=zh_by(d)) for d in range(1, ZH)]
    partners += [at(y_=y_by(d)) for d in range(1, Y)]
    partners += [at(zl_=zl_by(a), x_=x_by(b)) for a in range(ZL) for b in range(X) if a + b]
    barrier = pltpu.get_barrier_semaphore()
    for device in partners:
        pl.semaphore_signal(barrier, inc=1, device_id=device, device_id_type=MESH)
    own = jnp.concatenate(
        [prompt_ref[0].astype(F32), prompt_ref[1].astype(F32), suffix_ref[0].astype(F32)], 0
    ).astype(BF16)
    keys[zh, core, y] = own
    pl.semaphore_wait(barrier, len(partners))

    from_zh = {}
    from_y = {}
    from_core = {}
    for d in (2, 1, 3):
        block = keys.at[zh, core, y]
        from_zh[d] = sems.copy(block, block, at(zh_=zh_by(d)))

    def spread_y(dz):
        if dz:
            from_zh[dz].wait_recv()
        block = keys.at[zh_by(-dz), core, y]
        from_y[dz] = [sems.copy(block, block, at(y_=y_by(d))) for d in (2, 1, 3)]

    def to_core(dz):
        for made in from_y[dz]:
            made.wait_recv()
        part = keys.at[zh_by(-dz), core]
        from_core[dz] = sems.copy(part, part, sibling)

    spread_y(0)

    lane = lax.broadcasted_iota(jnp.int32, (1, ROWS), 1)
    row_fork = (lane * 3277) >> 16
    row_step = (lane - row_fork * (RECOMP * HEADS)) >> 2

    def project(t, carry):
        rows = pl.ds(pl.multiple_of(t * TILE, TILE), TILE)
        q = q_ref[rows, :]
        og = og_ref[rows, :]
        head = lax.broadcasted_iota(jnp.int32, (TILE, NOPE), 0) & (HEADS - 1)
        q_nope = q[:, :NOPE]
        zero = jnp.zeros_like(q_nope)
        q_exp = jnp.concatenate([jnp.where(head == h, q_nope, zero) for h in range(HEADS)], 1)
        o_exp = jnp.concatenate([jnp.where(head == h, og, zero) for h in range(HEADS)], 1)
        og_exp[rows, :] = o_exp
        q_t = q_nope.T
        head_t = lax.broadcasted_iota(jnp.int32, (NOPE, TILE), 1) & (HEADS - 1)
        qn_exp_t[:, rows] = jnp.concatenate(
            [jnp.where(head_t == h, q_t, zero) for h in range(HEADS)], 0
        )
        whole = jnp.concatenate([dot(q_exp, ku_ref[...]).astype(BF16), q[:, NOPE:]], 1)
        qry[rows, :] = whole
        qry_t[:, rows] = whole.T
        grad = dot_nt(o_exp[:, :VHEAD], vu_ref[pl.ds(0, LATENT), :])
        for h in range(1, HEADS):
            grad += dot_nt(
                o_exp[:, h * VHEAD : (h + 1) * VHEAD], vu_ref[pl.ds(h * LATENT, LATENT), :]
            )
        grad = grad.astype(BF16)
        lgr[rows, :] = grad
        lgr_t[:, rows] = grad.T
        return carry

    lax.fori_loop(0, TILES, project, 0)

    def gather_rows(f, carry):
        limit, prompt = carry
        mine = row_fork == f
        return jnp.where(mine, length_ref[f], limit), jnp.where(mine, fork_ref[f], prompt)

    none = jnp.zeros((1, ROWS), jnp.int32)
    row_limit, row_prompt = lax.fori_loop(0, FORKS, gather_rows, (none, none))
    row_limit = row_limit - RECOMP + row_step
    first = jnp.broadcast_to(jnp.where(row_prompt == 0, 0.0, HIDDEN), (PKEYS, ROWS))
    second = jnp.broadcast_to(jnp.where(row_prompt == 1, 0.0, HIDDEN), (PKEYS, ROWS))
    position = ctx * SKEYS + lax.broadcasted_iota(jnp.int32, (SKEYS, ROWS), 0)

    def make_bias(b, carry):
        bz, bc, by = b // (CORE * Y), (b // Y) % CORE, b % Y
        fork = bz * (Y * CORE) + by * CORE + bc
        last = jnp.where(row_fork == fork, row_limit, -1)
        seen = jnp.where(position <= last, 0.0, HIDDEN)
        bias[bz, pl.ds(pl.multiple_of((bc * Y + by) * BLOCK, BLOCK), BLOCK), :] = (
            jnp.concatenate([first, second, seen], 0)
        )
        return carry

    to_core(0)
    lax.fori_loop(0, Y * CORE * ZH, make_bias, 0)

    def scores_of(dz):
        from_core[dz].wait_recv()
        part = zh_by(-dz)
        tile = keys[part].reshape(KEYS, WIDTH)
        s = dot(tile, qry_t[...]) + bias[part]
        peak = jnp.max(s, 0, keepdims=True)
        p = jnp.exp((s - peak) * SCALE)
        score[part] = p
        grad = dot(tile[:, :LATENT], lgr_t[...])
        pgrad[part] = grad
        total = jnp.sum(p, 0, keepdims=True)
        mean = jnp.sum(p * grad, 0, keepdims=True) / total
        peaks[dz] = peak
        return part, peak, total, mean

    def merged(left, right):
        top = jnp.maximum(left[0], right[0])
        shrink_left = jnp.exp((left[0] - top) * SCALE)
        shrink_right = jnp.exp((right[0] - top) * SCALE)
        total_left, total_right = left[1] * shrink_left, right[1] * shrink_right
        total = total_left + total_right
        mean = (total_left * left[2] + total_right * right[2]) / total
        return (top, total, mean), shrink_left, shrink_right

    def sums_of(part, mean):
        tile_t = keys[part].reshape(KEYS, WIDTH).T
        p = score[part]
        return dot(tile_t, p.astype(BF16)), dot(
            tile_t, (p * (pgrad[part] - mean)).astype(BF16)
        )

    def add_sums(state, new, part):
        both, shrink_left, shrink_right = merged(state, new)
        acc, grad = sums_of(part, new[2])
        old = acc_t[...]
        acc_t[...] = shrink_left * old + shrink_right * acc
        dif_t[...] = shrink_left * (dif_t[...] + (state[2] - both[2]) * old) + shrink_right * (
            grad + (new[2] - both[2]) * acc
        )
        return both

    part, *state = scores_of(0)
    spread_y(1)
    spread_y(3)
    acc_t[...], dif_t[...] = sums_of(part, state[2])
    to_core(1)
    to_core(3)
    spread_y(2)
    part, *new = scores_of(1)
    state = add_sums(state, new, part)
    to_core(2)
    part, *new = scores_of(3)
    state = add_sums(state, new, part)
    part, *new = scores_of(2)
    (peak, total, mean), _, _ = merged(state, new)

    delta = mean * total
    for t in range(TILES):
        cols = slice(t * TILE, (t + 1) * TILE)
        stat[t : t + 1, :] = peak[:, cols]
        stat[TILES + t : TILES + t + 1, :] = total[:, cols]
        stat[2 * TILES + t : 2 * TILES + t + 1, :] = delta[:, cols]
    stat[3 * TILES : 3 * TILES + 1, :] = jnp.zeros((1, TILE), F32)
    stat_copies = []
    for a in range(ZL):
        for b in range(X):
            if a + b:
                stat_copies.append(
                    sems.copy(stat, stat_all.at[ctx], at(zl_=zl_by(a), x_=x_by(b)))
                )
    stat_all[ctx] = stat[...]

    add_sums(state, new, part)

    for made in stat_copies:
        made.wait_recv()
    all_peak = stat_all[:, 0:TILES, :]
    top = jnp.max(all_peak, 0)
    shrink = jnp.exp((all_peak - top[None]) * SCALE)
    whole_total = jnp.sum(stat_all[:, TILES : 2 * TILES, :] * shrink, 0)
    whole_delta = jnp.sum(stat_all[:, 2 * TILES : 3 * TILES, :] * shrink, 0)
    inverse = 1.0 / whole_total

    def as_row(v):
        return jnp.concatenate([v[t : t + 1, :] for t in range(TILES)], 1)

    top, inverse, row_delta = as_row(top), as_row(inverse), as_row(whole_delta * inverse)
    weight = jnp.exp((peak - top) * SCALE) * inverse

    def send_x(src, dst):
        made = {}
        for e in (2, 1, 3, 0):
            made[e] = [
                sems.copy(
                    src.at[x_by(d), zl_by(e)], dst.at[d - 1, zl_by(e)], at(x_=x_by(d))
                )
                for d in (2, 1, 3)
            ]
        return made

    scaled = (acc_t[:LATENT, :] * weight).astype(BF16)
    for h in range(HEADS):
        cols = slice(h * VHEAD, (h + 1) * VHEAD)
        part = dot(scaled, og_exp[:, cols]).reshape(ZL, W1, TILE)
        w1f[h] = part
        w1b[h] = part.astype(BF16)
    w1_x = send_x(w1b, w1x)

    shift = row_delta - mean
    factor = weight * SCALE
    lat = (factor * (dif_t[:LATENT, :] - shift * acc_t[:LATENT, :])).astype(BF16)
    rope = factor * (dif_t[LATENT:, :] - shift * acc_t[LATENT:, :])
    kup = dot_nt(qn_exp_t[...], lat)
    for b in range(LATENT // TILE):
        w2f[b * 512 : (b + 1) * 512, :] = kup[:, b * TILE : (b + 1) * TILE]
    spread = dot(ku_ref[...], lat)
    head_of = lane & (HEADS - 1)
    nope = jnp.zeros((NOPE, ROWS), F32)
    for h in range(HEADS):
        nope = jnp.where(head_of == h, spread[h * NOPE : (h + 1) * NOPE, :], nope)
    for t in range(TILES):
        cols = slice(t * TILE, (t + 1) * TILE)
        base = 2048 + t * QUERY
        w2f[base : base + NOPE, :] = nope[:, cols]
        w2f[base + NOPE : base + QUERY, :] = rope[:, cols]
    w2f[2048 + TILES * QUERY : 3072, :] = jnp.zeros((64, TILE), F32)
    w2b[...] = w2f[...].reshape(X, ZL, W2, TILE).astype(BF16)
    w2_x = send_x(w2b, w2x)

    core_sums, y_sums, zh_sums = {}, {}, {}

    def key_grads(dz):
        part = zh_by(-dz)
        p = score[part] * (jnp.exp((peaks[dz] - top) * SCALE) * inverse)
        sg = (p * (pgrad[part] - row_delta) * SCALE).astype(BF16)
        grad = dot(sg, qry[...])
        value = dot(p.astype(BF16), lgr[...])
        kgrad[part, :, :, :LATENT] = (grad[:, :LATENT] + value).reshape(CORE, Y * BLOCK, LATENT)
        kgrad[part, :, :, LATENT:] = grad[:, LATENT:].reshape(CORE, Y * BLOCK, ROPE)
        c1s[part] = kgrad[part, 1 - core].astype(BF16)
        core_sums[dz] = sems.copy(c1s.at[part], c1r.at[part], sibling)

    def add_cores(dz):
        part = zh_by(-dz)
        core_sums[dz].wait_recv()
        both = kgrad[part, core] + c1r[part].astype(F32)
        kgrad[part, core] = both
        c2s[dz] = both.reshape(Y, BLOCK, WIDTH).astype(BF16)
        y_sums[dz] = [
            sems.copy(c2s.at[dz, y_by(d)], c2r.at[dz, d - 1], at(y_=y_by(d))) for d in (2, 1, 3)
        ]

    def add_ys(dz):
        for made in y_sums[dz]:
            made.wait_recv()
        rows = pl.ds(pl.multiple_of(y * BLOCK, BLOCK), BLOCK)
        mine = kgrad[zh_by(-dz), core, rows, :]
        for i in range(Y - 1):
            mine += c2r[dz, i].astype(F32)
        if dz == 0:
            return mine
        c3s[dz - 1] = mine.astype(BF16)
        zh_sums[dz] = sems.copy(c3s.at[dz - 1], c3r.at[dz - 1], at(zh_=zh_by(-dz)))

    def sum_x(made, full, came, middle, dst):
        out = []
        for e in (2, 1, 3, 0):
            for m in made[e]:
                m.wait_recv()
            to = zl_by(e)
            add = full(to) + came[0, to].astype(F32) + came[1, to].astype(F32)
            middle[to] = (add + came[2, to].astype(F32)).astype(BF16)
            if e:
                out.append(sems.copy(middle.at[to], dst.at[e - 1], at(zl_=to)))
        return out

    def spread_x(whole, e):
        block = whole.at[x, zl_by(-e)]
        return [sems.copy(block, block, at(x_=x_by(d))) for d in (2, 1, 3)]

    def sum_zl(made, middle, came, whole):
        for m in made:
            m.wait_recv()
        add = middle[zl].astype(F32)
        for i in range(ZL - 1):
            add += came[i].astype(F32)
        whole[x, zl] = add.astype(BF16)
        block = whole.at[x, zl]
        back = {e: sems.copy(block, block, at(zl_=zl_by(e))) for e in (2, 1, 3)}
        return back, spread_x(whole, 0)

    def gather_x(back, out, whole):
        for e in (1, 3, 2):
            back[e].wait_recv()
            out += spread_x(whole, e)

    def w2_rows(to):
        return w2f[pl.ds(pl.multiple_of((x * ZL + to) * W2, W2), W2), :]

    key_grads(2)
    key_grads(1)
    add_cores(2)
    key_grads(3)
    add_cores(1)
    key_grads(0)
    w1_z = sum_x(w1_x, lambda to: w1f[x, to], w1x, w1m, w1z)
    add_cores(3)
    add_ys(2)
    w2_z = sum_x(w2_x, w2_rows, w2x, w2m, w2z)
    add_ys(1)
    add_ys(3)
    add_cores(0)
    w1_back, w1_x = sum_zl(w1_z, w1m, w1z, w1a)
    final = add_ys(0)
    w2_back, w2_x = sum_zl(w2_z, w2m, w2z, w2a)
    gather_x(w1_back, w1_x, w1a)
    gather_x(w2_back, w2_x, w2a)

    for dz in (1, 3, 2):
        zh_sums[dz].wait_recv()
        final += c3r[dz - 1].astype(F32)
    prompt_out[0] = final[:PKEYS]
    prompt_out[1] = final[PKEYS : 2 * PKEYS]
    suffix_out[0] = final[2 * PKEYS :]

    for made in w1_x:
        made.wait_recv()
    value_up_out[...] = w1a[...].reshape(HEADS * LATENT, VHEAD).astype(F32)
    for made in w2_x:
        made.wait_recv()
    w2f[...] = w2a[...].reshape(3072, TILE).astype(F32)
    for b in range(LATENT // TILE):
        key_up_out[:, b * TILE : (b + 1) * TILE] = w2f[b * 512 : (b + 1) * 512, :]
    for t in range(TILES):
        base = 2048 + t * QUERY
        query_out[t * TILE : (t + 1) * TILE, :] = w2f[base : base + QUERY, :].T
    for made in sems.started:
        made.wait_send()


def shards(prompt, suffix, queries, key_up, value_up, out_grad, fork_prompt, suffix_length):
    vmem = pl.BlockSpec(memory_space=pltpu.VMEM)
    smem = pl.BlockSpec(memory_space=pltpu.SMEM)
    copies = 128
    outs = pl.pallas_call(
        kernel,
        out_shape=(
            jax.ShapeDtypeStruct((2, PKEYS, WIDTH), F32),
            jax.ShapeDtypeStruct((1, SKEYS, WIDTH), F32),
            jax.ShapeDtypeStruct((ROWS, QUERY), F32),
            jax.ShapeDtypeStruct((HEADS * NOPE, LATENT), F32),
            jax.ShapeDtypeStruct((HEADS * LATENT, VHEAD), F32),
        ),
        in_specs=[vmem] * 6 + [smem] * 2,
        out_specs=(vmem,) * 5,
        scratch_shapes=[
            pltpu.VMEM((ZH, CORE, Y, BLOCK, WIDTH), BF16),
            pltpu.VMEM((ROWS, WIDTH), BF16),
            pltpu.VMEM((WIDTH, ROWS), BF16),
            pltpu.VMEM((ROWS, LATENT), BF16),
            pltpu.VMEM((LATENT, ROWS), BF16),
            pltpu.VMEM((ROWS, HEADS * VHEAD), BF16),
            pltpu.VMEM((HEADS * NOPE, ROWS), BF16),
            pltpu.VMEM((ZH, KEYS, ROWS), F32),
            pltpu.VMEM((ZH, KEYS, ROWS), F32),
            pltpu.VMEM((ZH, KEYS, ROWS), F32),
            pltpu.VMEM((ZH, 1, ROWS), F32),
            pltpu.VMEM((WIDTH, ROWS), F32),
            pltpu.VMEM((WIDTH, ROWS), F32),
            pltpu.VMEM((ZH, CORE, Y * BLOCK, WIDTH), F32),
            pltpu.VMEM((16, TILE), F32),
            pltpu.VMEM((ZL * X, 16, TILE), F32),
            pltpu.VMEM((ZH, Y * BLOCK, WIDTH), BF16),
            pltpu.VMEM((ZH, Y * BLOCK, WIDTH), BF16),
            pltpu.VMEM((ZH, Y, BLOCK, WIDTH), BF16),
            pltpu.VMEM((ZH, Y - 1, BLOCK, WIDTH), BF16),
            pltpu.VMEM((ZH - 1, BLOCK, WIDTH), BF16),
            pltpu.VMEM((ZH - 1, BLOCK, WIDTH), BF16),
            pltpu.VMEM((X, ZL, W1, TILE), F32),
            pltpu.VMEM((X, ZL, W1, TILE), BF16),
            pltpu.VMEM((X - 1, ZL, W1, TILE), BF16),
            pltpu.VMEM((ZL, W1, TILE), BF16),
            pltpu.VMEM((ZL - 1, W1, TILE), BF16),
            pltpu.VMEM((X, ZL, W1, TILE), BF16),
            pltpu.VMEM((X * ZL * W2, TILE), F32),
            pltpu.VMEM((X, ZL, W2, TILE), BF16),
            pltpu.VMEM((X - 1, ZL, W2, TILE), BF16),
            pltpu.VMEM((ZL, W2, TILE), BF16),
            pltpu.VMEM((ZL - 1, W2, TILE), BF16),
            pltpu.VMEM((X, ZL, W2, TILE), BF16),
            pltpu.SemaphoreType.DMA((copies,)),
            pltpu.SemaphoreType.DMA((copies,)),
        ],
        compiler_params=pltpu.CompilerParams(
            collective_id=0, has_side_effects=True, vmem_limit_bytes=52 << 20
        ),
        cost_estimate=pl.CostEstimate(
            flops=8_000_000_000, bytes_accessed=6_000_000, transcendentals=700_000
        ),
        name="latent_backward",
    )(
        prompt,
        suffix,
        queries.reshape(ROWS, QUERY),
        key_up.reshape(HEADS * NOPE, LATENT),
        value_up.reshape(HEADS * LATENT, VHEAD),
        out_grad.reshape(ROWS, VHEAD),
        fork_prompt,
        suffix_length,
    )
    prompt_grad, suffix_grad, query_grad, key_up_grad, value_up_grad = outs
    return (
        prompt_grad,
        suffix_grad,
        query_grad.reshape(FORKS, RECOMP, HEADS, QUERY),
        key_up_grad.reshape(HEADS, NOPE, LATENT),
        value_up_grad.reshape(HEADS, LATENT, VHEAD),
    )


def solution(mesh):
    return jax.shard_map(
        shards,
        mesh=mesh,
        in_specs=(
            P(None, ("ctx", "sample"), None),
            P("sample", "ctx", None),
            P(None, None, "sample", None),
            P("sample", None, None),
            P("sample", None, None),
            P(None, None, "sample", None),
            P(),
            P(),
        ),
        out_specs=(
            P(None, ("ctx", "sample"), None),
            P("sample", "ctx", None),
            P(None, None, "sample", None),
            P("sample", None, None),
            P("sample", None, None),
        ),
        check_vma=False,
    )
```

```python
import functools

import jax
import jax.numpy as jnp
from jax import lax
from jax.experimental import pallas as pl
from jax.experimental.pallas import tpu as pltpu
from jax.sharding import PartitionSpec as P

MESH = pl.DeviceIdType.MESH
F32 = jnp.float32
BF16 = jnp.bfloat16
HIDDEN = -1e30

ZL, X, ZH, Y, CORE = 4, 4, 4, 4, 2
FORKS, RECOMP, HEADS = 32, 5, 4
NOPE, ROPE, LATENT, VHEAD = 128, 64, 512, 128
WIDTH = LATENT + ROPE
QUERY = NOPE + ROPE
ROWS = FORKS * RECOMP * HEADS
TILE = 128
TILES = ROWS // TILE
PKEYS, SKEYS = 8, 16
BLOCK = 2 * PKEYS + SKEYS
KEYS = CORE * Y * BLOCK
SCALE = QUERY**-0.5
W1 = HEADS * LATENT // 16
W2 = 192


def dot(a, b):
    return jnp.dot(a, b, preferred_element_type=F32)


def dot_nt(a, b):
    return lax.dot_general(a, b, (((1,), (1,)), ((), ())), preferred_element_type=F32)


class Sems:
    def __init__(self, send, recv):
        self.send, self.recv, self.used, self.started = send, recv, 0, []

    def copy(self, src, dst, device):
        k = self.used
        self.used += 1
        made = pltpu.make_async_remote_copy(
            src_ref=src,
            dst_ref=dst,
            send_sem=self.send.at[k],
            recv_sem=self.recv.at[k],
            device_id=device,
            device_id_type=MESH,
        )
        made.start()
        self.started.append(made)
        return made


def kernel(
    prompt_ref, suffix_ref, q_any, ku_any, vu_any, og_any, fork_ref, length_ref,
    keys_out, w1_out, w2_out,
    keys, qry, qry_t, lgr, lgr_t, og_exp, qn_exp_t, bias, score, pgrad, peaks,
    acc_t, dif_t, kgrad, stat, stat_all, c1s, c1r, c2s, c2r, c3s, c3r,
    w1f, w1b, w1x, w1m, w1z, w1a, w2f, w2b, w2x, w2m, w2z, w2a,
    q_ref, ku_ref, vu_ref, og_ref, send_sem, recv_sem, load_sem,
):
    ctx, sample = lax.axis_index("ctx"), lax.axis_index("sample")
    zl, x = ctx // X, ctx % X
    zh, y, core = sample // (Y * CORE), (sample // CORE) % Y, sample % CORE

    def at(zl_=zl, x_=x, zh_=zh, y_=y, core_=core):
        return (zl_ * X + x_, zh_ * (Y * CORE) + y_ * CORE + core_)

    sibling = at(core_=1 - core)

    def zh_by(d):
        return (zh + d + ZH) % ZH

    def y_by(d):
        return (y + d + Y) % Y

    def x_by(d):
        return (x + d + X) % X

    def zl_by(d):
        return (zl + d + ZL) % ZL

    sems = Sems(send_sem, recv_sem)
    loads = [
        pltpu.make_async_copy(src, dst, load_sem.at[k])
        for k, (src, dst) in enumerate(
            ((q_any, q_ref), (ku_any, ku_ref), (vu_any, vu_ref), (og_any, og_ref))
        )
    ]
    for made in loads:
        made.start()

    partners = [sibling]
    partners += [at(zh_=zh_by(d)) for d in range(1, ZH)]
    partners += [at(y_=y_by(d)) for d in range(1, Y)]
    partners += [at(zl_=zl_by(a), x_=x_by(b)) for a in range(ZL) for b in range(X) if a + b]
    barrier = pltpu.get_barrier_semaphore()
    for device in partners:
        pl.semaphore_signal(barrier, inc=1, device_id=device, device_id_type=MESH)
    own = jnp.concatenate(
        [prompt_ref[0].astype(F32), prompt_ref[1].astype(F32), suffix_ref[0].astype(F32)], 0
    ).astype(BF16)
    keys[zh, core, y] = own
    pl.semaphore_wait(barrier, len(partners))

    from_zh = {}
    from_y = {}
    from_core = {}
    for d in (2, 1, 3):
        block = keys.at[zh, core, y]
        from_zh[d] = sems.copy(block, block, at(zh_=zh_by(d)))

    def spread_y(dz):
        if dz:
            from_zh[dz].wait_recv()
        block = keys.at[zh_by(-dz), core, y]
        from_y[dz] = [sems.copy(block, block, at(y_=y_by(d))) for d in (2, 1, 3)]

    def to_core(dz):
        for made in from_y[dz]:
            made.wait_recv()
        part = keys.at[zh_by(-dz), core]
        from_core[dz] = sems.copy(part, part, sibling)

    spread_y(0)

    lane = lax.broadcasted_iota(jnp.int32, (1, ROWS), 1)
    row_fork = (lane * 3277) >> 16
    row_step = (lane - row_fork * (RECOMP * HEADS)) >> 2

    def project(t, carry):
        rows = pl.ds(pl.multiple_of(t * TILE, TILE), TILE)
        steps = pl.ds(t * (TILE // HEADS), TILE // HEADS)
        q = q_ref[steps].reshape(TILE, QUERY)
        og = og_ref[steps].reshape(TILE, VHEAD)
        head = lax.broadcasted_iota(jnp.int32, (TILE, NOPE), 0) & (HEADS - 1)
        q_nope = q[:, :NOPE]
        zero = jnp.zeros_like(q_nope)
        q_exp = jnp.concatenate([jnp.where(head == h, q_nope, zero) for h in range(HEADS)], 1)
        o_exp = jnp.concatenate([jnp.where(head == h, og, zero) for h in range(HEADS)], 1)
        og_exp[rows, :] = o_exp
        q_t = q_nope.T
        head_t = lax.broadcasted_iota(jnp.int32, (NOPE, TILE), 1) & (HEADS - 1)
        qn_exp_t[:, rows] = jnp.concatenate(
            [jnp.where(head_t == h, q_t, zero) for h in range(HEADS)], 0
        )
        whole = jnp.concatenate([dot(q_exp, ku_ref[...]).astype(BF16), q[:, NOPE:]], 1)
        qry[rows, :] = whole
        qry_t[:, rows] = whole.T
        grad = dot_nt(o_exp[:, :VHEAD], vu_ref[pl.ds(0, LATENT), :])
        for h in range(1, HEADS):
            grad += dot_nt(
                o_exp[:, h * VHEAD : (h + 1) * VHEAD], vu_ref[pl.ds(h * LATENT, LATENT), :]
            )
        grad = grad.astype(BF16)
        lgr[rows, :] = grad
        lgr_t[:, rows] = grad.T
        return carry

    for made in loads:
        made.wait()
    lax.fori_loop(0, TILES, project, 0)

    def gather_rows(f, carry):
        limit, prompt = carry
        mine = row_fork == f
        return jnp.where(mine, length_ref[f], limit), jnp.where(mine, fork_ref[f], prompt)

    none = jnp.zeros((1, ROWS), jnp.int32)
    row_limit, row_prompt = lax.fori_loop(0, FORKS, gather_rows, (none, none))
    row_limit = row_limit - RECOMP + row_step
    first = jnp.broadcast_to(jnp.where(row_prompt == 0, 0.0, HIDDEN), (PKEYS, ROWS))
    second = jnp.broadcast_to(jnp.where(row_prompt == 1, 0.0, HIDDEN), (PKEYS, ROWS))
    position = ctx * SKEYS + lax.broadcasted_iota(jnp.int32, (SKEYS, ROWS), 0)

    def make_bias(b, carry):
        bz, bc, by = b // (CORE * Y), (b // Y) % CORE, b % Y
        fork = bz * (Y * CORE) + by * CORE + bc
        last = jnp.where(row_fork == fork, row_limit, -1)
        seen = jnp.where(position <= last, 0.0, HIDDEN)
        bias[bz, pl.ds(pl.multiple_of((bc * Y + by) * BLOCK, BLOCK), BLOCK), :] = (
            jnp.concatenate([first, second, seen], 0)
        )
        return carry

    to_core(0)
    lax.fori_loop(0, Y * CORE * ZH, make_bias, 0)

    def scores_of(dz):
        from_core[dz].wait_recv()
        part = zh_by(-dz)
        tile = keys[part].reshape(KEYS, WIDTH)
        s = dot(tile, qry_t[...]) + bias[part]
        peak = jnp.max(s, 0, keepdims=True)
        p = jnp.exp((s - peak) * SCALE)
        score[part] = p
        grad = dot(tile[:, :LATENT], lgr_t[...])
        pgrad[part] = grad
        total = jnp.sum(p, 0, keepdims=True)
        mean = jnp.sum(p * grad, 0, keepdims=True) / total
        peaks[dz] = peak
        return part, peak, total, mean

    def merged(left, right):
        top = jnp.maximum(left[0], right[0])
        shrink_left = jnp.exp((left[0] - top) * SCALE)
        shrink_right = jnp.exp((right[0] - top) * SCALE)
        total_left, total_right = left[1] * shrink_left, right[1] * shrink_right
        total = total_left + total_right
        mean = (total_left * left[2] + total_right * right[2]) / total
        return (top, total, mean), shrink_left, shrink_right

    def sums_of(part, mean):
        tile_t = keys[part].reshape(KEYS, WIDTH).T
        p = score[part]
        return dot(tile_t, p.astype(BF16)), dot(
            tile_t, (p * (pgrad[part] - mean)).astype(BF16)
        )

    def add_sums(state, new, part):
        both, shrink_left, shrink_right = merged(state, new)
        acc, grad = sums_of(part, new[2])
        old = acc_t[...]
        acc_t[...] = shrink_left * old + shrink_right * acc
        dif_t[...] = shrink_left * (dif_t[...] + (state[2] - both[2]) * old) + shrink_right * (
            grad + (new[2] - both[2]) * acc
        )
        return both

    part, *state = scores_of(0)
    spread_y(1)
    spread_y(3)
    acc_t[...], dif_t[...] = sums_of(part, state[2])
    to_core(1)
    to_core(3)
    spread_y(2)
    part, *new = scores_of(1)
    state = add_sums(state, new, part)
    to_core(2)
    part, *new = scores_of(3)
    state = add_sums(state, new, part)
    part, *new = scores_of(2)
    (peak, total, mean), _, _ = merged(state, new)

    delta = mean * total
    for t in range(TILES):
        cols = slice(t * TILE, (t + 1) * TILE)
        stat[t : t + 1, :] = peak[:, cols]
        stat[TILES + t : TILES + t + 1, :] = total[:, cols]
        stat[2 * TILES + t : 2 * TILES + t + 1, :] = delta[:, cols]
    stat[3 * TILES : 3 * TILES + 1, :] = jnp.zeros((1, TILE), F32)
    stat_copies = []
    for a in range(ZL):
        for b in range(X):
            if a + b:
                stat_copies.append(
                    sems.copy(stat, stat_all.at[ctx], at(zl_=zl_by(a), x_=x_by(b)))
                )
    stat_all[ctx] = stat[...]

    add_sums(state, new, part)

    for made in stat_copies:
        made.wait_recv()
    all_peak = stat_all[:, 0:TILES, :]
    top = jnp.max(all_peak, 0)
    shrink = jnp.exp((all_peak - top[None]) * SCALE)
    whole_total = jnp.sum(stat_all[:, TILES : 2 * TILES, :] * shrink, 0)
    whole_delta = jnp.sum(stat_all[:, 2 * TILES : 3 * TILES, :] * shrink, 0)
    inverse = 1.0 / whole_total

    def as_row(v):
        return jnp.concatenate([v[t : t + 1, :] for t in range(TILES)], 1)

    top, inverse, row_delta = as_row(top), as_row(inverse), as_row(whole_delta * inverse)
    weight = jnp.exp((peak - top) * SCALE) * inverse

    def send_x(src, dst):
        made = {}
        for e in (2, 1, 3, 0):
            to = zl_by(e)
            made[e] = [
                sems.copy(src(x_by(d), to), dst.at[d - 1, to], at(x_=x_by(d)))
                for d in (2, 1, 3)
            ]
        return made

    def w2_rows(to_x, to_zl):
        return pl.ds(pl.multiple_of((to_x * ZL + to_zl) * W2, W2), W2)

    scaled = (acc_t[:LATENT, :] * weight).astype(BF16)
    for h in range(HEADS):
        cols = slice(h * VHEAD, (h + 1) * VHEAD)
        part = dot(scaled, og_exp[:, cols]).reshape(ZL, W1, TILE)
        w1f[h] = part
        w1b[h] = part.astype(BF16)
    w1_x = send_x(lambda *to: w1b.at[to], w1x)

    shift = row_delta - mean
    factor = weight * SCALE
    lat = (factor * (dif_t[:LATENT, :] - shift * acc_t[:LATENT, :])).astype(BF16)
    rope = factor * (dif_t[LATENT:, :] - shift * acc_t[LATENT:, :])

    def put(row, part):
        w2f[row : row + part.shape[0], :] = part
        w2b[row : row + part.shape[0], :] = part.astype(BF16)

    for b in range(LATENT // TILE):
        put(b * 512, dot_nt(qn_exp_t[...], lat[b * TILE : (b + 1) * TILE, :]))
    spread = dot(ku_ref[...], lat)
    head_of = lane & (HEADS - 1)
    nope = spread[:NOPE, :]
    for h in range(1, HEADS):
        nope = jnp.where(head_of == h, spread[h * NOPE : (h + 1) * NOPE, :], nope)
    for t in range(TILES):
        cols = slice(t * TILE, (t + 1) * TILE)
        put(2048 + t * QUERY, jnp.concatenate([nope[:, cols], rope[:, cols]], 0))
    put(2048 + TILES * QUERY, jnp.zeros((64, TILE), F32))
    w2_x = send_x(lambda *to: w2b.at[w2_rows(*to), :], w2x)

    core_sums, y_sums, zh_sums = {}, {}, {}

    def key_grads(dz):
        part = zh_by(-dz)
        p = score[part] * (jnp.exp((peaks[dz] - top) * SCALE) * inverse)
        sg = (p * (pgrad[part] - row_delta) * SCALE).astype(BF16)
        grad = dot(sg, qry[...])
        value = dot(p.astype(BF16), lgr[...])
        kgrad[part, :, :, :LATENT] = (grad[:, :LATENT] + value).reshape(CORE, Y * BLOCK, LATENT)
        kgrad[part, :, :, LATENT:] = grad[:, LATENT:].reshape(CORE, Y * BLOCK, ROPE)
        c1s[part] = kgrad[part, 1 - core].astype(BF16)
        core_sums[dz] = sems.copy(c1s.at[part], c1r.at[part], sibling)

    def add_cores(dz):
        part = zh_by(-dz)
        core_sums[dz].wait_recv()
        both = kgrad[part, core] + c1r[part].astype(F32)
        kgrad[part, core] = both
        c2s[dz] = both.reshape(Y, BLOCK, WIDTH).astype(BF16)
        y_sums[dz] = [
            sems.copy(c2s.at[dz, y_by(d)], c2r.at[dz, d - 1], at(y_=y_by(d))) for d in (2, 1, 3)
        ]

    def add_ys(dz):
        for made in y_sums[dz]:
            made.wait_recv()
        rows = pl.ds(pl.multiple_of(y * BLOCK, BLOCK), BLOCK)
        mine = kgrad[zh_by(-dz), core, rows, :]
        for i in range(Y - 1):
            mine += c2r[dz, i].astype(F32)
        if dz == 0:
            return mine
        c3s[dz - 1] = mine.astype(BF16)
        zh_sums[dz] = sems.copy(c3s.at[dz - 1], c3r.at[dz - 1], at(zh_=zh_by(-dz)))

    def sum_x(made, full, came, middle, dst):
        out = []
        for e in (2, 1, 3, 0):
            for m in made[e]:
                m.wait_recv()
            to = zl_by(e)
            add = full(to) + came[0, to].astype(F32) + came[1, to].astype(F32)
            middle[to] = (add + came[2, to].astype(F32)).astype(BF16)
            if e:
                out.append(sems.copy(middle.at[to], dst.at[e - 1], at(zl_=to)))
        return out

    def spread_x(whole, e):
        block = whole.at[x, zl_by(-e)]
        return [sems.copy(block, block, at(x_=x_by(d))) for d in (2, 1, 3)]

    def sum_zl(made, middle, came, whole):
        for m in made:
            m.wait_recv()
        add = middle[zl].astype(F32)
        for i in range(ZL - 1):
            add += came[i].astype(F32)
        whole[x, zl] = add.astype(BF16)
        block = whole.at[x, zl]
        back = {e: sems.copy(block, block, at(zl_=zl_by(e))) for e in (2, 1, 3)}
        return back, spread_x(whole, 0)

    def gather_x(back, out, whole):
        for e in (1, 3, 2):
            back[e].wait_recv()
            out += spread_x(whole, e)

    for dz in (2, 1, 3, 0):
        key_grads(dz)
    w1_z = sum_x(w1_x, lambda to: w1f[x, to], w1x, w1m, w1z)
    for dz in (2, 1, 3, 0):
        add_cores(dz)
    w1_back, w1_x = sum_zl(w1_z, w1m, w1z, w1a)
    w2_z = sum_x(w2_x, lambda to: w2f[w2_rows(x, to), :], w2x, w2m, w2z)
    for dz in (2, 1, 3):
        add_ys(dz)
    final = add_ys(0)
    gather_x(w1_back, w1_x, w1a)
    w2_back, w2_x = sum_zl(w2_z, w2m, w2z, w2a)
    gather_x(w2_back, w2_x, w2a)

    for dz in (1, 3, 2):
        zh_sums[dz].wait_recv()
        final += c3r[dz - 1].astype(F32)
    keys_out[...] = final
    for made in w1_x:
        made.wait_recv()
    w1_out[...] = w1a[...].reshape(HEADS * LATENT, VHEAD)
    for made in w2_x:
        made.wait_recv()
    w2_out[...] = w2a[...].reshape(X * ZL * W2, TILE)
    for made in sems.started:
        made.wait_send()


def unpack(keys_ref, w1_ref, w2_ref, prompt_out, suffix_out, query_out, key_up_out, value_up_out):
    prompt_out[0] = keys_ref[:PKEYS, :]
    prompt_out[1] = keys_ref[PKEYS : 2 * PKEYS, :]
    suffix_out[0] = keys_ref[2 * PKEYS :, :]
    value_up_out[...] = w1_ref[...].astype(F32)
    for b in range(LATENT // TILE):
        key_up_out[:, b * TILE : (b + 1) * TILE] = w2_ref[b * 512 : (b + 1) * 512, :].astype(F32)
    steps = TILE // HEADS
    for t in range(TILES):
        base = 2048 + t * QUERY
        part = w2_ref[base : base + QUERY, :].astype(F32).T
        query_out[t * steps : (t + 1) * steps] = part.reshape(steps, HEADS, QUERY)


def shards(prompt, suffix, queries, key_up, value_up, out_grad, fork_prompt, suffix_length):
    vmem = pl.BlockSpec(memory_space=pltpu.VMEM)
    smem = pl.BlockSpec(memory_space=pltpu.SMEM)
    copies = 128
    hbm = pl.BlockSpec(memory_space=pltpu.HBM)

    def in_hbm(v):
        return pltpu.with_memory_space_constraint(v, pltpu.HBM)

    steps = FORKS * RECOMP
    sums = pl.pallas_call(
        kernel,
        out_shape=(
            jax.ShapeDtypeStruct((BLOCK, WIDTH), F32),
            jax.ShapeDtypeStruct((HEADS * LATENT, VHEAD), BF16),
            jax.ShapeDtypeStruct((X * ZL * W2, TILE), BF16),
        ),
        in_specs=[vmem] * 2 + [hbm] * 4 + [smem] * 2,
        out_specs=(vmem,) * 3,
        scratch_shapes=[
            pltpu.VMEM((ZH, CORE, Y, BLOCK, WIDTH), BF16),
            pltpu.VMEM((ROWS, WIDTH), BF16),
            pltpu.VMEM((WIDTH, ROWS), BF16),
            pltpu.VMEM((ROWS, LATENT), BF16),
            pltpu.VMEM((LATENT, ROWS), BF16),
            pltpu.VMEM((ROWS, HEADS * VHEAD), BF16),
            pltpu.VMEM((HEADS * NOPE, ROWS), BF16),
            pltpu.VMEM((ZH, KEYS, ROWS), F32),
            pltpu.VMEM((ZH, KEYS, ROWS), F32),
            pltpu.VMEM((ZH, KEYS, ROWS), F32),
            pltpu.VMEM((ZH, 1, ROWS), F32),
            pltpu.VMEM((WIDTH, ROWS), F32),
            pltpu.VMEM((WIDTH, ROWS), F32),
            pltpu.VMEM((ZH, CORE, Y * BLOCK, WIDTH), F32),
            pltpu.VMEM((16, TILE), F32),
            pltpu.VMEM((ZL * X, 16, TILE), F32),
            pltpu.VMEM((ZH, Y * BLOCK, WIDTH), BF16),
            pltpu.VMEM((ZH, Y * BLOCK, WIDTH), BF16),
            pltpu.VMEM((ZH, Y, BLOCK, WIDTH), BF16),
            pltpu.VMEM((ZH, Y - 1, BLOCK, WIDTH), BF16),
            pltpu.VMEM((ZH - 1, BLOCK, WIDTH), BF16),
            pltpu.VMEM((ZH - 1, BLOCK, WIDTH), BF16),
            pltpu.VMEM((X, ZL, W1, TILE), F32),
            pltpu.VMEM((X, ZL, W1, TILE), BF16),
            pltpu.VMEM((X - 1, ZL, W1, TILE), BF16),
            pltpu.VMEM((ZL, W1, TILE), BF16),
            pltpu.VMEM((ZL - 1, W1, TILE), BF16),
            pltpu.VMEM((X, ZL, W1, TILE), BF16),
            pltpu.VMEM((X * ZL * W2, TILE), F32),
            pltpu.VMEM((X * ZL * W2, TILE), BF16),
            pltpu.VMEM((X - 1, ZL, W2, TILE), BF16),
            pltpu.VMEM((ZL, W2, TILE), BF16),
            pltpu.VMEM((ZL - 1, W2, TILE), BF16),
            pltpu.VMEM((X, ZL, W2, TILE), BF16),
            pltpu.VMEM((steps, HEADS, QUERY), BF16),
            pltpu.VMEM((HEADS * NOPE, LATENT), BF16),
            pltpu.VMEM((HEADS * LATENT, VHEAD), BF16),
            pltpu.VMEM((steps, HEADS, VHEAD), BF16),
            pltpu.SemaphoreType.DMA((copies,)),
            pltpu.SemaphoreType.DMA((copies,)),
            pltpu.SemaphoreType.DMA((4,)),
        ],
        compiler_params=pltpu.CompilerParams(
            collective_id=0, has_side_effects=True, vmem_limit_bytes=42 << 20
        ),
        cost_estimate=pl.CostEstimate(
            flops=8_000_000_000, bytes_accessed=6_000_000, transcendentals=700_000
        ),
        name="latent_backward",
    )(
        prompt,
        suffix,
        in_hbm(queries.reshape(steps, HEADS, QUERY)),
        in_hbm(key_up.reshape(HEADS * NOPE, LATENT)),
        in_hbm(value_up.reshape(HEADS * LATENT, VHEAD)),
        in_hbm(out_grad.reshape(steps, HEADS, VHEAD)),
        fork_prompt,
        suffix_length,
    )
    prompt_grad, suffix_grad, query_grad, key_up_grad, value_up_grad = pl.pallas_call(
        unpack,
        out_shape=(
            jax.ShapeDtypeStruct((2, PKEYS, WIDTH), F32),
            jax.ShapeDtypeStruct((1, SKEYS, WIDTH), F32),
            jax.ShapeDtypeStruct((steps, HEADS, QUERY), F32),
            jax.ShapeDtypeStruct((HEADS * NOPE, LATENT), F32),
            jax.ShapeDtypeStruct((HEADS * LATENT, VHEAD), F32),
        ),
        in_specs=[vmem] * 3,
        out_specs=(vmem,) * 5,
        compiler_params=pltpu.CompilerParams(vmem_limit_bytes=16 << 20),
        name="unpack_grads",
    )(*sums)
    return (
        prompt_grad,
        suffix_grad,
        query_grad.reshape(FORKS, RECOMP, HEADS, QUERY),
        key_up_grad.reshape(HEADS, NOPE, LATENT),
        value_up_grad.reshape(HEADS, LATENT, VHEAD),
    )


def solution(mesh):
    return jax.shard_map(
        shards,
        mesh=mesh,
        in_specs=(
            P(None, ("ctx", "sample"), None),
            P("sample", "ctx", None),
            P(None, None, "sample", None),
            P("sample", None, None),
            P("sample", None, None),
            P(None, None, "sample", None),
            P(),
            P(),
        ),
        out_specs=(
            P(None, ("ctx", "sample"), None),
            P("sample", "ctx", None),
            P(None, None, "sample", None),
            P("sample", None, None),
            P("sample", None, None),
        ),
        check_vma=False,
    )
```

```python
import functools

import jax
import jax.numpy as jnp
from jax import lax
from jax.experimental import pallas as pl
from jax.experimental.pallas import tpu as pltpu
from jax.sharding import PartitionSpec as P

MESH = pl.DeviceIdType.MESH
F32 = jnp.float32
BF16 = jnp.bfloat16
HIDDEN = -1e30

ZL, X, ZH, Y, CORE = 4, 4, 4, 4, 2
FORKS, RECOMP, HEADS = 32, 5, 4
NOPE, ROPE, LATENT, VHEAD = 128, 64, 512, 128
WIDTH = LATENT + ROPE
QUERY = NOPE + ROPE
ROWS = FORKS * RECOMP * HEADS
TILE = 128
TILES = ROWS // TILE
PKEYS, SKEYS = 8, 16
BLOCK = 2 * PKEYS + SKEYS
KEYS = CORE * Y * BLOCK
SCALE = QUERY**-0.5
W1 = HEADS * LATENT
W2 = HEADS * NOPE * LATENT // TILE
W3 = 1024


def dot(a, b):
    return jnp.dot(a, b, preferred_element_type=F32)


def dot_nt(a, b):
    return lax.dot_general(a, b, (((1,), (1,)), ((), ())), preferred_element_type=F32)


class Sems:
    def __init__(self, send, recv):
        self.send, self.recv, self.used, self.started = send, recv, 0, []

    def copy(self, src, dst, device):
        k = self.used
        self.used += 1
        made = pltpu.make_async_remote_copy(
            src_ref=src,
            dst_ref=dst,
            send_sem=self.send.at[k],
            recv_sem=self.recv.at[k],
            device_id=device,
            device_id_type=MESH,
        )
        made.start()
        self.started.append(made)
        return made


def kernel(
    prompt_ref, suffix_ref, q_any, ku_any, vu_any, og_any, fork_ref, length_ref,
    keys_out, w1_out, w2_out, w3_out,
    keys, qry, qry_t, lgr, lgr_t, og_exp, qn_exp_t, bias, score, pgrad, peaks,
    acc_t, dif_t, kgrad, stat, stat_all, c1s, c1r, c2s, c2r, c3s, c3h, c3r,
    w1f, w1b, w1x, w1m, w1z, w1a, w2f, w2b, w2x, w2m, w2z, w2a, w3f, w3b, w3x, w3m, w3z, w3a,
    q_ref, ku_ref, vu_ref, og_ref, send_sem, recv_sem, load_sem,
):
    ctx, sample = lax.axis_index("ctx"), lax.axis_index("sample")
    zl, x = ctx // X, ctx % X
    zh, y, core = sample // (Y * CORE), (sample // CORE) % Y, sample % CORE

    def at(zl_=zl, x_=x, zh_=zh, y_=y, core_=core):
        return (zl_ * X + x_, zh_ * (Y * CORE) + y_ * CORE + core_)

    sibling = at(core_=1 - core)

    def zh_by(d):
        return (zh + d + ZH) % ZH

    def y_by(d):
        return (y + d + Y) % Y

    def x_by(d):
        return (x + d + X) % X

    def zl_by(d):
        return (zl + d + ZL) % ZL

    sems = Sems(send_sem, recv_sem)
    loads = [
        pltpu.make_async_copy(src, dst, load_sem.at[k])
        for k, (src, dst) in enumerate(
            ((q_any, q_ref), (ku_any, ku_ref), (vu_any, vu_ref), (og_any, og_ref))
        )
    ]
    for made in loads:
        made.start()

    partners = [sibling]
    partners += [at(zh_=zh_by(d)) for d in (1, -1)]
    partners += [at(y_=y_by(d)) for d in range(1, Y)]
    partners += [at(zl_=zl_by(a), x_=x_by(b)) for a in range(ZL) for b in range(X) if a + b]
    barrier = pltpu.get_barrier_semaphore()
    for device in partners:
        pl.semaphore_signal(barrier, inc=1, device_id=device, device_id_type=MESH)
    own = jnp.concatenate(
        [prompt_ref[0].astype(F32), prompt_ref[1].astype(F32), suffix_ref[0].astype(F32)], 0
    ).astype(BF16)
    keys[zh, core, y] = own
    pl.semaphore_wait(barrier, len(partners))

    from_zh = {}
    from_y = {}
    from_core = {}
    for d in (1, 3):
        block = keys.at[zh, core, y]
        from_zh[d] = [sems.copy(block, block, at(zh_=zh_by(d)))]
    half = BLOCK // 2

    def relay(d, rows):
        from_zh[d][0].wait_recv()
        part = keys.at[zh_by(-d), core, y, rows]
        from_zh.setdefault(2, []).append(sems.copy(part, part, at(zh_=zh_by(d))))

    def spread_y(dz):
        if dz == 2:
            for made in from_zh[dz]:
                made.wait_recv()
        block = keys.at[zh_by(-dz), core, y]
        from_y[dz] = [sems.copy(block, block, at(y_=y_by(d))) for d in (2, 1, 3)]

    def to_core(dz):
        for made in from_y[dz]:
            made.wait_recv()
        part = keys.at[zh_by(-dz), core]
        from_core[dz] = sems.copy(part, part, sibling)

    spread_y(0)

    lane = lax.broadcasted_iota(jnp.int32, (1, ROWS), 1)
    row_fork = (lane * 3277) >> 16
    row_step = (lane - row_fork * (RECOMP * HEADS)) >> 2

    def project(t, carry):
        rows = pl.ds(pl.multiple_of(t * TILE, TILE), TILE)
        steps = pl.ds(t * (TILE // HEADS), TILE // HEADS)
        q = q_ref[steps].reshape(TILE, QUERY)
        og = og_ref[steps].reshape(TILE, VHEAD)
        head = lax.broadcasted_iota(jnp.int32, (TILE, NOPE), 0) & (HEADS - 1)
        q_nope = q[:, :NOPE]
        zero = jnp.zeros_like(q_nope)
        q_exp = jnp.concatenate([jnp.where(head == h, q_nope, zero) for h in range(HEADS)], 1)
        o_exp = jnp.concatenate([jnp.where(head == h, og, zero) for h in range(HEADS)], 1)
        og_exp[rows, :] = o_exp
        q_t = q_nope.T
        head_t = lax.broadcasted_iota(jnp.int32, (NOPE, TILE), 1) & (HEADS - 1)
        qn_exp_t[:, rows] = jnp.concatenate(
            [jnp.where(head_t == h, q_t, zero) for h in range(HEADS)], 0
        )
        whole = jnp.concatenate([dot(q_exp, ku_ref[...]).astype(BF16), q[:, NOPE:]], 1)
        qry[rows, :] = whole
        qry_t[:, rows] = whole.T
        grad = dot_nt(o_exp[:, :VHEAD], vu_ref[pl.ds(0, LATENT), :])
        for h in range(1, HEADS):
            grad += dot_nt(
                o_exp[:, h * VHEAD : (h + 1) * VHEAD], vu_ref[pl.ds(h * LATENT, LATENT), :]
            )
        grad = grad.astype(BF16)
        lgr[rows, :] = grad
        lgr_t[:, rows] = grad.T
        return carry

    for made in loads:
        made.wait()
    lax.fori_loop(0, 2, project, 0)
    relay(1, pl.ds(0, half))
    relay(3, pl.ds(half, half))
    spread_y(1)
    spread_y(3)
    lax.fori_loop(2, TILES, project, 0)

    def gather_rows(f, carry):
        limit, prompt = carry
        mine = row_fork == f
        return jnp.where(mine, length_ref[f], limit), jnp.where(mine, fork_ref[f], prompt)

    none = jnp.zeros((1, ROWS), jnp.int32)
    row_limit, row_prompt = lax.fori_loop(0, FORKS, gather_rows, (none, none))
    row_limit = row_limit - RECOMP + row_step
    first = jnp.broadcast_to(jnp.where(row_prompt == 0, 0.0, HIDDEN), (PKEYS, ROWS))
    second = jnp.broadcast_to(jnp.where(row_prompt == 1, 0.0, HIDDEN), (PKEYS, ROWS))
    position = ctx * SKEYS + lax.broadcasted_iota(jnp.int32, (SKEYS, ROWS), 0)

    def make_bias(b, carry):
        bz, bc, by = b // (CORE * Y), (b // Y) % CORE, b % Y
        fork = bz * (Y * CORE) + by * CORE + bc
        last = jnp.where(row_fork == fork, row_limit, -1)
        seen = jnp.where(position <= last, 0.0, HIDDEN)
        bias[bz, pl.ds(pl.multiple_of((bc * Y + by) * BLOCK, BLOCK), BLOCK), :] = (
            jnp.concatenate([first, second, seen], 0)
        )
        return carry

    to_core(0)
    lax.fori_loop(0, Y * CORE * ZH, make_bias, 0)

    def scores_of(dz):
        from_core[dz].wait_recv()
        part = zh_by(-dz)
        tile = keys[part].reshape(KEYS, WIDTH)
        s = dot(tile, qry_t[...]) + bias[part]
        peak = jnp.max(s, 0, keepdims=True)
        p = jnp.exp((s - peak) * SCALE)
        score[part] = p
        grad = dot(tile[:, :LATENT], lgr_t[...])
        pgrad[part] = grad
        total = jnp.sum(p, 0, keepdims=True)
        mean = jnp.sum(p * grad, 0, keepdims=True) / total
        peaks[dz] = peak
        return part, peak, total, mean

    def merged(left, right):
        top = jnp.maximum(left[0], right[0])
        shrink_left = jnp.exp((left[0] - top) * SCALE)
        shrink_right = jnp.exp((right[0] - top) * SCALE)
        total_left, total_right = left[1] * shrink_left, right[1] * shrink_right
        total = total_left + total_right
        mean = (total_left * left[2] + total_right * right[2]) / total
        return (top, total, mean), shrink_left, shrink_right

    def sums_of(part, mean):
        tile_t = keys[part].reshape(KEYS, WIDTH).T
        p = score[part]
        return dot(tile_t, p.astype(BF16)), dot(
            tile_t, (p * (pgrad[part] - mean)).astype(BF16)
        )

    def add_sums(state, new, part):
        both, shrink_left, shrink_right = merged(state, new)
        acc, grad = sums_of(part, new[2])
        old = acc_t[...]
        acc_t[...] = shrink_left * old + shrink_right * acc
        dif_t[...] = shrink_left * (dif_t[...] + (state[2] - both[2]) * old) + shrink_right * (
            grad + (new[2] - both[2]) * acc
        )
        return both

    part, *state = scores_of(0)
    acc_t[...], dif_t[...] = sums_of(part, state[2])
    to_core(1)
    to_core(3)
    spread_y(2)
    part, *new = scores_of(1)
    state = add_sums(state, new, part)
    to_core(2)
    part, *new = scores_of(3)
    state = add_sums(state, new, part)
    part, *new = scores_of(2)
    (peak, total, mean), _, _ = merged(state, new)

    delta = mean * total
    for t in range(TILES):
        cols = slice(t * TILE, (t + 1) * TILE)
        stat[t : t + 1, :] = peak[:, cols]
        stat[TILES + t : TILES + t + 1, :] = total[:, cols]
        stat[2 * TILES + t : 2 * TILES + t + 1, :] = delta[:, cols]
    stat[3 * TILES : 3 * TILES + 1, :] = jnp.zeros((1, TILE), F32)
    stat_copies = []
    for a in range(ZL):
        for b in range(X):
            if a + b:
                stat_copies.append(
                    sems.copy(stat, stat_all.at[ctx], at(zl_=zl_by(a), x_=x_by(b)))
                )
    stat_all[ctx] = stat[...]

    add_sums(state, new, part)

    for made in stat_copies:
        made.wait_recv()
    all_peak = stat_all[:, 0:TILES, :]
    top = jnp.max(all_peak, 0)
    shrink = jnp.exp((all_peak - top[None]) * SCALE)
    whole_total = jnp.sum(stat_all[:, TILES : 2 * TILES, :] * shrink, 0)
    whole_delta = jnp.sum(stat_all[:, 2 * TILES : 3 * TILES, :] * shrink, 0)
    inverse = 1.0 / whole_total

    def as_row(v):
        return jnp.concatenate([v[t : t + 1, :] for t in range(TILES)], 1)

    top, inverse, row_delta = as_row(top), as_row(inverse), as_row(whole_delta * inverse)
    weight = jnp.exp((peak - top) * SCALE) * inverse

    class Part:
        def __init__(self, full, sent, from_x, middle, from_zl, whole):
            self.full, self.sent, self.from_x = full, sent, from_x
            self.middle, self.from_zl, self.whole = middle, from_zl, whole
            self.rows = full.shape[0] // (X * ZL)

        def block(self, to_x, to_zl):
            return pl.ds(pl.multiple_of((to_x * ZL + to_zl) * self.rows, self.rows), self.rows)

        def put(self, row, part):
            self.full[row : row + part.shape[0], :] = part
            self.sent[row : row + part.shape[0], :] = part.astype(BF16)

        def send_x(self):
            self.at_x = {}
            for e in (2, 1, 3, 0):
                to = zl_by(e)
                self.at_x[e] = [
                    sems.copy(
                        self.sent.at[self.block(x_by(d), to), :],
                        self.from_x.at[d - 1, to],
                        at(x_=x_by(d)),
                    )
                    for d in (2, 1, 3)
                ]

        def sum_x(self):
            self.at_zl = []
            for e in (2, 1, 3, 0):
                for made in self.at_x[e]:
                    made.wait_recv()
                to = zl_by(e)
                add = self.full[self.block(x, to), :]
                for i in range(X - 1):
                    add += self.from_x[i, to].astype(F32)
                self.middle[to] = add.astype(BF16)
                if e:
                    self.at_zl.append(
                        sems.copy(self.middle.at[to], self.from_zl.at[e - 1], at(zl_=to))
                    )

        def spread_x(self, e):
            block = self.whole.at[self.block(x, zl_by(-e)), :]
            return [sems.copy(block, block, at(x_=x_by(d))) for d in (2, 1, 3)]

        def sum_zl(self):
            for made in self.at_zl:
                made.wait_recv()
            add = self.middle[zl].astype(F32)
            for i in range(ZL - 1):
                add += self.from_zl[i].astype(F32)
            own = self.block(x, zl)
            self.whole[own, :] = add.astype(BF16)
            block = self.whole.at[own, :]
            self.back = {e: sems.copy(block, block, at(zl_=zl_by(e))) for e in (2, 1, 3)}
            self.out = self.spread_x(0)

        def gather_x(self):
            for e in (1, 3, 2):
                self.back[e].wait_recv()
                self.out += self.spread_x(e)

        def done(self, result):
            for made in self.out:
                made.wait_recv()
            result[...] = self.whole[...]

    value_part = Part(w1f, w1b, w1x, w1m, w1z, w1a)
    key_part = Part(w2f, w2b, w2x, w2m, w2z, w2a)
    query_part = Part(w3f, w3b, w3x, w3m, w3z, w3a)
    scaled = (acc_t[:LATENT, :] * weight).astype(BF16)
    for h in range(HEADS):
        cols = slice(h * VHEAD, (h + 1) * VHEAD)
        value_part.put(h * LATENT, dot(scaled, og_exp[:, cols]))
    value_part.send_x()

    shift = row_delta - mean
    factor = weight * SCALE
    lat = (factor * (dif_t[:LATENT, :] - shift * acc_t[:LATENT, :])).astype(BF16)
    rope = factor * (dif_t[LATENT:, :] - shift * acc_t[LATENT:, :])
    for b in range(LATENT // TILE):
        key_part.put(
            b * HEADS * NOPE, dot_nt(qn_exp_t[...], lat[b * TILE : (b + 1) * TILE, :])
        )
    key_part.send_x()
    spread = dot(ku_ref[...], lat)
    head_of = lane & (HEADS - 1)
    nope = spread[:NOPE, :]
    for h in range(1, HEADS):
        nope = jnp.where(head_of == h, spread[h * NOPE : (h + 1) * NOPE, :], nope)
    for t in range(TILES):
        cols = slice(t * TILE, (t + 1) * TILE)
        query_part.put(t * QUERY, jnp.concatenate([nope[:, cols], rope[:, cols]], 0))
    query_part.put(TILES * QUERY, jnp.zeros((W3 - TILES * QUERY, TILE), F32))
    query_part.send_x()

    core_sums, y_sums, zh_sums = {}, {}, {}

    def key_grads(dz):
        part = zh_by(-dz)
        p = score[part] * (jnp.exp((peaks[dz] - top) * SCALE) * inverse)
        sg = (p * (pgrad[part] - row_delta) * SCALE).astype(BF16)
        grad = dot(sg, qry[...])
        value = dot(p.astype(BF16), lgr[...])
        kgrad[part, :, :, :LATENT] = (grad[:, :LATENT] + value).reshape(CORE, Y * BLOCK, LATENT)
        kgrad[part, :, :, LATENT:] = grad[:, LATENT:].reshape(CORE, Y * BLOCK, ROPE)
        c1s[part] = kgrad[part, 1 - core].astype(BF16)
        core_sums[dz] = sems.copy(c1s.at[part], c1r.at[part], sibling)

    def add_cores(dz):
        part = zh_by(-dz)
        core_sums[dz].wait_recv()
        both = kgrad[part, core] + c1r[part].astype(F32)
        kgrad[part, core] = both
        c2s[dz] = both.reshape(Y, BLOCK, WIDTH).astype(BF16)
        y_sums[dz] = [
            sems.copy(c2s.at[dz, y_by(d)], c2r.at[dz, d - 1], at(y_=y_by(d))) for d in (2, 1, 3)
        ]

    def add_ys(dz):
        for made in y_sums[dz]:
            made.wait_recv()
        rows = pl.ds(pl.multiple_of(y * BLOCK, BLOCK), BLOCK)
        mine = kgrad[zh_by(-dz), core, rows, :]
        for i in range(Y - 1):
            mine += c2r[dz, i].astype(F32)
        return mine

    def send_far(mine):
        c3s[2] = mine.astype(BF16)
        return [
            sems.copy(c3s.at[2, pl.ds(0, half)], c3h.at[0], at(zh_=zh_by(1))),
            sems.copy(c3s.at[2, pl.ds(half, half)], c3h.at[1], at(zh_=zh_by(-1))),
        ]

    def send_near(halves, up, down):
        for made in halves:
            made.wait_recv()
        c3s[0, :half] = (up[:half] + c3h[0].astype(F32)).astype(BF16)
        c3s[0, half:] = up[half:].astype(BF16)
        c3s[1, :half] = down[:half].astype(BF16)
        c3s[1, half:] = (down[half:] + c3h[1].astype(F32)).astype(BF16)
        return [
            sems.copy(c3s.at[0], c3r.at[0], at(zh_=zh_by(1))),
            sems.copy(c3s.at[1], c3r.at[1], at(zh_=zh_by(-1))),
        ]

    for dz in (2, 1, 3, 0):
        key_grads(dz)
    value_part.sum_x()
    for dz in (2, 1, 3, 0):
        add_cores(dz)
    key_part.sum_x()
    query_part.sum_x()
    halves = send_far(add_ys(2))
    value_part.sum_zl()
    up, down, final = add_ys(3), add_ys(1), add_ys(0)
    key_part.sum_zl()
    value_part.gather_x()
    query_part.sum_zl()
    near = send_near(halves, up, down)
    key_part.gather_x()
    query_part.gather_x()

    for made in near:
        made.wait_recv()
    keys_out[...] = final + c3r[0].astype(F32) + c3r[1].astype(F32)
    value_part.done(w1_out)
    key_part.done(w2_out)
    query_part.done(w3_out)
    for made in sems.started:
        made.wait_send()


def unpack(
    keys_ref, w1_ref, w2_ref, w3_ref,
    prompt_out, suffix_out, query_out, key_up_out, value_up_out,
):
    prompt_out[0] = keys_ref[:PKEYS, :]
    prompt_out[1] = keys_ref[PKEYS : 2 * PKEYS, :]
    suffix_out[0] = keys_ref[2 * PKEYS :, :]
    value_up_out[...] = w1_ref[...].astype(F32)
    for b in range(LATENT // TILE):
        key_up_out[:, b * TILE : (b + 1) * TILE] = w2_ref[b * 512 : (b + 1) * 512, :].astype(F32)
    steps = TILE // HEADS
    for t in range(TILES):
        part = w3_ref[t * QUERY : (t + 1) * QUERY, :].astype(F32).T
        query_out[t * steps : (t + 1) * steps] = part.reshape(steps, HEADS, QUERY)


def part_scratch(rows):
    block = rows // (X * ZL)
    return (
        pltpu.VMEM((rows, TILE), F32),
        pltpu.VMEM((rows, TILE), BF16),
        pltpu.VMEM((X - 1, ZL, block, TILE), BF16),
        pltpu.VMEM((ZL, block, TILE), BF16),
        pltpu.VMEM((ZL - 1, block, TILE), BF16),
        pltpu.VMEM((rows, TILE), BF16),
    )


def shards(prompt, suffix, queries, key_up, value_up, out_grad, fork_prompt, suffix_length):
    vmem = pl.BlockSpec(memory_space=pltpu.VMEM)
    smem = pl.BlockSpec(memory_space=pltpu.SMEM)
    copies = 152
    hbm = pl.BlockSpec(memory_space=pltpu.HBM)

    def in_hbm(v):
        return pltpu.with_memory_space_constraint(v, pltpu.HBM)

    steps = FORKS * RECOMP
    sums = pl.pallas_call(
        kernel,
        out_shape=(
            jax.ShapeDtypeStruct((BLOCK, WIDTH), F32),
            jax.ShapeDtypeStruct((W1, TILE), BF16),
            jax.ShapeDtypeStruct((W2, TILE), BF16),
            jax.ShapeDtypeStruct((W3, TILE), BF16),
        ),
        in_specs=[vmem] * 2 + [hbm] * 4 + [smem] * 2,
        out_specs=(vmem,) * 4,
        scratch_shapes=[
            pltpu.VMEM((ZH, CORE, Y, BLOCK, WIDTH), BF16),
            pltpu.VMEM((ROWS, WIDTH), BF16),
            pltpu.VMEM((WIDTH, ROWS), BF16),
            pltpu.VMEM((ROWS, LATENT), BF16),
            pltpu.VMEM((LATENT, ROWS), BF16),
            pltpu.VMEM((ROWS, HEADS * VHEAD), BF16),
            pltpu.VMEM((HEADS * NOPE, ROWS), BF16),
            pltpu.VMEM((ZH, KEYS, ROWS), F32),
            pltpu.VMEM((ZH, KEYS, ROWS), F32),
            pltpu.VMEM((ZH, KEYS, ROWS), F32),
            pltpu.VMEM((ZH, 1, ROWS), F32),
            pltpu.VMEM((WIDTH, ROWS), F32),
            pltpu.VMEM((WIDTH, ROWS), F32),
            pltpu.VMEM((ZH, CORE, Y * BLOCK, WIDTH), F32),
            pltpu.VMEM((16, TILE), F32),
            pltpu.VMEM((ZL * X, 16, TILE), F32),
            pltpu.VMEM((ZH, Y * BLOCK, WIDTH), BF16),
            pltpu.VMEM((ZH, Y * BLOCK, WIDTH), BF16),
            pltpu.VMEM((ZH, Y, BLOCK, WIDTH), BF16),
            pltpu.VMEM((ZH, Y - 1, BLOCK, WIDTH), BF16),
            pltpu.VMEM((ZH - 1, BLOCK, WIDTH), BF16),
            pltpu.VMEM((2, BLOCK // 2, WIDTH), BF16),
            pltpu.VMEM((2, BLOCK, WIDTH), BF16),
            *part_scratch(W1),
            *part_scratch(W2),
            *part_scratch(W3),
            pltpu.VMEM((steps, HEADS, QUERY), BF16),
            pltpu.VMEM((HEADS * NOPE, LATENT), BF16),
            pltpu.VMEM((HEADS * LATENT, VHEAD), BF16),
            pltpu.VMEM((steps, HEADS, VHEAD), BF16),
            pltpu.SemaphoreType.DMA((copies,)),
            pltpu.SemaphoreType.DMA((copies,)),
            pltpu.SemaphoreType.DMA((4,)),
        ],
        compiler_params=pltpu.CompilerParams(
            collective_id=0, has_side_effects=True, vmem_limit_bytes=42 << 20
        ),
        cost_estimate=pl.CostEstimate(
            flops=8_000_000_000, bytes_accessed=6_000_000, transcendentals=700_000
        ),
        name="latent_backward",
    )(
        in_hbm(prompt),
        in_hbm(suffix),
        in_hbm(queries.reshape(steps, HEADS, QUERY)),
        in_hbm(key_up.reshape(HEADS * NOPE, LATENT)),
        in_hbm(value_up.reshape(HEADS * LATENT, VHEAD)),
        in_hbm(out_grad.reshape(steps, HEADS, VHEAD)),
        in_hbm(fork_prompt),
        in_hbm(suffix_length),
    )
    prompt_grad, suffix_grad, query_grad, key_up_grad, value_up_grad = pl.pallas_call(
        unpack,
        out_shape=(
            jax.ShapeDtypeStruct((2, PKEYS, WIDTH), F32),
            jax.ShapeDtypeStruct((1, SKEYS, WIDTH), F32),
            jax.ShapeDtypeStruct((steps, HEADS, QUERY), F32),
            jax.ShapeDtypeStruct((HEADS * NOPE, LATENT), F32),
            jax.ShapeDtypeStruct((HEADS * LATENT, VHEAD), F32),
        ),
        in_specs=[vmem] * 4,
        out_specs=(vmem,) * 5,
        compiler_params=pltpu.CompilerParams(vmem_limit_bytes=16 << 20),
        name="unpack_grads",
    )(*sums)
    return (
        prompt_grad,
        suffix_grad,
        query_grad.reshape(FORKS, RECOMP, HEADS, QUERY),
        key_up_grad.reshape(HEADS, NOPE, LATENT),
        value_up_grad.reshape(HEADS, LATENT, VHEAD),
    )


def solution(mesh):
    return jax.shard_map(
        shards,
        mesh=mesh,
        in_specs=(
            P(None, ("ctx", "sample"), None),
            P("sample", "ctx", None),
            P(None, None, "sample", None),
            P("sample", None, None),
            P("sample", None, None),
            P(None, None, "sample", None),
            P(),
            P(),
        ),
        out_specs=(
            P(None, ("ctx", "sample"), None),
            P("sample", "ctx", None),
            P(None, None, "sample", None),
            P("sample", None, None),
            P("sample", None, None),
        ),
        check_vma=False,
    )
```

```python
import functools

import jax
import jax.numpy as jnp
from jax import lax
from jax.experimental import pallas as pl
from jax.experimental.pallas import tpu as pltpu
from jax.sharding import PartitionSpec as P

MESH = pl.DeviceIdType.MESH
F32 = jnp.float32
BF16 = jnp.bfloat16
HIDDEN = -1e30

ZL, X, ZH, Y, CORE = 4, 4, 4, 4, 2
FORKS, RECOMP, HEADS = 32, 5, 4
NOPE, ROPE, LATENT, VHEAD = 128, 64, 512, 128
WIDTH = LATENT + ROPE
QUERY = NOPE + ROPE
ROWS = FORKS * RECOMP * HEADS
TILE = 128
TILES = ROWS // TILE
PKEYS, SKEYS = 8, 16
BLOCK = 2 * PKEYS + SKEYS
KEYS = CORE * Y * BLOCK
SCALE = QUERY**-0.5
COLS = LATENT // (X * ZL)
RCOLS = ROPE // X


def dot(a, b):
    return jnp.dot(a, b, preferred_element_type=F32)


def dot_nt(a, b):
    return lax.dot_general(a, b, (((1,), (1,)), ((), ())), preferred_element_type=F32)


class Sems:
    def __init__(self, send, recv):
        self.send, self.recv, self.used, self.started = send, recv, 0, []

    def copy(self, src, dst, device):
        k = self.used
        self.used += 1
        made = pltpu.make_async_remote_copy(
            src_ref=src,
            dst_ref=dst,
            send_sem=self.send.at[k],
            recv_sem=self.recv.at[k],
            device_id=device,
            device_id_type=MESH,
        )
        made.start()
        self.started.append(made)
        return made


def kernel(
    prompt_ref, suffix_ref, q_any, ku_any, vu_any, og_any, fork_ref, length_ref,
    keys_out, value_out, key_up_out, query_out,
    keys, qry, qry_t, lgr, lgr_t, og_exp, qn_exp_t, bias, score, pgrad, peaks,
    acc_t, dif_t, kgrad, stat, stat_all, c1s, c1r, c2s, c2r, c3s, c3h, c3r,
    lat_s, lat_r, lat_m, lat_z, rope_s, rope_r, rope_z, abs_a, value_a, rope_a,
    q_ref, ku_ref, vu_ref, og_ref, send_sem, recv_sem, load_sem,
):
    ctx, sample = lax.axis_index("ctx"), lax.axis_index("sample")
    zl, x = ctx // X, ctx % X
    zh, y, core = sample // (Y * CORE), (sample // CORE) % Y, sample % CORE

    def at(zl_=zl, x_=x, zh_=zh, y_=y, core_=core):
        return (zl_ * X + x_, zh_ * (Y * CORE) + y_ * CORE + core_)

    sibling = at(core_=1 - core)

    def zh_by(d):
        return (zh + d + ZH) % ZH

    def y_by(d):
        return (y + d + Y) % Y

    def x_by(d):
        return (x + d + X) % X

    def zl_by(d):
        return (zl + d + ZL) % ZL

    sems = Sems(send_sem, recv_sem)
    loads = [
        pltpu.make_async_copy(src, dst, load_sem.at[k])
        for k, (src, dst) in enumerate(
            ((q_any, q_ref), (ku_any, ku_ref), (vu_any, vu_ref), (og_any, og_ref))
        )
    ]
    for made in loads:
        made.start()

    partners = [sibling]
    partners += [at(zh_=zh_by(d)) for d in (1, -1)]
    partners += [at(y_=y_by(d)) for d in range(1, Y)]
    partners += [at(y_=y_by(d), core_=1 - core) for d in range(1, Y)]
    partners += [at(zl_=zl_by(a), x_=x_by(b)) for a in range(ZL) for b in range(X) if a + b]
    barrier = pltpu.get_barrier_semaphore()
    for device in partners:
        pl.semaphore_signal(barrier, inc=1, device_id=device, device_id_type=MESH)
    own = jnp.concatenate(
        [prompt_ref[0].astype(F32), prompt_ref[1].astype(F32), suffix_ref[0].astype(F32)], 0
    ).astype(BF16)
    keys[zh, core, y] = own
    pl.semaphore_wait(barrier, len(partners))

    from_zh = {}
    from_y = {}
    from_core = {}
    for d in (1, 3):
        block = keys.at[zh, core, y]
        from_zh[d] = [sems.copy(block, block, at(zh_=zh_by(d)))]
    half = BLOCK // 2

    def relay(d, rows):
        from_zh[d][0].wait_recv()
        part = keys.at[zh_by(-d), core, y, rows]
        from_zh.setdefault(2, []).append(sems.copy(part, part, at(zh_=zh_by(d))))

    def spread_y(dz):
        if dz == 2:
            for made in from_zh[dz]:
                made.wait_recv()
        block = keys.at[zh_by(-dz), core, y]
        from_y[dz] = [sems.copy(block, block, at(y_=y_by(d))) for d in (2, 1, 3)]
        if dz == 2:
            from_core[dz] = [
                sems.copy(block, block, at(y_=y_by(d), core_=1 - core)) for d in (2, 1, 3, 0)
            ]

    def to_core(dz):
        for made in from_y[dz]:
            made.wait_recv()
        part = keys.at[zh_by(-dz), core]
        from_core[dz] = [sems.copy(part, part, sibling)]

    spread_y(0)

    lane = lax.broadcasted_iota(jnp.int32, (1, ROWS), 1)
    row_fork = (lane * 3277) >> 16
    row_step = (lane - row_fork * (RECOMP * HEADS)) >> 2

    def project(t, carry):
        rows = pl.ds(pl.multiple_of(t * TILE, TILE), TILE)
        steps = pl.ds(t * (TILE // HEADS), TILE // HEADS)
        q = q_ref[steps].reshape(TILE, QUERY)
        og = og_ref[steps].reshape(TILE, VHEAD)
        head = lax.broadcasted_iota(jnp.int32, (TILE, NOPE), 0) & (HEADS - 1)
        q_nope = q[:, :NOPE]
        zero = jnp.zeros_like(q_nope)
        q_exp = jnp.concatenate([jnp.where(head == h, q_nope, zero) for h in range(HEADS)], 1)
        o_exp = jnp.concatenate([jnp.where(head == h, og, zero) for h in range(HEADS)], 1)
        og_exp[rows, :] = o_exp
        q_t = q_nope.T
        head_t = lax.broadcasted_iota(jnp.int32, (NOPE, TILE), 1) & (HEADS - 1)
        qn_exp_t[:, rows] = jnp.concatenate(
            [jnp.where(head_t == h, q_t, zero) for h in range(HEADS)], 0
        )
        whole = jnp.concatenate([dot(q_exp, ku_ref[...]).astype(BF16), q[:, NOPE:]], 1)
        qry[rows, :] = whole
        qry_t[:, rows] = whole.T
        grad = dot_nt(o_exp[:, :VHEAD], vu_ref[pl.ds(0, LATENT), :])
        for h in range(1, HEADS):
            grad += dot_nt(
                o_exp[:, h * VHEAD : (h + 1) * VHEAD], vu_ref[pl.ds(h * LATENT, LATENT), :]
            )
        grad = grad.astype(BF16)
        lgr[rows, :] = grad
        lgr_t[:, rows] = grad.T
        return carry

    for made in loads:
        made.wait()
    lax.fori_loop(0, 2, project, 0)
    relay(1, pl.ds(0, half))
    relay(3, pl.ds(half, half))
    spread_y(1)
    spread_y(3)
    lax.fori_loop(2, TILES, project, 0)

    def gather_rows(f, carry):
        limit, prompt = carry
        mine = row_fork == f
        return jnp.where(mine, length_ref[f], limit), jnp.where(mine, fork_ref[f], prompt)

    none = jnp.zeros((1, ROWS), jnp.int32)
    row_limit, row_prompt = lax.fori_loop(0, FORKS, gather_rows, (none, none))
    row_limit = row_limit - RECOMP + row_step
    first = jnp.broadcast_to(jnp.where(row_prompt == 0, 0.0, HIDDEN), (PKEYS, ROWS))
    second = jnp.broadcast_to(jnp.where(row_prompt == 1, 0.0, HIDDEN), (PKEYS, ROWS))
    position = ctx * SKEYS + lax.broadcasted_iota(jnp.int32, (SKEYS, ROWS), 0)

    def make_bias(b, carry):
        bz, bc, by = b // (CORE * Y), (b // Y) % CORE, b % Y
        fork = bz * (Y * CORE) + by * CORE + bc
        last = jnp.where(row_fork == fork, row_limit, -1)
        seen = jnp.where(position <= last, 0.0, HIDDEN)
        bias[bz, pl.ds(pl.multiple_of((bc * Y + by) * BLOCK, BLOCK), BLOCK), :] = (
            jnp.concatenate([first, second, seen], 0)
        )
        return carry

    to_core(0)
    lax.fori_loop(0, Y * CORE * ZH, make_bias, 0)

    def scores_of(dz):
        for made in from_core[dz]:
            made.wait_recv()
        part = zh_by(-dz)
        tile = keys[part].reshape(KEYS, WIDTH)
        s = dot(tile, qry_t[...]) + bias[part]
        peak = jnp.max(s, 0, keepdims=True)
        p = jnp.exp((s - peak) * SCALE)
        score[part] = p
        grad = dot(tile[:, :LATENT], lgr_t[...])
        pgrad[part] = grad
        total = jnp.sum(p, 0, keepdims=True)
        mean = jnp.sum(p * grad, 0, keepdims=True) / total
        peaks[dz] = peak
        return part, peak, total, mean

    def merged(left, right):
        top = jnp.maximum(left[0], right[0])
        shrink_left = jnp.exp((left[0] - top) * SCALE)
        shrink_right = jnp.exp((right[0] - top) * SCALE)
        total_left, total_right = left[1] * shrink_left, right[1] * shrink_right
        total = total_left + total_right
        mean = (total_left * left[2] + total_right * right[2]) / total
        return (top, total, mean), shrink_left, shrink_right

    def sums_of(part, mean):
        tile_t = keys[part].reshape(KEYS, WIDTH).T
        p = score[part]
        return dot(tile_t, p.astype(BF16)), dot(
            tile_t, (p * (pgrad[part] - mean)).astype(BF16)
        )

    def add_sums(state, new, part):
        both, shrink_left, shrink_right = merged(state, new)
        acc, grad = sums_of(part, new[2])
        old = acc_t[...]
        acc_t[...] = shrink_left * old + shrink_right * acc
        dif_t[...] = shrink_left * (dif_t[...] + (state[2] - both[2]) * old) + shrink_right * (
            grad + (new[2] - both[2]) * acc
        )
        return both

    part, *state = scores_of(0)
    acc_t[...], dif_t[...] = sums_of(part, state[2])
    to_core(1)
    to_core(3)
    spread_y(2)
    part, *new = scores_of(1)
    state = add_sums(state, new, part)
    part, *new = scores_of(3)
    state = add_sums(state, new, part)
    for made in from_y[2]:
        made.wait_recv()
    part, *new = scores_of(2)
    (peak, total, mean), _, _ = merged(state, new)

    delta = mean * total
    for t in range(TILES):
        cols = slice(t * TILE, (t + 1) * TILE)
        stat[t : t + 1, :] = peak[:, cols]
        stat[TILES + t : TILES + t + 1, :] = total[:, cols]
        stat[2 * TILES + t : 2 * TILES + t + 1, :] = delta[:, cols]
    stat[3 * TILES : 3 * TILES + 1, :] = jnp.zeros((1, TILE), F32)
    stat_copies = []
    for a in range(ZL):
        for b in range(X):
            if a + b:
                stat_copies.append(
                    sems.copy(stat, stat_all.at[ctx], at(zl_=zl_by(a), x_=x_by(b)))
                )
    stat_all[ctx] = stat[...]

    add_sums(state, new, part)
    for b in range(X):
        for c in range(ZL):
            rows = slice((b * ZL + c) * COLS, (b * ZL + c + 1) * COLS)
            lat_s[b, c, 0] = acc_t[rows, :].astype(BF16)
            lat_s[b, c, 1] = dif_t[rows, :].astype(BF16)
        rows = slice(LATENT + b * RCOLS, LATENT + (b + 1) * RCOLS)
        rope_s[b, 0] = acc_t[rows, :].astype(BF16)
        rope_s[b, 1] = dif_t[rows, :].astype(BF16)
    lat_x = {}
    for e in (2, 1, 3, 0):
        to = zl_by(e)
        lat_x[e] = [
            sems.copy(lat_s.at[x_by(d), to], lat_r.at[d - 1, to], at(x_=x_by(d)))
            for d in (2, 1, 3)
        ]
    rope_x = [
        sems.copy(rope_s.at[x_by(d)], rope_r.at[d - 1], at(x_=x_by(d))) for d in (2, 1, 3)
    ]

    for made in stat_copies:
        made.wait_recv()
    all_peak = stat_all[:, 0:TILES, :]
    top = jnp.max(all_peak, 0)
    shrink = jnp.exp((all_peak - top[None]) * SCALE)
    whole_total = jnp.sum(stat_all[:, TILES : 2 * TILES, :] * shrink, 0)
    whole_delta = jnp.sum(stat_all[:, 2 * TILES : 3 * TILES, :] * shrink, 0)
    inverse = 1.0 / whole_total

    def as_row(v):
        return jnp.concatenate([v[t : t + 1, :] for t in range(TILES)], 1)

    def weigh(d):
        if d == 0:
            one = stat
        else:
            one = stat_all.at[zl * X + x_by(-d)]
        factor = jnp.exp((one[0:TILES, :] - top) * SCALE) * inverse
        shift = whole_delta * inverse - one[2 * TILES : 3 * TILES, :] / one[TILES : 2 * TILES, :]
        return as_row(factor), as_row(shift)

    weights = [weigh(d) for d in range(X)]
    top, inverse, row_delta = as_row(top), as_row(inverse), as_row(whole_delta * inverse)

    def weighted(own, came):
        out, grad = None, None
        for d, (factor, shift) in enumerate(weights):
            acc, dif = own if d == 0 else came(d - 1)
            part, part_grad = factor * acc, factor * (dif - shift * acc)
            out = part if d == 0 else out + part
            grad = part_grad if d == 0 else grad + part_grad
        return out, grad * SCALE

    lat_zl = []

    def sum_x(e):
        for made in lat_x[e]:
            made.wait_recv()
        to = zl_by(e)
        rows = pl.ds(pl.multiple_of((x * ZL + to) * COLS, COLS), COLS)

        def came(i):
            return lat_r[i, to, 0].astype(F32), lat_r[i, to, 1].astype(F32)

        out, grad = weighted((acc_t[rows, :], dif_t[rows, :]), came)
        lat_m[to, 0] = out.astype(BF16)
        lat_m[to, 1] = grad.astype(BF16)
        if e:
            lat_zl.append(sems.copy(lat_m.at[to], lat_z.at[e - 1], at(zl_=to)))

    def sum_rope_x():
        for made in rope_x:
            made.wait_recv()
        rows = pl.ds(pl.multiple_of(LATENT + x * RCOLS, RCOLS), RCOLS)

        def came(i):
            return rope_r[i, 0].astype(F32), rope_r[i, 1].astype(F32)

        _, grad = weighted((acc_t[rows, :], dif_t[rows, :]), came)
        rope_z[zl] = grad.astype(BF16)
        block = rope_z.at[zl]
        return [sems.copy(block, block, at(zl_=zl_by(e))) for e in (2, 1, 3)]

    def block_of(to_x, to_zl):
        return pl.ds(pl.multiple_of((to_x * ZL + to_zl) * COLS, COLS), COLS)

    def spread_x(e):
        rows = block_of(x, zl_by(-e))
        for whole in (abs_a, value_a):
            block = whole.at[rows, :]
            for d in (2, 1, 3):
                at_x[d].append(sems.copy(block, block, at(x_=x_by(d))))

    at_x = {1: [], 2: [], 3: []}

    def sum_zl():
        for made in lat_zl:
            made.wait_recv()
        out = lat_m[zl, 0].astype(F32)
        grad = lat_m[zl, 1].astype(F32)
        for i in range(ZL - 1):
            out += lat_z[i, 0].astype(F32)
            grad += lat_z[i, 1].astype(F32)
        rows = block_of(x, zl)
        abs_a[rows, :] = grad.astype(BF16)
        value_a[rows, :] = dot(out.astype(BF16), og_exp[...]).astype(BF16)
        back = {}
        for e in (2, 1, 3):
            back[e] = [
                sems.copy(whole.at[rows, :], whole.at[rows, :], at(zl_=zl_by(e)))
                for whole in (abs_a, value_a)
            ]
        spread_x(0)
        return back

    def sum_rope_zl(made):
        for m in made:
            m.wait_recv()
        grad = rope_z[0].astype(F32)
        for i in range(1, ZL):
            grad += rope_z[i].astype(F32)
        rope_a[x] = grad.astype(BF16)
        block = rope_a.at[x]
        for d in (2, 1, 3):
            at_x[d].append(sems.copy(block, block, at(x_=x_by(d))))

    def gather_x(back):
        for e in (1, 3, 2):
            for made in back[e]:
                made.wait_recv()
            spread_x(e)

    def finish(d):
        if d:
            for made in at_x[d]:
                made.wait_recv()
        b = x_by(-d)
        cols = pl.ds(pl.multiple_of(b * TILE, TILE), TILE)
        lat = abs_a[cols, :]
        key_up_out[b] = dot_nt(qn_exp_t[...], lat)
        return dot(ku_ref[:, cols], lat)

    core_sums, y_sums, zh_sums = {}, {}, {}

    def key_grads(dz):
        part = zh_by(-dz)
        p = score[part] * (jnp.exp((peaks[dz] - top) * SCALE) * inverse)
        sg = (p * (pgrad[part] - row_delta) * SCALE).astype(BF16)
        grad = dot(sg, qry[...])
        value = dot(p.astype(BF16), lgr[...])
        kgrad[part, :, :, :LATENT] = (grad[:, :LATENT] + value).reshape(CORE, Y * BLOCK, LATENT)
        kgrad[part, :, :, LATENT:] = grad[:, LATENT:].reshape(CORE, Y * BLOCK, ROPE)
        c1s[part] = kgrad[part, 1 - core].astype(BF16)
        core_sums[dz] = sems.copy(c1s.at[part], c1r.at[part], sibling)

    def add_cores(dz):
        part = zh_by(-dz)
        core_sums[dz].wait_recv()
        both = kgrad[part, core] + c1r[part].astype(F32)
        kgrad[part, core] = both
        c2s[dz] = both.reshape(Y, BLOCK, WIDTH).astype(BF16)
        y_sums[dz] = [
            sems.copy(c2s.at[dz, y_by(d)], c2r.at[dz, d - 1], at(y_=y_by(d))) for d in (2, 1, 3)
        ]

    def add_ys(dz):
        for made in y_sums[dz]:
            made.wait_recv()
        rows = pl.ds(pl.multiple_of(y * BLOCK, BLOCK), BLOCK)
        mine = kgrad[zh_by(-dz), core, rows, :]
        for i in range(Y - 1):
            mine += c2r[dz, i].astype(F32)
        return mine

    def send_far(mine):
        c3s[2] = mine.astype(BF16)
        return [
            sems.copy(c3s.at[2, pl.ds(0, half)], c3h.at[0], at(zh_=zh_by(1))),
            sems.copy(c3s.at[2, pl.ds(half, half)], c3h.at[1], at(zh_=zh_by(-1))),
        ]

    def send_near(halves, up, down):
        for made in halves:
            made.wait_recv()
        c3s[0, :half] = (up[:half] + c3h[0].astype(F32)).astype(BF16)
        c3s[0, half:] = up[half:].astype(BF16)
        c3s[1, :half] = down[:half].astype(BF16)
        c3s[1, half:] = (down[half:] + c3h[1].astype(F32)).astype(BF16)
        return [
            sems.copy(c3s.at[0], c3r.at[0], at(zh_=zh_by(1))),
            sems.copy(c3s.at[1], c3r.at[1], at(zh_=zh_by(-1))),
        ]

    sum_x(2)
    key_grads(2)
    sum_x(1)
    key_grads(1)
    add_cores(2)
    key_grads(3)
    add_cores(1)
    sum_x(3)
    key_grads(0)
    add_cores(3)
    sum_x(0)
    rope_zl = sum_rope_x()
    add_cores(0)
    halves = send_far(add_ys(2))
    back = sum_zl()
    sum_rope_zl(rope_zl)
    up, down, final = add_ys(3), add_ys(1), add_ys(0)
    gather_x(back)
    near = send_near(halves, up, down)

    spread = finish(0)
    for d in (1, 3, 2):
        spread += finish(d)
    for b in range(X):
        query_out[NOPE + b * RCOLS : NOPE + (b + 1) * RCOLS, :] = rope_a[b].astype(F32)
    head_of = lane & (HEADS - 1)
    nope = spread[:NOPE, :]
    for h in range(1, HEADS):
        nope = jnp.where(head_of == h, spread[h * NOPE : (h + 1) * NOPE, :], nope)
    query_out[:NOPE, :] = nope
    value_out[...] = value_a[...]
    for made in near:
        made.wait_recv()
    keys_out[...] = final + c3r[0].astype(F32) + c3r[1].astype(F32)
    for made in sems.started:
        made.wait_send()


def unpack(
    keys_ref, value_ref, key_up_ref, query_ref,
    prompt_out, suffix_out, query_out, key_up_out, value_up_out,
):
    prompt_out[0] = keys_ref[:PKEYS, :]
    prompt_out[1] = keys_ref[PKEYS : 2 * PKEYS, :]
    suffix_out[0] = keys_ref[2 * PKEYS :, :]
    for h in range(HEADS):
        value_up_out[h * LATENT : (h + 1) * LATENT, :] = value_ref[
            :, h * VHEAD : (h + 1) * VHEAD
        ].astype(F32)
    for b in range(X):
        key_up_out[:, b * TILE : (b + 1) * TILE] = key_up_ref[b]
    steps = TILE // HEADS
    for t in range(TILES):
        part = query_ref[:, t * TILE : (t + 1) * TILE].T
        query_out[t * steps : (t + 1) * steps] = part.reshape(steps, HEADS, QUERY)


def shards(prompt, suffix, queries, key_up, value_up, out_grad, fork_prompt, suffix_length):
    vmem = pl.BlockSpec(memory_space=pltpu.VMEM)
    smem = pl.BlockSpec(memory_space=pltpu.SMEM)
    copies = 152
    hbm = pl.BlockSpec(memory_space=pltpu.HBM)

    def in_hbm(v):
        return pltpu.with_memory_space_constraint(v, pltpu.HBM)

    steps = FORKS * RECOMP
    sums = pl.pallas_call(
        kernel,
        out_shape=(
            jax.ShapeDtypeStruct((BLOCK, WIDTH), F32),
            jax.ShapeDtypeStruct((LATENT, HEADS * VHEAD), BF16),
            jax.ShapeDtypeStruct((X, HEADS * NOPE, TILE), F32),
            jax.ShapeDtypeStruct((QUERY, ROWS), F32),
        ),
        in_specs=[vmem] * 2 + [hbm] * 4 + [smem] * 2,
        out_specs=(vmem,) * 4,
        scratch_shapes=[
            pltpu.VMEM((ZH, CORE, Y, BLOCK, WIDTH), BF16),
            pltpu.VMEM((ROWS, WIDTH), BF16),
            pltpu.VMEM((WIDTH, ROWS), BF16),
            pltpu.VMEM((ROWS, LATENT), BF16),
            pltpu.VMEM((LATENT, ROWS), BF16),
            pltpu.VMEM((ROWS, HEADS * VHEAD), BF16),
            pltpu.VMEM((HEADS * NOPE, ROWS), BF16),
            pltpu.VMEM((ZH, KEYS, ROWS), F32),
            pltpu.VMEM((ZH, KEYS, ROWS), F32),
            pltpu.VMEM((ZH, KEYS, ROWS), F32),
            pltpu.VMEM((ZH, 1, ROWS), F32),
            pltpu.VMEM((WIDTH, ROWS), F32),
            pltpu.VMEM((WIDTH, ROWS), F32),
            pltpu.VMEM((ZH, CORE, Y * BLOCK, WIDTH), F32),
            pltpu.VMEM((16, TILE), F32),
            pltpu.VMEM((ZL * X, 16, TILE), F32),
            pltpu.VMEM((ZH, Y * BLOCK, WIDTH), BF16),
            pltpu.VMEM((ZH, Y * BLOCK, WIDTH), BF16),
            pltpu.VMEM((ZH, Y, BLOCK, WIDTH), BF16),
            pltpu.VMEM((ZH, Y - 1, BLOCK, WIDTH), BF16),
            pltpu.VMEM((ZH - 1, BLOCK, WIDTH), BF16),
            pltpu.VMEM((2, BLOCK // 2, WIDTH), BF16),
            pltpu.VMEM((2, BLOCK, WIDTH), BF16),
            pltpu.VMEM((X, ZL, 2, COLS, ROWS), BF16),
            pltpu.VMEM((X - 1, ZL, 2, COLS, ROWS), BF16),
            pltpu.VMEM((ZL, 2, COLS, ROWS), BF16),
            pltpu.VMEM((ZL - 1, 2, COLS, ROWS), BF16),
            pltpu.VMEM((X, 2, RCOLS, ROWS), BF16),
            pltpu.VMEM((X - 1, 2, RCOLS, ROWS), BF16),
            pltpu.VMEM((ZL, RCOLS, ROWS), BF16),
            pltpu.VMEM((LATENT, ROWS), BF16),
            pltpu.VMEM((LATENT, HEADS * VHEAD), BF16),
            pltpu.VMEM((X, RCOLS, ROWS), BF16),
            pltpu.VMEM((steps, HEADS, QUERY), BF16),
            pltpu.VMEM((HEADS * NOPE, LATENT), BF16),
            pltpu.VMEM((HEADS * LATENT, VHEAD), BF16),
            pltpu.VMEM((steps, HEADS, VHEAD), BF16),
            pltpu.SemaphoreType.DMA((copies,)),
            pltpu.SemaphoreType.DMA((copies,)),
            pltpu.SemaphoreType.DMA((4,)),
        ],
        compiler_params=pltpu.CompilerParams(
            collective_id=0, has_side_effects=True, vmem_limit_bytes=42 << 20
        ),
        cost_estimate=pl.CostEstimate(
            flops=8_000_000_000, bytes_accessed=6_000_000, transcendentals=700_000
        ),
        name="latent_backward",
    )(
        in_hbm(prompt),
        in_hbm(suffix),
        in_hbm(queries.reshape(steps, HEADS, QUERY)),
        in_hbm(key_up.reshape(HEADS * NOPE, LATENT)),
        in_hbm(value_up.reshape(HEADS * LATENT, VHEAD)),
        in_hbm(out_grad.reshape(steps, HEADS, VHEAD)),
        in_hbm(fork_prompt),
        in_hbm(suffix_length),
    )
    prompt_grad, suffix_grad, query_grad, key_up_grad, value_up_grad = pl.pallas_call(
        unpack,
        out_shape=(
            jax.ShapeDtypeStruct((2, PKEYS, WIDTH), F32),
            jax.ShapeDtypeStruct((1, SKEYS, WIDTH), F32),
            jax.ShapeDtypeStruct((steps, HEADS, QUERY), F32),
            jax.ShapeDtypeStruct((HEADS * NOPE, LATENT), F32),
            jax.ShapeDtypeStruct((HEADS * LATENT, VHEAD), F32),
        ),
        in_specs=[vmem] * 4,
        out_specs=(vmem,) * 5,
        compiler_params=pltpu.CompilerParams(vmem_limit_bytes=16 << 20),
        name="unpack_grads",
    )(*sums)
    return (
        prompt_grad,
        suffix_grad,
        query_grad.reshape(FORKS, RECOMP, HEADS, QUERY),
        key_up_grad.reshape(HEADS, NOPE, LATENT),
        value_up_grad.reshape(HEADS, LATENT, VHEAD),
    )


def solution(mesh):
    return jax.shard_map(
        shards,
        mesh=mesh,
        in_specs=(
            P(None, ("ctx", "sample"), None),
            P("sample", "ctx", None),
            P(None, None, "sample", None),
            P("sample", None, None),
            P("sample", None, None),
            P(None, None, "sample", None),
            P(),
            P(),
        ),
        out_specs=(
            P(None, ("ctx", "sample"), None),
            P("sample", "ctx", None),
            P(None, None, "sample", None),
            P("sample", None, None),
            P("sample", None, None),
        ),
        check_vma=False,
    )
```

```python
import functools

import jax
import jax.numpy as jnp
from jax import lax
from jax.experimental import pallas as pl
from jax.experimental.pallas import tpu as pltpu
from jax.sharding import PartitionSpec as P

MESH = pl.DeviceIdType.MESH
F32 = jnp.float32
BF16 = jnp.bfloat16
HIDDEN = -1e30

ZL, X, ZH, Y, CORE = 4, 4, 4, 4, 2
FORKS, RECOMP, HEADS = 32, 5, 4
NOPE, ROPE, LATENT, VHEAD = 128, 64, 512, 128
WIDTH = LATENT + ROPE
QUERY = NOPE + ROPE
ROWS = FORKS * RECOMP * HEADS
TILE = 128
TILES = ROWS // TILE
PKEYS, SKEYS = 8, 16
BLOCK = 2 * PKEYS + SKEYS
KEYS = CORE * Y * BLOCK
SCALE = QUERY**-0.5
COLS = LATENT // (X * ZL)
RCOLS = ROPE // X


def dot(a, b):
    return jnp.dot(a, b, preferred_element_type=F32)


def dot_nt(a, b):
    return lax.dot_general(a, b, (((1,), (1,)), ((), ())), preferred_element_type=F32)


class Sems:
    def __init__(self, send, recv):
        self.send, self.recv, self.used, self.started = send, recv, 0, []

    def copy(self, src, dst, device):
        k = self.used
        self.used += 1
        made = pltpu.make_async_remote_copy(
            src_ref=src,
            dst_ref=dst,
            send_sem=self.send.at[k],
            recv_sem=self.recv.at[k],
            device_id=device,
            device_id_type=MESH,
        )
        made.start()
        self.started.append(made)
        return made


def kernel(
    prompt_ref, suffix_ref, q_any, ku_any, vu_any, og_any, fork_ref, length_ref,
    keys_out, value_out, key_up_out, query_out,
    keys, qry, qry_t, lgr, lgr_t, og_exp, qn_exp_t, bias, score, pgrad, peaks,
    acc_t, dif_t, kgrad, stat, stat_all, c1s, c1r, c2s, c2r, c3s, c3h, c3r,
    far_s, far_r, near_s, near_r, lat_m, lat_z, rope_s, rope_r, rope_z, whole, rope_a,
    q_ref, ku_ref, vu_ref, og_ref, send_sem, recv_sem, load_sem,
):
    ctx, sample = lax.axis_index("ctx"), lax.axis_index("sample")
    zl, x = ctx // X, ctx % X
    zh, y, core = sample // (Y * CORE), (sample // CORE) % Y, sample % CORE

    def at(zl_=zl, x_=x, zh_=zh, y_=y, core_=core):
        return (zl_ * X + x_, zh_ * (Y * CORE) + y_ * CORE + core_)

    sibling = at(core_=1 - core)

    def zh_by(d):
        return (zh + d + ZH) % ZH

    def y_by(d):
        return (y + d + Y) % Y

    def x_by(d):
        return (x + d + X) % X

    def zl_by(d):
        return (zl + d + ZL) % ZL

    sems = Sems(send_sem, recv_sem)
    loads = [
        pltpu.make_async_copy(src, dst, load_sem.at[k])
        for k, (src, dst) in enumerate(
            ((q_any, q_ref), (ku_any, ku_ref), (vu_any, vu_ref), (og_any, og_ref))
        )
    ]
    for made in loads:
        made.start()

    partners = [sibling]
    partners += [at(zh_=zh_by(d)) for d in (1, -1)]
    partners += [at(y_=y_by(d)) for d in range(1, Y)]
    partners += [at(y_=y_by(d), core_=1 - core) for d in range(1, Y)]
    partners += [at(zl_=zl_by(a), x_=x_by(b)) for a in range(ZL) for b in range(X) if a + b]
    barrier = pltpu.get_barrier_semaphore()
    for device in partners:
        pl.semaphore_signal(barrier, inc=1, device_id=device, device_id_type=MESH)
    own = jnp.concatenate(
        [prompt_ref[0].astype(F32), prompt_ref[1].astype(F32), suffix_ref[0].astype(F32)], 0
    ).astype(BF16)
    keys[zh, core, y] = own
    pl.semaphore_wait(barrier, len(partners))

    from_zh = {}
    from_y = {}
    from_core = {}
    for d in (1, 3):
        block = keys.at[zh, core, y]
        from_zh[d] = [sems.copy(block, block, at(zh_=zh_by(d)))]
    half = BLOCK // 2

    def relay(d, rows):
        from_zh[d][0].wait_recv()
        part = keys.at[zh_by(-d), core, y, rows]
        from_zh.setdefault(2, []).append(sems.copy(part, part, at(zh_=zh_by(d))))

    def spread_y(dz):
        if dz == 2:
            for made in from_zh[dz]:
                made.wait_recv()
        block = keys.at[zh_by(-dz), core, y]
        from_y[dz] = [sems.copy(block, block, at(y_=y_by(d))) for d in (2, 1, 3)]
        if dz == 2:
            from_core[dz] = [
                sems.copy(block, block, at(y_=y_by(d), core_=1 - core)) for d in (2, 1, 3, 0)
            ]

    def to_core(dz):
        for made in from_y[dz]:
            made.wait_recv()
        part = keys.at[zh_by(-dz), core]
        from_core[dz] = [sems.copy(part, part, sibling)]

    spread_y(0)

    lane = lax.broadcasted_iota(jnp.int32, (1, ROWS), 1)
    row_fork = (lane * 3277) >> 16
    row_step = (lane - row_fork * (RECOMP * HEADS)) >> 2

    def project(t, carry):
        rows = pl.ds(pl.multiple_of(t * TILE, TILE), TILE)
        steps = pl.ds(t * (TILE // HEADS), TILE // HEADS)
        q = q_ref[steps].reshape(TILE, QUERY)
        og = og_ref[steps].reshape(TILE, VHEAD)
        head = lax.broadcasted_iota(jnp.int32, (TILE, NOPE), 0) & (HEADS - 1)
        q_nope = q[:, :NOPE]
        zero = jnp.zeros_like(q_nope)
        q_exp = jnp.concatenate([jnp.where(head == h, q_nope, zero) for h in range(HEADS)], 1)
        o_exp = jnp.concatenate([jnp.where(head == h, og, zero) for h in range(HEADS)], 1)
        og_exp[rows, :] = o_exp
        q_t = q_nope.T
        head_t = lax.broadcasted_iota(jnp.int32, (NOPE, TILE), 1) & (HEADS - 1)
        qn_exp_t[:, rows] = jnp.concatenate(
            [jnp.where(head_t == h, q_t, zero) for h in range(HEADS)], 0
        )
        whole = jnp.concatenate([dot(q_exp, ku_ref[...]).astype(BF16), q[:, NOPE:]], 1)
        qry[rows, :] = whole
        qry_t[:, rows] = whole.T
        grad = dot_nt(o_exp[:, :VHEAD], vu_ref[pl.ds(0, LATENT), :])
        for h in range(1, HEADS):
            grad += dot_nt(
                o_exp[:, h * VHEAD : (h + 1) * VHEAD], vu_ref[pl.ds(h * LATENT, LATENT), :]
            )
        grad = grad.astype(BF16)
        lgr[rows, :] = grad
        lgr_t[:, rows] = grad.T
        return carry

    for made in loads:
        made.wait()
    lax.fori_loop(0, 2, project, 0)
    relay(1, pl.ds(0, half))
    relay(3, pl.ds(half, half))
    spread_y(1)
    spread_y(3)
    lax.fori_loop(2, TILES, project, 0)

    def gather_rows(f, carry):
        limit, prompt = carry
        mine = row_fork == f
        return jnp.where(mine, length_ref[f], limit), jnp.where(mine, fork_ref[f], prompt)

    none = jnp.zeros((1, ROWS), jnp.int32)
    row_limit, row_prompt = lax.fori_loop(0, FORKS, gather_rows, (none, none))
    row_limit = row_limit - RECOMP + row_step
    first = jnp.broadcast_to(jnp.where(row_prompt == 0, 0.0, HIDDEN), (PKEYS, ROWS))
    second = jnp.broadcast_to(jnp.where(row_prompt == 1, 0.0, HIDDEN), (PKEYS, ROWS))
    position = ctx * SKEYS + lax.broadcasted_iota(jnp.int32, (SKEYS, ROWS), 0)

    def make_bias(b, carry):
        bz, bc, by = b // (CORE * Y), (b // Y) % CORE, b % Y
        fork = bz * (Y * CORE) + by * CORE + bc
        last = jnp.where(row_fork == fork, row_limit, -1)
        seen = jnp.where(position <= last, 0.0, HIDDEN)
        bias[bz, pl.ds(pl.multiple_of((bc * Y + by) * BLOCK, BLOCK), BLOCK), :] = (
            jnp.concatenate([first, second, seen], 0)
        )
        return carry

    to_core(0)
    lax.fori_loop(0, Y * CORE * ZH, make_bias, 0)

    def scores_of(dz):
        for made in from_core[dz]:
            made.wait_recv()
        part = zh_by(-dz)
        tile = keys[part].reshape(KEYS, WIDTH)
        s = dot(tile, qry_t[...]) + bias[part]
        peak = jnp.max(s, 0, keepdims=True)
        p = jnp.exp((s - peak) * SCALE)
        score[part] = p
        grad = dot(tile[:, :LATENT], lgr_t[...])
        pgrad[part] = grad
        total = jnp.sum(p, 0, keepdims=True)
        mean = jnp.sum(p * grad, 0, keepdims=True) / total
        peaks[dz] = peak
        return part, peak, total, mean

    def merged(left, right):
        top = jnp.maximum(left[0], right[0])
        shrink_left = jnp.exp((left[0] - top) * SCALE)
        shrink_right = jnp.exp((right[0] - top) * SCALE)
        total_left, total_right = left[1] * shrink_left, right[1] * shrink_right
        total = total_left + total_right
        mean = (total_left * left[2] + total_right * right[2]) / total
        return (top, total, mean), shrink_left, shrink_right

    def sums_of(part, mean):
        tile_t = keys[part].reshape(KEYS, WIDTH).T
        p = score[part]
        return dot(tile_t, p.astype(BF16)), dot(
            tile_t, (p * (pgrad[part] - mean)).astype(BF16)
        )

    def add_sums(state, new, part):
        both, shrink_left, shrink_right = merged(state, new)
        acc, grad = sums_of(part, new[2])
        old = acc_t[...]
        acc_t[...] = shrink_left * old + shrink_right * acc
        dif_t[...] = shrink_left * (dif_t[...] + (state[2] - both[2]) * old) + shrink_right * (
            grad + (new[2] - both[2]) * acc
        )
        return both

    part, *state = scores_of(0)
    acc_t[...], dif_t[...] = sums_of(part, state[2])
    to_core(1)
    to_core(3)
    spread_y(2)
    part, *new = scores_of(1)
    state = add_sums(state, new, part)
    part, *new = scores_of(3)
    state = add_sums(state, new, part)
    for made in from_y[2]:
        made.wait_recv()
    part, *new = scores_of(2)
    (peak, total, mean), _, _ = merged(state, new)

    delta = mean * total
    for t in range(TILES):
        cols = slice(t * TILE, (t + 1) * TILE)
        stat[t : t + 1, :] = peak[:, cols]
        stat[TILES + t : TILES + t + 1, :] = total[:, cols]
        stat[2 * TILES + t : 2 * TILES + t + 1, :] = delta[:, cols]
    stat[3 * TILES : 3 * TILES + 1, :] = jnp.zeros((1, TILE), F32)
    stat_copies = []
    for a in range(ZL):
        for b in range(X):
            if a + b:
                stat_copies.append(
                    sems.copy(stat, stat_all.at[ctx], at(zl_=zl_by(a), x_=x_by(b)))
                )
    stat_all[ctx] = stat[...]

    add_sums(state, new, part)
    half_cols = COLS // 2
    ORDER = (2, 1, 3, 0)
    far_x = {}
    for e in ORDER:
        to = zl_by(e)
        for k in range(2):
            start = (x_by(2) * ZL + to) * COLS + k * half_cols
            rows = pl.ds(pl.multiple_of(start, half_cols), half_cols)
            far_s[to, k, 0] = acc_t[rows, :].astype(BF16)
            far_s[to, k, 1] = dif_t[rows, :].astype(BF16)
        far_x[e] = [
            sems.copy(far_s.at[to, k], far_r.at[k, to], at(x_=x_by(1 - 2 * k))) for k in range(2)
        ]
    for b in range(X):
        rows = slice(LATENT + b * RCOLS, LATENT + (b + 1) * RCOLS)
        rope_s[b, 0] = acc_t[rows, :].astype(BF16)
        rope_s[b, 1] = dif_t[rows, :].astype(BF16)
    rope_x = [
        sems.copy(rope_s.at[x_by(d)], rope_r.at[d - 1], at(x_=x_by(d))) for d in (2, 1, 3)
    ]

    for made in stat_copies:
        made.wait_recv()
    all_peak = stat_all[:, 0:TILES, :]
    top = jnp.max(all_peak, 0)
    shrink = jnp.exp((all_peak - top[None]) * SCALE)
    whole_total = jnp.sum(stat_all[:, TILES : 2 * TILES, :] * shrink, 0)
    whole_delta = jnp.sum(stat_all[:, 2 * TILES : 3 * TILES, :] * shrink, 0)
    inverse = 1.0 / whole_total

    def as_row(v):
        return jnp.concatenate([v[t : t + 1, :] for t in range(TILES)], 1)

    def weigh(d):
        if d == 0:
            one = stat
        else:
            one = stat_all.at[zl * X + x_by(-d)]
        factor = jnp.exp((one[0:TILES, :] - top) * SCALE) * inverse
        shift = whole_delta * inverse - one[2 * TILES : 3 * TILES, :] / one[TILES : 2 * TILES, :]
        return as_row(factor), as_row(shift)

    weights = [weigh(d) for d in range(X)]
    top, inverse, row_delta = as_row(top), as_row(inverse), as_row(whole_delta * inverse)

    def weighted(d, acc, dif):
        factor, shift = weights[d]
        return factor * acc, (factor * SCALE) * (dif - shift * acc)

    def block_of(to_x, to_zl):
        return pl.ds(pl.multiple_of((to_x * ZL + to_zl) * COLS, COLS), COLS)

    near_x = {}

    def send_near_x(e):
        to = zl_by(e)
        near_x[e] = []
        for k in range(2):
            far_x[e][k].wait_recv()
            rows = block_of(x_by(1 - 2 * k), to)
            own = weighted(0, acc_t[rows, :], dif_t[rows, :])
            came = weighted(1 + 2 * k, far_r[k, to, 0].astype(F32), far_r[k, to, 1].astype(F32))
            added = slice(k * half_cols, (k + 1) * half_cols)
            other = slice((1 - k) * half_cols, (2 - k) * half_cols)
            for i in range(2):
                near_s[k, to, i, added] = (own[i][added] + came[i]).astype(BF16)
                near_s[k, to, i, other] = own[i][other].astype(BF16)
            near_x[e].append(
                sems.copy(near_s.at[k, to], near_r.at[k, to], at(x_=x_by(1 - 2 * k)))
            )

    lat_zl = []

    def sum_x(e):
        for made in near_x[e]:
            made.wait_recv()
        to = zl_by(e)
        rows = block_of(x, to)
        own = weighted(0, acc_t[rows, :], dif_t[rows, :])
        for i in range(2):
            add = own[i] + near_r[0, to, i].astype(F32) + near_r[1, to, i].astype(F32)
            lat_m[to, i] = add.astype(BF16)
        if e:
            lat_zl.append(sems.copy(lat_m.at[to], lat_z.at[e - 1], at(zl_=to)))

    def sum_rope_x():
        for made in rope_x:
            made.wait_recv()
        rows = pl.ds(pl.multiple_of(LATENT + x * RCOLS, RCOLS), RCOLS)

        grad = weighted(0, acc_t[rows, :], dif_t[rows, :])[1]
        for d in (1, 2, 3):
            grad += weighted(d, rope_r[d - 1, 0].astype(F32), rope_r[d - 1, 1].astype(F32))[1]
        rope_z[zl] = grad.astype(BF16)
        block = rope_z.at[zl]
        return [sems.copy(block, block, at(zl_=zl_by(e))) for e in (2, 1, 3)]

    to_near = {}
    to_far = []

    def spread_x(e):
        block = whole.at[block_of(x, zl_by(-e)), :]
        to_near[e] = [sems.copy(block, block, at(x_=x_by(1 - 2 * k))) for k in range(2)]

    def forward_x(e):
        for k in range(2):
            to_near[e][k].wait_recv()
            start = (x_by(2 * k - 1) * ZL + zl_by(-e)) * COLS + k * half_cols
            block = whole.at[pl.ds(pl.multiple_of(start, half_cols), half_cols), :]
            to_far.append(sems.copy(block, block, at(x_=x_by(1 - 2 * k))))

    rope_far = []

    def sum_zl():
        for made in lat_zl:
            made.wait_recv()
        out = lat_m[zl, 0].astype(F32)
        grad = lat_m[zl, 1].astype(F32)
        for i in range(ZL - 1):
            out += lat_z[i, 0].astype(F32)
            grad += lat_z[i, 1].astype(F32)
        rows = block_of(x, zl)
        whole[rows, :ROWS] = grad.astype(BF16)
        whole[rows, ROWS:] = dot(out.astype(BF16), og_exp[...]).astype(BF16)
        block = whole.at[rows, :]
        back = {e: sems.copy(block, block, at(zl_=zl_by(e))) for e in (2, 1, 3)}
        spread_x(0)
        return back

    def sum_rope_zl(made):
        for m in made:
            m.wait_recv()
        grad = rope_z[0].astype(F32)
        for i in range(1, ZL):
            grad += rope_z[i].astype(F32)
        rope_a[x] = grad.astype(BF16)
        block = rope_a.at[x]
        for d in (2, 1, 3):
            rope_far.append(sems.copy(block, block, at(x_=x_by(d))))

    def gather_x(back):
        done = 0
        for e in (1, 3, 2):
            back[e].wait_recv()
            spread_x(e)
            forward_x(done)
            done = e
        forward_x(done)

    def finish(d):
        b = x_by(-d)
        cols = pl.ds(pl.multiple_of(b * TILE, TILE), TILE)
        lat = whole[cols, :ROWS]
        key_up_out[b] = dot_nt(qn_exp_t[...], lat)
        return dot(ku_ref[:, cols], lat)

    core_sums, y_sums, zh_sums = {}, {}, {}

    def key_grads(dz):
        part = zh_by(-dz)
        p = score[part] * (jnp.exp((peaks[dz] - top) * SCALE) * inverse)
        sg = (p * (pgrad[part] - row_delta) * SCALE).astype(BF16)
        grad = dot(sg, qry[...])
        value = dot(p.astype(BF16), lgr[...])
        kgrad[part, :, :, :LATENT] = (grad[:, :LATENT] + value).reshape(CORE, Y * BLOCK, LATENT)
        kgrad[part, :, :, LATENT:] = grad[:, LATENT:].reshape(CORE, Y * BLOCK, ROPE)
        c1s[part] = kgrad[part, 1 - core].astype(BF16)
        core_sums[dz] = sems.copy(c1s.at[part], c1r.at[part], sibling)

    def add_cores(dz):
        part = zh_by(-dz)
        core_sums[dz].wait_recv()
        both = kgrad[part, core] + c1r[part].astype(F32)
        kgrad[part, core] = both
        c2s[dz] = both.reshape(Y, BLOCK, WIDTH).astype(BF16)
        y_sums[dz] = [
            sems.copy(c2s.at[dz, y_by(d)], c2r.at[dz, d - 1], at(y_=y_by(d))) for d in (2, 1, 3)
        ]

    def add_ys(dz):
        for made in y_sums[dz]:
            made.wait_recv()
        rows = pl.ds(pl.multiple_of(y * BLOCK, BLOCK), BLOCK)
        mine = kgrad[zh_by(-dz), core, rows, :]
        for i in range(Y - 1):
            mine += c2r[dz, i].astype(F32)
        return mine

    def send_far(mine):
        c3s[2] = mine.astype(BF16)
        return [
            sems.copy(c3s.at[2, pl.ds(0, half)], c3h.at[0], at(zh_=zh_by(1))),
            sems.copy(c3s.at[2, pl.ds(half, half)], c3h.at[1], at(zh_=zh_by(-1))),
        ]

    def send_near(halves, up, down):
        for made in halves:
            made.wait_recv()
        c3s[0, :half] = (up[:half] + c3h[0].astype(F32)).astype(BF16)
        c3s[0, half:] = up[half:].astype(BF16)
        c3s[1, :half] = down[:half].astype(BF16)
        c3s[1, half:] = (down[half:] + c3h[1].astype(F32)).astype(BF16)
        return [
            sems.copy(c3s.at[0], c3r.at[0], at(zh_=zh_by(1))),
            sems.copy(c3s.at[1], c3r.at[1], at(zh_=zh_by(-1))),
        ]

    for e in ORDER:
        send_near_x(e)
    key_grads(2)
    key_grads(1)
    add_cores(2)
    sum_x(2)
    key_grads(3)
    add_cores(1)
    sum_x(1)
    key_grads(0)
    add_cores(3)
    sum_x(3)
    rope_zl = sum_rope_x()
    sum_x(0)
    add_cores(0)
    halves = send_far(add_ys(2))
    back = sum_zl()
    sum_rope_zl(rope_zl)
    up, down, final = add_ys(3), add_ys(1), add_ys(0)
    gather_x(back)
    near = send_near(halves, up, down)

    spread = finish(0) + finish(1) + finish(3)
    for made in to_far:
        made.wait_recv()
    spread += finish(2)
    for made in rope_far:
        made.wait_recv()
    for b in range(X):
        query_out[NOPE + b * RCOLS : NOPE + (b + 1) * RCOLS, :] = rope_a[b].astype(F32)
    head_of = lane & (HEADS - 1)
    nope = spread[:NOPE, :]
    for h in range(1, HEADS):
        nope = jnp.where(head_of == h, spread[h * NOPE : (h + 1) * NOPE, :], nope)
    query_out[:NOPE, :] = nope
    value_out[...] = whole[:, ROWS:]
    for made in near:
        made.wait_recv()
    keys_out[...] = final + c3r[0].astype(F32) + c3r[1].astype(F32)
    for made in sems.started:
        made.wait_send()


def unpack(
    keys_ref, value_ref, key_up_ref, query_ref,
    prompt_out, suffix_out, query_out, key_up_out, value_up_out,
):
    prompt_out[0] = keys_ref[:PKEYS, :]
    prompt_out[1] = keys_ref[PKEYS : 2 * PKEYS, :]
    suffix_out[0] = keys_ref[2 * PKEYS :, :]
    for h in range(HEADS):
        value_up_out[h * LATENT : (h + 1) * LATENT, :] = value_ref[
            :, h * VHEAD : (h + 1) * VHEAD
        ].astype(F32)
    for b in range(X):
        key_up_out[:, b * TILE : (b + 1) * TILE] = key_up_ref[b]
    steps = TILE // HEADS
    for t in range(TILES):
        part = query_ref[:, t * TILE : (t + 1) * TILE].T
        query_out[t * steps : (t + 1) * steps] = part.reshape(steps, HEADS, QUERY)


def shards(prompt, suffix, queries, key_up, value_up, out_grad, fork_prompt, suffix_length):
    vmem = pl.BlockSpec(memory_space=pltpu.VMEM)
    smem = pl.BlockSpec(memory_space=pltpu.SMEM)
    copies = 152
    hbm = pl.BlockSpec(memory_space=pltpu.HBM)

    def in_hbm(v):
        return pltpu.with_memory_space_constraint(v, pltpu.HBM)

    steps = FORKS * RECOMP
    sums = pl.pallas_call(
        kernel,
        out_shape=(
            jax.ShapeDtypeStruct((BLOCK, WIDTH), F32),
            jax.ShapeDtypeStruct((LATENT, HEADS * VHEAD), BF16),
            jax.ShapeDtypeStruct((X, HEADS * NOPE, TILE), F32),
            jax.ShapeDtypeStruct((QUERY, ROWS), F32),
        ),
        in_specs=[vmem] * 2 + [hbm] * 4 + [smem] * 2,
        out_specs=(vmem,) * 4,
        scratch_shapes=[
            pltpu.VMEM((ZH, CORE, Y, BLOCK, WIDTH), BF16),
            pltpu.VMEM((ROWS, WIDTH), BF16),
            pltpu.VMEM((WIDTH, ROWS), BF16),
            pltpu.VMEM((ROWS, LATENT), BF16),
            pltpu.VMEM((LATENT, ROWS), BF16),
            pltpu.VMEM((ROWS, HEADS * VHEAD), BF16),
            pltpu.VMEM((HEADS * NOPE, ROWS), BF16),
            pltpu.VMEM((ZH, KEYS, ROWS), F32),
            pltpu.VMEM((ZH, KEYS, ROWS), F32),
            pltpu.VMEM((ZH, KEYS, ROWS), F32),
            pltpu.VMEM((ZH, 1, ROWS), F32),
            pltpu.VMEM((WIDTH, ROWS), F32),
            pltpu.VMEM((WIDTH, ROWS), F32),
            pltpu.VMEM((ZH, CORE, Y * BLOCK, WIDTH), F32),
            pltpu.VMEM((16, TILE), F32),
            pltpu.VMEM((ZL * X, 16, TILE), F32),
            pltpu.VMEM((ZH, Y * BLOCK, WIDTH), BF16),
            pltpu.VMEM((ZH, Y * BLOCK, WIDTH), BF16),
            pltpu.VMEM((ZH, Y, BLOCK, WIDTH), BF16),
            pltpu.VMEM((ZH, Y - 1, BLOCK, WIDTH), BF16),
            pltpu.VMEM((ZH - 1, BLOCK, WIDTH), BF16),
            pltpu.VMEM((2, BLOCK // 2, WIDTH), BF16),
            pltpu.VMEM((2, BLOCK, WIDTH), BF16),
            pltpu.VMEM((ZL, 2, 2, COLS // 2, ROWS), BF16),
            pltpu.VMEM((2, ZL, 2, COLS // 2, ROWS), BF16),
            pltpu.VMEM((2, ZL, 2, COLS, ROWS), BF16),
            pltpu.VMEM((2, ZL, 2, COLS, ROWS), BF16),
            pltpu.VMEM((ZL, 2, COLS, ROWS), BF16),
            pltpu.VMEM((ZL - 1, 2, COLS, ROWS), BF16),
            pltpu.VMEM((X, 2, RCOLS, ROWS), BF16),
            pltpu.VMEM((X - 1, 2, RCOLS, ROWS), BF16),
            pltpu.VMEM((ZL, RCOLS, ROWS), BF16),
            pltpu.VMEM((LATENT, ROWS + HEADS * VHEAD), BF16),
            pltpu.VMEM((X, RCOLS, ROWS), BF16),
            pltpu.VMEM((steps, HEADS, QUERY), BF16),
            pltpu.VMEM((HEADS * NOPE, LATENT), BF16),
            pltpu.VMEM((HEADS * LATENT, VHEAD), BF16),
            pltpu.VMEM((steps, HEADS, VHEAD), BF16),
            pltpu.SemaphoreType.DMA((copies,)),
            pltpu.SemaphoreType.DMA((copies,)),
            pltpu.SemaphoreType.DMA((4,)),
        ],
        compiler_params=pltpu.CompilerParams(
            collective_id=0, has_side_effects=True, vmem_limit_bytes=42 << 20
        ),
        cost_estimate=pl.CostEstimate(
            flops=8_000_000_000, bytes_accessed=6_000_000, transcendentals=700_000
        ),
        name="latent_backward",
    )(
        in_hbm(prompt),
        in_hbm(suffix),
        in_hbm(queries.reshape(steps, HEADS, QUERY)),
        in_hbm(key_up.reshape(HEADS * NOPE, LATENT)),
        in_hbm(value_up.reshape(HEADS * LATENT, VHEAD)),
        in_hbm(out_grad.reshape(steps, HEADS, VHEAD)),
        in_hbm(fork_prompt),
        in_hbm(suffix_length),
    )
    prompt_grad, suffix_grad, query_grad, key_up_grad, value_up_grad = pl.pallas_call(
        unpack,
        out_shape=(
            jax.ShapeDtypeStruct((2, PKEYS, WIDTH), F32),
            jax.ShapeDtypeStruct((1, SKEYS, WIDTH), F32),
            jax.ShapeDtypeStruct((steps, HEADS, QUERY), F32),
            jax.ShapeDtypeStruct((HEADS * NOPE, LATENT), F32),
            jax.ShapeDtypeStruct((HEADS * LATENT, VHEAD), F32),
        ),
        in_specs=[vmem] * 4,
        out_specs=(vmem,) * 5,
        compiler_params=pltpu.CompilerParams(vmem_limit_bytes=16 << 20),
        name="unpack_grads",
    )(*sums)
    return (
        prompt_grad,
        suffix_grad,
        query_grad.reshape(FORKS, RECOMP, HEADS, QUERY),
        key_up_grad.reshape(HEADS, NOPE, LATENT),
        value_up_grad.reshape(HEADS, LATENT, VHEAD),
    )


def solution(mesh):
    return jax.shard_map(
        shards,
        mesh=mesh,
        in_specs=(
            P(None, ("ctx", "sample"), None),
            P("sample", "ctx", None),
            P(None, None, "sample", None),
            P("sample", None, None),
            P("sample", None, None),
            P(None, None, "sample", None),
            P(),
            P(),
        ),
        out_specs=(
            P(None, ("ctx", "sample"), None),
            P("sample", "ctx", None),
            P(None, None, "sample", None),
            P("sample", None, None),
            P("sample", None, None),
        ),
        check_vma=False,
    )
```

```python
import functools

import jax
import jax.numpy as jnp
from jax import lax
from jax.experimental import pallas as pl
from jax.experimental.pallas import tpu as pltpu
from jax.sharding import PartitionSpec as P

MESH = pl.DeviceIdType.MESH
F32 = jnp.float32
BF16 = jnp.bfloat16
HIDDEN = -1e30

ZL, X, ZH, Y, CORE = 4, 4, 4, 4, 2
FORKS, RECOMP, HEADS = 32, 5, 4
NOPE, ROPE, LATENT, VHEAD = 128, 64, 512, 128
WIDTH = LATENT + ROPE
QUERY = NOPE + ROPE
ROWS = FORKS * RECOMP * HEADS
TILE = 128
TILES = ROWS // TILE
PKEYS, SKEYS = 8, 16
BLOCK = 2 * PKEYS + SKEYS
KEYS = CORE * Y * BLOCK
SCALE = QUERY**-0.5
COLS = LATENT // (X * ZL)
GROUP = COLS // 2
RCOLS = ROPE // X


def dot(a, b):
    return jnp.dot(a, b, preferred_element_type=F32)


def dot_nt(a, b):
    return lax.dot_general(a, b, (((1,), (1,)), ((), ())), preferred_element_type=F32)


class Sems:
    def __init__(self, send, recv):
        self.send, self.recv, self.used, self.started = send, recv, 0, []

    def copy(self, src, dst, device):
        k = self.used
        self.used += 1
        made = pltpu.make_async_remote_copy(
            src_ref=src,
            dst_ref=dst,
            send_sem=self.send.at[k],
            recv_sem=self.recv.at[k],
            device_id=device,
            device_id_type=MESH,
        )
        made.start()
        self.started.append(made)
        return made


def kernel(
    prompt_ref, suffix_ref, q_any, ku_any, vu_any, og_any, fork_ref, length_ref,
    keys_out, value_out, key_up_out, query_out,
    keys, qry, qry_t, lgr, lgr_t, og_exp, qn_exp_t, bias, score, pgrad, peaks,
    acc_t, dif_t, kgrad, stat, stat_all, c1s, c1r, c2s, c2r, c3s, c3h, c3r,
    far_s, far_r, near_s, near_r, lat_m, lat_z, rope_s, rope_r, rope_z, whole, rope_a,
    q_ref, ku_ref, vu_ref, og_ref, send_sem, recv_sem, load_sem,
):
    ctx, sample = lax.axis_index("ctx"), lax.axis_index("sample")
    zl, x = ctx // X, ctx % X
    zh, y, core = sample // (Y * CORE), (sample // CORE) % Y, sample % CORE

    def at(zl_=zl, x_=x, zh_=zh, y_=y, core_=core):
        return (zl_ * X + x_, zh_ * (Y * CORE) + y_ * CORE + core_)

    sibling = at(core_=1 - core)

    def zh_by(d):
        return (zh + d + ZH) % ZH

    def y_by(d):
        return (y + d + Y) % Y

    def x_by(d):
        return (x + d + X) % X

    def zl_by(d):
        return (zl + d + ZL) % ZL

    sems = Sems(send_sem, recv_sem)
    loads = [
        pltpu.make_async_copy(src, dst, load_sem.at[k])
        for k, (src, dst) in enumerate(
            ((q_any, q_ref), (ku_any, ku_ref), (vu_any, vu_ref), (og_any, og_ref))
        )
    ]
    for made in loads:
        made.start()

    partners = [sibling]
    partners += [at(zh_=zh_by(d)) for d in (1, -1)]
    partners += [at(y_=y_by(d)) for d in range(1, Y)]
    partners += [at(y_=y_by(d), core_=1 - core) for d in range(1, Y)]
    partners += [at(zl_=zl_by(a), x_=x_by(b)) for a in range(ZL) for b in range(X) if a + b]
    barrier = pltpu.get_barrier_semaphore()
    for device in partners:
        pl.semaphore_signal(barrier, inc=1, device_id=device, device_id_type=MESH)
    own = jnp.concatenate(
        [prompt_ref[0].astype(F32), prompt_ref[1].astype(F32), suffix_ref[0].astype(F32)], 0
    ).astype(BF16)
    keys[zh, core, y] = own
    pl.semaphore_wait(barrier, len(partners))

    from_zh = {}
    from_y = {}
    from_core = {}
    for d in (1, 3):
        block = keys.at[zh, core, y]
        from_zh[d] = [sems.copy(block, block, at(zh_=zh_by(d)))]
    half = BLOCK // 2

    def relay(d, rows):
        from_zh[d][0].wait_recv()
        part = keys.at[zh_by(-d), core, y, rows]
        from_zh.setdefault(2, []).append(sems.copy(part, part, at(zh_=zh_by(d))))

    def spread_y(dz):
        if dz == 2:
            for made in from_zh[dz]:
                made.wait_recv()
        block = keys.at[zh_by(-dz), core, y]
        from_y[dz] = [sems.copy(block, block, at(y_=y_by(d))) for d in (2, 1, 3)]
        if dz == 2:
            from_core[dz] = [
                sems.copy(block, block, at(y_=y_by(d), core_=1 - core)) for d in (2, 1, 3, 0)
            ]

    def to_core(dz):
        for made in from_y[dz]:
            made.wait_recv()
        part = keys.at[zh_by(-dz), core]
        from_core[dz] = [sems.copy(part, part, sibling)]

    spread_y(0)

    lane = lax.broadcasted_iota(jnp.int32, (1, ROWS), 1)
    row_fork = (lane * 3277) >> 16
    row_step = (lane - row_fork * (RECOMP * HEADS)) >> 2

    def project(t, carry):
        rows = pl.ds(pl.multiple_of(t * TILE, TILE), TILE)
        steps = pl.ds(t * (TILE // HEADS), TILE // HEADS)
        q = q_ref[steps].reshape(TILE, QUERY)
        og = og_ref[steps].reshape(TILE, VHEAD)
        head = lax.broadcasted_iota(jnp.int32, (TILE, NOPE), 0) & (HEADS - 1)
        q_nope = q[:, :NOPE]
        zero = jnp.zeros_like(q_nope)
        q_exp = jnp.concatenate([jnp.where(head == h, q_nope, zero) for h in range(HEADS)], 1)
        o_exp = jnp.concatenate([jnp.where(head == h, og, zero) for h in range(HEADS)], 1)
        og_exp[rows, :] = o_exp
        q_t = q_nope.T
        head_t = lax.broadcasted_iota(jnp.int32, (NOPE, TILE), 1) & (HEADS - 1)
        qn_exp_t[:, rows] = jnp.concatenate(
            [jnp.where(head_t == h, q_t, zero) for h in range(HEADS)], 0
        )
        whole = jnp.concatenate([dot(q_exp, ku_ref[...]).astype(BF16), q[:, NOPE:]], 1)
        qry[rows, :] = whole
        qry_t[:, rows] = whole.T
        grad = dot_nt(o_exp[:, :VHEAD], vu_ref[pl.ds(0, LATENT), :])
        for h in range(1, HEADS):
            grad += dot_nt(
                o_exp[:, h * VHEAD : (h + 1) * VHEAD], vu_ref[pl.ds(h * LATENT, LATENT), :]
            )
        grad = grad.astype(BF16)
        lgr[rows, :] = grad
        lgr_t[:, rows] = grad.T
        return carry

    for made in loads:
        made.wait()
    lax.fori_loop(0, 2, project, 0)
    relay(1, pl.ds(0, half))
    relay(3, pl.ds(half, half))
    spread_y(1)
    spread_y(3)
    lax.fori_loop(2, TILES, project, 0)

    def gather_rows(f, carry):
        limit, prompt = carry
        mine = row_fork == f
        return jnp.where(mine, length_ref[f], limit), jnp.where(mine, fork_ref[f], prompt)

    none = jnp.zeros((1, ROWS), jnp.int32)
    row_limit, row_prompt = lax.fori_loop(0, FORKS, gather_rows, (none, none))
    row_limit = row_limit - RECOMP + row_step
    first = jnp.broadcast_to(jnp.where(row_prompt == 0, 0.0, HIDDEN), (PKEYS, ROWS))
    second = jnp.broadcast_to(jnp.where(row_prompt == 1, 0.0, HIDDEN), (PKEYS, ROWS))
    position = ctx * SKEYS + lax.broadcasted_iota(jnp.int32, (SKEYS, ROWS), 0)

    def make_bias(b, carry):
        bz, bc, by = b // (CORE * Y), (b // Y) % CORE, b % Y
        fork = bz * (Y * CORE) + by * CORE + bc
        last = jnp.where(row_fork == fork, row_limit, -1)
        seen = jnp.where(position <= last, 0.0, HIDDEN)
        bias[bz, pl.ds(pl.multiple_of((bc * Y + by) * BLOCK, BLOCK), BLOCK), :] = (
            jnp.concatenate([first, second, seen], 0)
        )
        return carry

    to_core(0)
    lax.fori_loop(0, Y * CORE * ZH, make_bias, 0)

    def scores_of(dz):
        for made in from_core[dz]:
            made.wait_recv()
        part = zh_by(-dz)
        tile = keys[part].reshape(KEYS, WIDTH)
        s = dot(tile, qry_t[...]) + bias[part]
        peak = jnp.max(s, 0, keepdims=True)
        p = jnp.exp((s - peak) * SCALE)
        score[part] = p
        grad = dot(tile[:, :LATENT], lgr_t[...])
        pgrad[part] = grad
        total = jnp.sum(p, 0, keepdims=True)
        mean = jnp.sum(p * grad, 0, keepdims=True) / total
        peaks[dz] = peak
        return part, peak, total, mean

    def merged(left, right):
        top = jnp.maximum(left[0], right[0])
        shrink_left = jnp.exp((left[0] - top) * SCALE)
        shrink_right = jnp.exp((right[0] - top) * SCALE)
        total_left, total_right = left[1] * shrink_left, right[1] * shrink_right
        total = total_left + total_right
        mean = (total_left * left[2] + total_right * right[2]) / total
        return (top, total, mean), shrink_left, shrink_right

    def sums_of(part, mean):
        tile_t = keys[part].reshape(KEYS, WIDTH).T
        p = score[part]
        return dot(tile_t, p.astype(BF16)), dot(
            tile_t, (p * (pgrad[part] - mean)).astype(BF16)
        )

    def add_sums(state, new, part):
        both, shrink_left, shrink_right = merged(state, new)
        acc, grad = sums_of(part, new[2])
        old = acc_t[...]
        acc_t[...] = shrink_left * old + shrink_right * acc
        dif_t[...] = shrink_left * (dif_t[...] + (state[2] - both[2]) * old) + shrink_right * (
            grad + (new[2] - both[2]) * acc
        )
        return both

    part, *state = scores_of(0)
    acc_t[...], dif_t[...] = sums_of(part, state[2])
    to_core(1)
    to_core(3)
    spread_y(2)
    part, *new = scores_of(1)
    state = add_sums(state, new, part)
    part, *new = scores_of(3)
    state = add_sums(state, new, part)
    for made in from_y[2]:
        made.wait_recv()
    part, *new = scores_of(2)
    (peak, total, mean), _, _ = merged(state, new)

    delta = mean * total
    for t in range(TILES):
        cols = slice(t * TILE, (t + 1) * TILE)
        stat[t : t + 1, :] = peak[:, cols]
        stat[TILES + t : TILES + t + 1, :] = total[:, cols]
        stat[2 * TILES + t : 2 * TILES + t + 1, :] = delta[:, cols]
    stat[3 * TILES : 3 * TILES + 1, :] = jnp.zeros((1, TILE), F32)
    stat_copies = []
    for a in range(ZL):
        for b in range(X):
            if a + b:
                stat_copies.append(
                    sems.copy(stat, stat_all.at[ctx], at(zl_=zl_by(a), x_=x_by(b)))
                )
    stat_all[ctx] = stat[...]

    add_sums(state, new, part)
    ORDER = (2, 1, 3, 0)
    FAR_LANES = (slice(0, 3 * TILE), slice(3 * TILE, ROWS))
    OUT_LANES = (slice(0, ROWS), slice(ROWS, ROWS + HEADS * VHEAD))

    def block_of(to_x, to_zl, g):
        return pl.ds(pl.multiple_of((to_x * ZL + to_zl) * COLS + g * GROUP, GROUP), GROUP)

    far_x = {}
    for g in range(2):
        for e in ORDER:
            to = zl_by(e)
            rows = block_of(x_by(2), to, g)
            far_s[to, g, 0] = acc_t[rows, :].astype(BF16)
            far_s[to, g, 1] = dif_t[rows, :].astype(BF16)
            far_x[e, g] = [
                sems.copy(
                    far_s.at[to, g, :, :, FAR_LANES[k]],
                    far_r.at[to, g, :, :, FAR_LANES[k]],
                    at(x_=x_by(1 - 2 * k)),
                )
                for k in range(2)
            ]
    for b in range(X):
        rows = slice(LATENT + b * RCOLS, LATENT + (b + 1) * RCOLS)
        rope_s[b, 0] = acc_t[rows, :].astype(BF16)
        rope_s[b, 1] = dif_t[rows, :].astype(BF16)
    rope_x = [
        sems.copy(rope_s.at[x_by(d)], rope_r.at[d - 1], at(x_=x_by(d))) for d in (2, 1, 3)
    ]

    for made in stat_copies:
        made.wait_recv()
    all_peak = stat_all[:, 0:TILES, :]
    top = jnp.max(all_peak, 0)
    shrink = jnp.exp((all_peak - top[None]) * SCALE)
    whole_total = jnp.sum(stat_all[:, TILES : 2 * TILES, :] * shrink, 0)
    whole_delta = jnp.sum(stat_all[:, 2 * TILES : 3 * TILES, :] * shrink, 0)
    inverse = 1.0 / whole_total

    def as_row(v):
        return jnp.concatenate([v[t : t + 1, :] for t in range(TILES)], 1)

    def weigh(d):
        if d == 0:
            one = stat
        else:
            one = stat_all.at[zl * X + x_by(-d)]
        factor = jnp.exp((one[0:TILES, :] - top) * SCALE) * inverse
        shift = whole_delta * inverse - one[2 * TILES : 3 * TILES, :] / one[TILES : 2 * TILES, :]
        return as_row(factor), as_row(shift)

    weights = [weigh(d) for d in range(X)]
    top, inverse, row_delta = as_row(top), as_row(inverse), as_row(whole_delta * inverse)

    def weighted(d, acc, dif, lanes=slice(0, ROWS)):
        factor, shift = weights[d][0][:, lanes], weights[d][1][:, lanes]
        return factor * acc, (factor * SCALE) * (dif - shift * acc)

    near_x = {}

    def send_near_x(e, g):
        to = zl_by(e)
        near_x[e, g] = []
        for k in range(2):
            far_x[e, g][k].wait_recv()
            rows = block_of(x_by(1 - 2 * k), to, g)
            own = weighted(0, acc_t[rows, :], dif_t[rows, :])
            added, other = FAR_LANES[k], FAR_LANES[1 - k]
            came = weighted(
                1 + 2 * k,
                far_r[to, g, 0, :, added].astype(F32),
                far_r[to, g, 1, :, added].astype(F32),
                added,
            )
            for i in range(2):
                near_s[k, to, g, i, :, added] = (own[i][:, added] + came[i]).astype(BF16)
                near_s[k, to, g, i, :, other] = own[i][:, other].astype(BF16)
            near_x[e, g].append(
                sems.copy(near_s.at[k, to, g], near_r.at[k, to, g], at(x_=x_by(1 - 2 * k)))
            )

    lat_zl = [[], []]

    def sum_x(e, g):
        for made in near_x[e, g]:
            made.wait_recv()
        to = zl_by(e)
        rows = block_of(x, to, g)
        own = weighted(0, acc_t[rows, :], dif_t[rows, :])
        for i in range(2):
            add = own[i] + near_r[0, to, g, i].astype(F32) + near_r[1, to, g, i].astype(F32)
            lat_m[to, g, i] = add.astype(BF16)
        if e:
            lat_zl[g].append(sems.copy(lat_m.at[to, g], lat_z.at[e - 1, g], at(zl_=to)))

    def sum_rope_x():
        for made in rope_x:
            made.wait_recv()
        rows = pl.ds(pl.multiple_of(LATENT + x * RCOLS, RCOLS), RCOLS)

        grad = weighted(0, acc_t[rows, :], dif_t[rows, :])[1]
        for d in (1, 2, 3):
            grad += weighted(d, rope_r[d - 1, 0].astype(F32), rope_r[d - 1, 1].astype(F32))[1]
        rope_z[zl] = grad.astype(BF16)
        block = rope_z.at[zl]
        return [sems.copy(block, block, at(zl_=zl_by(e))) for e in (2, 1, 3)]

    to_near = {}
    to_far = []

    def spread_x(e, g):
        block = whole.at[block_of(x, zl_by(-e), g), :]
        to_near[e, g] = [sems.copy(block, block, at(x_=x_by(1 - 2 * k))) for k in range(2)]

    def forward_x(e, g):
        for k in range(2):
            to_near[e, g][k].wait_recv()
            block = whole.at[block_of(x_by(2 * k - 1), zl_by(-e), g), OUT_LANES[k]]
            to_far.append(sems.copy(block, block, at(x_=x_by(1 - 2 * k))))

    rope_far = []

    def sum_zl(g):
        for made in lat_zl[g]:
            made.wait_recv()
        out = lat_m[zl, g, 0].astype(F32)
        grad = lat_m[zl, g, 1].astype(F32)
        for i in range(ZL - 1):
            out += lat_z[i, g, 0].astype(F32)
            grad += lat_z[i, g, 1].astype(F32)
        rows = block_of(x, zl, g)
        whole[rows, :ROWS] = grad.astype(BF16)
        whole[rows, ROWS:] = dot(out.astype(BF16), og_exp[...]).astype(BF16)
        block = whole.at[rows, :]
        back = {e: sems.copy(block, block, at(zl_=zl_by(e))) for e in (2, 1, 3)}
        spread_x(0, g)
        return back

    def sum_rope_zl(made):
        for m in made:
            m.wait_recv()
        grad = rope_z[0].astype(F32)
        for i in range(1, ZL):
            grad += rope_z[i].astype(F32)
        rope_a[x] = grad.astype(BF16)
        block = rope_a.at[x]
        for d in (2, 1, 3):
            rope_far.append(sems.copy(block, block, at(x_=x_by(d))))

    def gather_x(back, g):
        done = 0
        for e in (1, 3, 2):
            back[e].wait_recv()
            spread_x(e, g)
            forward_x(done, g)
            done = e

    def finish(d):
        b = x_by(-d)
        cols = pl.ds(pl.multiple_of(b * TILE, TILE), TILE)
        lat = whole[cols, :ROWS]
        key_up_out[b] = dot_nt(qn_exp_t[...], lat)
        return dot(ku_ref[:, cols], lat)

    core_sums, y_sums, zh_sums = {}, {}, {}

    def key_grads(dz):
        part = zh_by(-dz)
        p = score[part] * (jnp.exp((peaks[dz] - top) * SCALE) * inverse)
        sg = (p * (pgrad[part] - row_delta) * SCALE).astype(BF16)
        grad = dot(sg, qry[...])
        value = dot(p.astype(BF16), lgr[...])
        kgrad[part, :, :, :LATENT] = (grad[:, :LATENT] + value).reshape(CORE, Y * BLOCK, LATENT)
        kgrad[part, :, :, LATENT:] = grad[:, LATENT:].reshape(CORE, Y * BLOCK, ROPE)
        c1s[part] = kgrad[part, 1 - core].astype(BF16)
        core_sums[dz] = sems.copy(c1s.at[part], c1r.at[part], sibling)

    def add_cores(dz):
        part = zh_by(-dz)
        core_sums[dz].wait_recv()
        both = kgrad[part, core] + c1r[part].astype(F32)
        kgrad[part, core] = both
        c2s[dz] = both.reshape(Y, BLOCK, WIDTH).astype(BF16)
        y_sums[dz] = [
            sems.copy(c2s.at[dz, y_by(d)], c2r.at[dz, d - 1], at(y_=y_by(d))) for d in (2, 1, 3)
        ]

    def add_ys(dz):
        for made in y_sums[dz]:
            made.wait_recv()
        rows = pl.ds(pl.multiple_of(y * BLOCK, BLOCK), BLOCK)
        mine = kgrad[zh_by(-dz), core, rows, :]
        for i in range(Y - 1):
            mine += c2r[dz, i].astype(F32)
        return mine

    def send_far(mine):
        c3s[2] = mine.astype(BF16)
        return [
            sems.copy(c3s.at[2, pl.ds(0, half)], c3h.at[0], at(zh_=zh_by(1))),
            sems.copy(c3s.at[2, pl.ds(half, half)], c3h.at[1], at(zh_=zh_by(-1))),
        ]

    def send_near(halves, up, down):
        for made in halves:
            made.wait_recv()
        c3s[0, :half] = (up[:half] + c3h[0].astype(F32)).astype(BF16)
        c3s[0, half:] = up[half:].astype(BF16)
        c3s[1, :half] = down[:half].astype(BF16)
        c3s[1, half:] = (down[half:] + c3h[1].astype(F32)).astype(BF16)
        return [
            sems.copy(c3s.at[0], c3r.at[0], at(zh_=zh_by(1))),
            sems.copy(c3s.at[1], c3r.at[1], at(zh_=zh_by(-1))),
        ]

    for g in range(2):
        for e in ORDER:
            send_near_x(e, g)
    key_grads(2)
    for e in ORDER:
        sum_x(e, 0)
    key_grads(1)
    add_cores(2)
    for e in ORDER:
        sum_x(e, 1)
    rope_zl = sum_rope_x()
    key_grads(3)
    add_cores(1)
    key_grads(0)
    add_cores(3)
    back_0 = sum_zl(0)
    add_cores(0)
    halves = send_far(add_ys(2))
    back_1 = sum_zl(1)
    sum_rope_zl(rope_zl)
    gather_x(back_0, 0)
    up, down, final = add_ys(3), add_ys(1), add_ys(0)
    near = send_near(halves, up, down)
    gather_x(back_1, 1)
    forward_x(2, 0)
    forward_x(2, 1)

    spread = finish(0) + finish(1) + finish(3)
    for made in to_far:
        made.wait_recv()
    spread += finish(2)
    for made in rope_far:
        made.wait_recv()
    for b in range(X):
        query_out[NOPE + b * RCOLS : NOPE + (b + 1) * RCOLS, :] = rope_a[b].astype(F32)
    head_of = lane & (HEADS - 1)
    nope = spread[:NOPE, :]
    for h in range(1, HEADS):
        nope = jnp.where(head_of == h, spread[h * NOPE : (h + 1) * NOPE, :], nope)
    query_out[:NOPE, :] = nope
    value_out[...] = whole[:, ROWS:]
    for made in near:
        made.wait_recv()
    keys_out[...] = final + c3r[0].astype(F32) + c3r[1].astype(F32)
    for made in sems.started:
        made.wait_send()


def unpack(
    keys_ref, value_ref, key_up_ref, query_ref,
    prompt_out, suffix_out, query_out, key_up_out, value_up_out,
):
    prompt_out[0] = keys_ref[:PKEYS, :]
    prompt_out[1] = keys_ref[PKEYS : 2 * PKEYS, :]
    suffix_out[0] = keys_ref[2 * PKEYS :, :]
    for h in range(HEADS):
        value_up_out[h * LATENT : (h + 1) * LATENT, :] = value_ref[
            :, h * VHEAD : (h + 1) * VHEAD
        ].astype(F32)
    for b in range(X):
        key_up_out[:, b * TILE : (b + 1) * TILE] = key_up_ref[b]
    steps = TILE // HEADS
    for t in range(TILES):
        part = query_ref[:, t * TILE : (t + 1) * TILE].T
        query_out[t * steps : (t + 1) * steps] = part.reshape(steps, HEADS, QUERY)


def shards(prompt, suffix, queries, key_up, value_up, out_grad, fork_prompt, suffix_length):
    vmem = pl.BlockSpec(memory_space=pltpu.VMEM)
    smem = pl.BlockSpec(memory_space=pltpu.SMEM)
    copies = 184
    hbm = pl.BlockSpec(memory_space=pltpu.HBM)

    def in_hbm(v):
        return pltpu.with_memory_space_constraint(v, pltpu.HBM)

    steps = FORKS * RECOMP
    sums = pl.pallas_call(
        kernel,
        out_shape=(
            jax.ShapeDtypeStruct((BLOCK, WIDTH), F32),
            jax.ShapeDtypeStruct((LATENT, HEADS * VHEAD), BF16),
            jax.ShapeDtypeStruct((X, HEADS * NOPE, TILE), F32),
            jax.ShapeDtypeStruct((QUERY, ROWS), F32),
        ),
        in_specs=[vmem] * 2 + [hbm] * 4 + [smem] * 2,
        out_specs=(vmem,) * 4,
        scratch_shapes=[
            pltpu.VMEM((ZH, CORE, Y, BLOCK, WIDTH), BF16),
            pltpu.VMEM((ROWS, WIDTH), BF16),
            pltpu.VMEM((WIDTH, ROWS), BF16),
            pltpu.VMEM((ROWS, LATENT), BF16),
            pltpu.VMEM((LATENT, ROWS), BF16),
            pltpu.VMEM((ROWS, HEADS * VHEAD), BF16),
            pltpu.VMEM((HEADS * NOPE, ROWS), BF16),
            pltpu.VMEM((ZH, KEYS, ROWS), F32),
            pltpu.VMEM((ZH, KEYS, ROWS), F32),
            pltpu.VMEM((ZH, KEYS, ROWS), F32),
            pltpu.VMEM((ZH, 1, ROWS), F32),
            pltpu.VMEM((WIDTH, ROWS), F32),
            pltpu.VMEM((WIDTH, ROWS), F32),
            pltpu.VMEM((ZH, CORE, Y * BLOCK, WIDTH), F32),
            pltpu.VMEM((16, TILE), F32),
            pltpu.VMEM((ZL * X, 16, TILE), F32),
            pltpu.VMEM((ZH, Y * BLOCK, WIDTH), BF16),
            pltpu.VMEM((ZH, Y * BLOCK, WIDTH), BF16),
            pltpu.VMEM((ZH, Y, BLOCK, WIDTH), BF16),
            pltpu.VMEM((ZH, Y - 1, BLOCK, WIDTH), BF16),
            pltpu.VMEM((ZH - 1, BLOCK, WIDTH), BF16),
            pltpu.VMEM((2, BLOCK // 2, WIDTH), BF16),
            pltpu.VMEM((2, BLOCK, WIDTH), BF16),
            pltpu.VMEM((ZL, 2, 2, GROUP, ROWS), BF16),
            pltpu.VMEM((ZL, 2, 2, GROUP, ROWS), BF16),
            pltpu.VMEM((2, ZL, 2, 2, GROUP, ROWS), BF16),
            pltpu.VMEM((2, ZL, 2, 2, GROUP, ROWS), BF16),
            pltpu.VMEM((ZL, 2, 2, GROUP, ROWS), BF16),
            pltpu.VMEM((ZL - 1, 2, 2, GROUP, ROWS), BF16),
            pltpu.VMEM((X, 2, RCOLS, ROWS), BF16),
            pltpu.VMEM((X - 1, 2, RCOLS, ROWS), BF16),
            pltpu.VMEM((ZL, RCOLS, ROWS), BF16),
            pltpu.VMEM((LATENT, ROWS + HEADS * VHEAD), BF16),
            pltpu.VMEM((X, RCOLS, ROWS), BF16),
            pltpu.VMEM((steps, HEADS, QUERY), BF16),
            pltpu.VMEM((HEADS * NOPE, LATENT), BF16),
            pltpu.VMEM((HEADS * LATENT, VHEAD), BF16),
            pltpu.VMEM((steps, HEADS, VHEAD), BF16),
            pltpu.SemaphoreType.DMA((copies,)),
            pltpu.SemaphoreType.DMA((copies,)),
            pltpu.SemaphoreType.DMA((4,)),
        ],
        compiler_params=pltpu.CompilerParams(
            collective_id=0, has_side_effects=True, vmem_limit_bytes=42 << 20
        ),
        cost_estimate=pl.CostEstimate(
            flops=8_000_000_000, bytes_accessed=6_000_000, transcendentals=700_000
        ),
        name="latent_backward",
    )(
        in_hbm(prompt),
        in_hbm(suffix),
        in_hbm(queries.reshape(steps, HEADS, QUERY)),
        in_hbm(key_up.reshape(HEADS * NOPE, LATENT)),
        in_hbm(value_up.reshape(HEADS * LATENT, VHEAD)),
        in_hbm(out_grad.reshape(steps, HEADS, VHEAD)),
        in_hbm(fork_prompt),
        in_hbm(suffix_length),
    )
    prompt_grad, suffix_grad, query_grad, key_up_grad, value_up_grad = pl.pallas_call(
        unpack,
        out_shape=(
            jax.ShapeDtypeStruct((2, PKEYS, WIDTH), F32),
            jax.ShapeDtypeStruct((1, SKEYS, WIDTH), F32),
            jax.ShapeDtypeStruct((steps, HEADS, QUERY), F32),
            jax.ShapeDtypeStruct((HEADS * NOPE, LATENT), F32),
            jax.ShapeDtypeStruct((HEADS * LATENT, VHEAD), F32),
        ),
        in_specs=[vmem] * 4,
        out_specs=(vmem,) * 5,
        compiler_params=pltpu.CompilerParams(vmem_limit_bytes=16 << 20),
        name="unpack_grads",
    )(*sums)
    return (
        prompt_grad,
        suffix_grad,
        query_grad.reshape(FORKS, RECOMP, HEADS, QUERY),
        key_up_grad.reshape(HEADS, NOPE, LATENT),
        value_up_grad.reshape(HEADS, LATENT, VHEAD),
    )


def solution(mesh):
    return jax.shard_map(
        shards,
        mesh=mesh,
        in_specs=(
            P(None, ("ctx", "sample"), None),
            P("sample", "ctx", None),
            P(None, None, "sample", None),
            P("sample", None, None),
            P("sample", None, None),
            P(None, None, "sample", None),
            P(),
            P(),
        ),
        out_specs=(
            P(None, ("ctx", "sample"), None),
            P("sample", "ctx", None),
            P(None, None, "sample", None),
            P("sample", None, None),
            P("sample", None, None),
        ),
        check_vma=False,
    )
```

```python
import functools

import jax
import jax.numpy as jnp
from jax import lax
from jax.experimental import pallas as pl
from jax.experimental.pallas import tpu as pltpu
from jax.sharding import PartitionSpec as P

MESH = pl.DeviceIdType.MESH
F32 = jnp.float32
BF16 = jnp.bfloat16
HIDDEN = -1e30

ZL, X, ZH, Y, CORE = 4, 4, 4, 4, 2
FORKS, RECOMP, HEADS = 32, 5, 4
NOPE, ROPE, LATENT, VHEAD = 128, 64, 512, 128
WIDTH = LATENT + ROPE
QUERY = NOPE + ROPE
ROWS = FORKS * RECOMP * HEADS
TILE = 128
TILES = ROWS // TILE
PKEYS, SKEYS = 8, 16
BLOCK = 2 * PKEYS + SKEYS
KEYS = CORE * Y * BLOCK
SCALE = QUERY**-0.5
COLS = LATENT // (X * ZL)
GROUP = COLS // 2
RCOLS = ROPE // X


def dot(a, b):
    return jnp.dot(a, b, preferred_element_type=F32)


def dot_nt(a, b):
    return lax.dot_general(a, b, (((1,), (1,)), ((), ())), preferred_element_type=F32)


class Sems:
    def __init__(self, send, recv):
        self.send, self.recv, self.used, self.started = send, recv, 0, []

    def copy(self, src, dst, device):
        k = self.used
        self.used += 1
        made = pltpu.make_async_remote_copy(
            src_ref=src,
            dst_ref=dst,
            send_sem=self.send.at[k],
            recv_sem=self.recv.at[k],
            device_id=device,
            device_id_type=MESH,
        )
        made.start()
        self.started.append(made)
        return made


def kernel(
    prompt_any, suffix_any, q_any, ku_any, vu_any, og_any, fork_any, length_any,
    keys_out, value_out, key_up_out, query_out,
    keys, qry, qry_t, lgr, lgr_t, og_exp, qn_exp_t, bias, score, pgrad, peaks,
    acc_t, dif_t, kgrad, stat, stat_all, c1s, c1r, c2s, c2r, c3s, c3h, c3r,
    far_s, far_r, near_s, near_r, lat_m, lat_z, rope_s, rope_r, rope_z, whole, rope_a,
    prompt_ref, suffix_ref, q_ref, ku_ref, vu_ref, og_ref, fork_ref, length_ref,
    send_sem, recv_sem, load_sem,
):
    ctx, sample = lax.axis_index("ctx"), lax.axis_index("sample")
    zl, x = ctx // X, ctx % X
    zh, y, core = sample // (Y * CORE), (sample // CORE) % Y, sample % CORE

    def at(zl_=zl, x_=x, zh_=zh, y_=y, core_=core):
        return (zl_ * X + x_, zh_ * (Y * CORE) + y_ * CORE + core_)

    sibling = at(core_=1 - core)

    def zh_by(d):
        return (zh + d + ZH) % ZH

    def y_by(d):
        return (y + d + Y) % Y

    def x_by(d):
        return (x + d + X) % X

    def zl_by(d):
        return (zl + d + ZL) % ZL

    sems = Sems(send_sem, recv_sem)
    pairs = (
        (prompt_any, prompt_ref), (suffix_any, suffix_ref), (q_any, q_ref), (ku_any, ku_ref),
        (og_any, og_ref), (vu_any, vu_ref), (fork_any, fork_ref), (length_any, length_ref),
    )
    loads = [pltpu.make_async_copy(*pair, load_sem.at[k]) for k, pair in enumerate(pairs)]
    for made in loads[:2]:
        made.start()

    partners = [at(zh_=zh_by(d)) for d in (1, -1)]
    partners += [at(zl_=zl_by(a), x_=x_by(b)) for a in (2, 1, 3, 0) for b in (2, 1, 3, 0) if a + b]
    partners += [at(y_=y_by(d)) for d in (2, 1, 3)]
    partners += [at(y_=y_by(d), core_=1 - core) for d in (2, 1, 3)]
    partners += [sibling]
    barrier = pltpu.get_barrier_semaphore()
    for device in partners:
        pl.semaphore_signal(barrier, inc=1, device_id=device, device_id_type=MESH)
    for made in loads[2:]:
        made.start()
    for made in loads[:2]:
        made.wait()
    own = jnp.concatenate(
        [prompt_ref[0].astype(F32), prompt_ref[1].astype(F32), suffix_ref[0].astype(F32)], 0
    ).astype(BF16)
    keys[zh, core, y] = own
    pl.semaphore_wait(barrier, len(partners))

    from_zh = {}
    from_y = {}
    from_core = {}
    for d in (1, 3):
        block = keys.at[zh, core, y]
        from_zh[d] = [sems.copy(block, block, at(zh_=zh_by(d)))]
    half = BLOCK // 2

    def relay(d, rows):
        from_zh[d][0].wait_recv()
        part = keys.at[zh_by(-d), core, y, rows]
        from_zh.setdefault(2, []).append(sems.copy(part, part, at(zh_=zh_by(d))))

    def spread_y(dz):
        if dz == 2:
            for made in from_zh[dz]:
                made.wait_recv()
        block = keys.at[zh_by(-dz), core, y]
        from_y[dz] = [sems.copy(block, block, at(y_=y_by(d))) for d in (2, 1, 3)]
        if dz == 2:
            from_core[dz] = [
                sems.copy(block, block, at(y_=y_by(d), core_=1 - core)) for d in (2, 1, 3, 0)
            ]

    def to_core(dz):
        for made in from_y[dz]:
            made.wait_recv()
        part = keys.at[zh_by(-dz), core]
        from_core[dz] = [sems.copy(part, part, sibling)]

    spread_y(0)

    lane = lax.broadcasted_iota(jnp.int32, (1, ROWS), 1)
    row_fork = (lane * 3277) >> 16
    row_step = (lane - row_fork * (RECOMP * HEADS)) >> 2

    def project(t, carry):
        rows = pl.ds(pl.multiple_of(t * TILE, TILE), TILE)
        steps = pl.ds(t * (TILE // HEADS), TILE // HEADS)
        q = q_ref[steps].reshape(TILE, QUERY)
        og = og_ref[steps].reshape(TILE, VHEAD)
        head = lax.broadcasted_iota(jnp.int32, (TILE, NOPE), 0) & (HEADS - 1)
        q_nope = q[:, :NOPE]
        zero = jnp.zeros_like(q_nope)
        q_exp = jnp.concatenate([jnp.where(head == h, q_nope, zero) for h in range(HEADS)], 1)
        o_exp = jnp.concatenate([jnp.where(head == h, og, zero) for h in range(HEADS)], 1)
        og_exp[rows, :] = o_exp
        q_t = q_nope.T
        head_t = lax.broadcasted_iota(jnp.int32, (NOPE, TILE), 1) & (HEADS - 1)
        qn_exp_t[:, rows] = jnp.concatenate(
            [jnp.where(head_t == h, q_t, zero) for h in range(HEADS)], 0
        )
        whole = jnp.concatenate([dot(q_exp, ku_ref[...]).astype(BF16), q[:, NOPE:]], 1)
        qry[rows, :] = whole
        qry_t[:, rows] = whole.T
        grad = dot_nt(o_exp[:, :VHEAD], vu_ref[pl.ds(0, LATENT), :])
        for h in range(1, HEADS):
            grad += dot_nt(
                o_exp[:, h * VHEAD : (h + 1) * VHEAD], vu_ref[pl.ds(h * LATENT, LATENT), :]
            )
        grad = grad.astype(BF16)
        lgr[rows, :] = grad
        lgr_t[:, rows] = grad.T
        return carry

    for made in loads[2:]:
        made.wait()
    lax.fori_loop(0, 2, project, 0)
    relay(1, pl.ds(0, half))
    relay(3, pl.ds(half, half))
    spread_y(1)
    spread_y(3)
    lax.fori_loop(2, TILES, project, 0)

    def gather_rows(f, carry):
        limit, prompt = carry
        mine = row_fork == f
        return jnp.where(mine, length_ref[f], limit), jnp.where(mine, fork_ref[f], prompt)

    none = jnp.zeros((1, ROWS), jnp.int32)
    row_limit, row_prompt = lax.fori_loop(0, FORKS, gather_rows, (none, none))
    row_limit = row_limit - RECOMP + row_step
    first = jnp.broadcast_to(jnp.where(row_prompt == 0, 0.0, HIDDEN), (PKEYS, ROWS))
    second = jnp.broadcast_to(jnp.where(row_prompt == 1, 0.0, HIDDEN), (PKEYS, ROWS))
    position = ctx * SKEYS + lax.broadcasted_iota(jnp.int32, (SKEYS, ROWS), 0)

    def make_bias(b, carry):
        bz, bc, by = b // (CORE * Y), (b // Y) % CORE, b % Y
        fork = bz * (Y * CORE) + by * CORE + bc
        last = jnp.where(row_fork == fork, row_limit, -1)
        seen = jnp.where(position <= last, 0.0, HIDDEN)
        bias[bz, pl.ds(pl.multiple_of((bc * Y + by) * BLOCK, BLOCK), BLOCK), :] = (
            jnp.concatenate([first, second, seen], 0)
        )
        return carry

    to_core(0)
    lax.fori_loop(0, Y * CORE * ZH, make_bias, 0)

    def scores_of(dz):
        for made in from_core[dz]:
            made.wait_recv()
        part = zh_by(-dz)
        tile = keys[part].reshape(KEYS, WIDTH)
        s = dot(tile, qry_t[...]) + bias[part]
        peak = jnp.max(s, 0, keepdims=True)
        p = jnp.exp((s - peak) * SCALE)
        score[part] = p
        grad = dot(tile[:, :LATENT], lgr_t[...])
        pgrad[part] = grad
        total = jnp.sum(p, 0, keepdims=True)
        mean = jnp.sum(p * grad, 0, keepdims=True) / total
        peaks[dz] = peak
        return part, peak, total, mean

    def merged(left, right):
        top = jnp.maximum(left[0], right[0])
        shrink_left = jnp.exp((left[0] - top) * SCALE)
        shrink_right = jnp.exp((right[0] - top) * SCALE)
        total_left, total_right = left[1] * shrink_left, right[1] * shrink_right
        total = total_left + total_right
        mean = (total_left * left[2] + total_right * right[2]) / total
        return (top, total, mean), shrink_left, shrink_right

    def sums_of(part, mean):
        tile_t = keys[part].reshape(KEYS, WIDTH).T
        p = score[part]
        return dot(tile_t, p.astype(BF16)), dot(
            tile_t, (p * (pgrad[part] - mean)).astype(BF16)
        )

    def add_sums(state, new, part):
        both, shrink_left, shrink_right = merged(state, new)
        acc, grad = sums_of(part, new[2])
        old = acc_t[...]
        acc_t[...] = shrink_left * old + shrink_right * acc
        dif_t[...] = shrink_left * (dif_t[...] + (state[2] - both[2]) * old) + shrink_right * (
            grad + (new[2] - both[2]) * acc
        )
        return both

    part, *state = scores_of(0)
    acc_t[...], dif_t[...] = sums_of(part, state[2])
    to_core(1)
    to_core(3)
    spread_y(2)
    part, *new = scores_of(1)
    state = add_sums(state, new, part)
    part, *new = scores_of(3)
    state = add_sums(state, new, part)
    for made in from_y[2]:
        made.wait_recv()
    part, *new = scores_of(2)
    (peak, total, mean), _, _ = merged(state, new)

    delta = mean * total
    for t in range(TILES):
        cols = slice(t * TILE, (t + 1) * TILE)
        stat[t : t + 1, :] = peak[:, cols]
        stat[TILES + t : TILES + t + 1, :] = total[:, cols]
        stat[2 * TILES + t : 2 * TILES + t + 1, :] = delta[:, cols]
    stat[3 * TILES : 3 * TILES + 1, :] = jnp.zeros((1, TILE), F32)
    stat_copies = []
    for a in range(ZL):
        for b in range(X):
            if a + b:
                stat_copies.append(
                    sems.copy(stat, stat_all.at[ctx], at(zl_=zl_by(a), x_=x_by(b)))
                )
    stat_all[ctx] = stat[...]

    add_sums(state, new, part)
    ORDER = (2, 1, 3, 0)
    FAR_LANES = (slice(0, 3 * TILE), slice(3 * TILE, ROWS))
    OUT_LANES = (slice(0, ROWS), slice(ROWS, ROWS + HEADS * VHEAD))

    def block_of(to_x, to_zl, g):
        return pl.ds(pl.multiple_of((to_x * ZL + to_zl) * COLS + g * GROUP, GROUP), GROUP)

    far_x = {}
    for g in range(2):
        for e in ORDER:
            to = zl_by(e)
            rows = block_of(x_by(2), to, g)
            far_s[to, g, 0] = acc_t[rows, :].astype(BF16)
            far_s[to, g, 1] = dif_t[rows, :].astype(BF16)
            far_x[e, g] = [
                sems.copy(
                    far_s.at[to, g, :, :, FAR_LANES[k]],
                    far_r.at[to, g, :, :, FAR_LANES[k]],
                    at(x_=x_by(1 - 2 * k)),
                )
                for k in range(2)
            ]
    for b in range(X):
        rows = slice(LATENT + b * RCOLS, LATENT + (b + 1) * RCOLS)
        rope_s[b, 0] = acc_t[rows, :].astype(BF16)
        rope_s[b, 1] = dif_t[rows, :].astype(BF16)
    rope_x = [
        sems.copy(rope_s.at[x_by(d)], rope_r.at[d - 1], at(x_=x_by(d))) for d in (2, 1, 3)
    ]

    for made in stat_copies:
        made.wait_recv()
    all_peak = stat_all[:, 0:TILES, :]
    top = jnp.max(all_peak, 0)
    shrink = jnp.exp((all_peak - top[None]) * SCALE)
    whole_total = jnp.sum(stat_all[:, TILES : 2 * TILES, :] * shrink, 0)
    whole_delta = jnp.sum(stat_all[:, 2 * TILES : 3 * TILES, :] * shrink, 0)
    inverse = 1.0 / whole_total

    def as_row(v):
        return jnp.concatenate([v[t : t + 1, :] for t in range(TILES)], 1)

    def weigh(d):
        if d == 0:
            one = stat
        else:
            one = stat_all.at[zl * X + x_by(-d)]
        factor = jnp.exp((one[0:TILES, :] - top) * SCALE) * inverse
        shift = whole_delta * inverse - one[2 * TILES : 3 * TILES, :] / one[TILES : 2 * TILES, :]
        return as_row(factor), as_row(shift)

    weights = [weigh(d) for d in range(X)]
    top, inverse, row_delta = as_row(top), as_row(inverse), as_row(whole_delta * inverse)

    def weighted(d, acc, dif, lanes=slice(0, ROWS)):
        factor, shift = weights[d][0][:, lanes], weights[d][1][:, lanes]
        return factor * acc, (factor * SCALE) * (dif - shift * acc)

    near_x = {}

    def send_near_x(e, g):
        to = zl_by(e)
        near_x[e, g] = []
        for k in range(2):
            far_x[e, g][k].wait_recv()
            rows = block_of(x_by(1 - 2 * k), to, g)
            own = weighted(0, acc_t[rows, :], dif_t[rows, :])
            added, other = FAR_LANES[k], FAR_LANES[1 - k]
            came = weighted(
                1 + 2 * k,
                far_r[to, g, 0, :, added].astype(F32),
                far_r[to, g, 1, :, added].astype(F32),
                added,
            )
            for i in range(2):
                near_s[k, to, g, i, :, added] = (own[i][:, added] + came[i]).astype(BF16)
                near_s[k, to, g, i, :, other] = own[i][:, other].astype(BF16)
            near_x[e, g].append(
                sems.copy(near_s.at[k, to, g], near_r.at[k, to, g], at(x_=x_by(1 - 2 * k)))
            )

    lat_zl = [[], []]

    def sum_x(e, g):
        for made in near_x[e, g]:
            made.wait_recv()
        to = zl_by(e)
        rows = block_of(x, to, g)
        own = weighted(0, acc_t[rows, :], dif_t[rows, :])
        for i in range(2):
            add = own[i] + near_r[0, to, g, i].astype(F32) + near_r[1, to, g, i].astype(F32)
            lat_m[to, g, i] = add.astype(BF16)
        if e:
            lat_zl[g].append(sems.copy(lat_m.at[to, g], lat_z.at[e - 1, g], at(zl_=to)))

    def sum_rope_x():
        for made in rope_x:
            made.wait_recv()
        rows = pl.ds(pl.multiple_of(LATENT + x * RCOLS, RCOLS), RCOLS)

        grad = weighted(0, acc_t[rows, :], dif_t[rows, :])[1]
        for d in (1, 2, 3):
            grad += weighted(d, rope_r[d - 1, 0].astype(F32), rope_r[d - 1, 1].astype(F32))[1]
        rope_z[zl] = grad.astype(BF16)
        block = rope_z.at[zl]
        return [sems.copy(block, block, at(zl_=zl_by(e))) for e in (2, 1, 3)]

    to_near = {}
    to_far = []

    def spread_x(e, g):
        block = whole.at[block_of(x, zl_by(-e), g), :]
        to_near[e, g] = [sems.copy(block, block, at(x_=x_by(1 - 2 * k))) for k in range(2)]

    def forward_x(e, g):
        for k in range(2):
            to_near[e, g][k].wait_recv()
            block = whole.at[block_of(x_by(2 * k - 1), zl_by(-e), g), OUT_LANES[k]]
            to_far.append(sems.copy(block, block, at(x_=x_by(1 - 2 * k))))

    rope_far = []

    def sum_zl(g):
        for made in lat_zl[g]:
            made.wait_recv()
        out = lat_m[zl, g, 0].astype(F32)
        grad = lat_m[zl, g, 1].astype(F32)
        for i in range(ZL - 1):
            out += lat_z[i, g, 0].astype(F32)
            grad += lat_z[i, g, 1].astype(F32)
        rows = block_of(x, zl, g)
        whole[rows, :ROWS] = grad.astype(BF16)
        whole[rows, ROWS:] = dot(out.astype(BF16), og_exp[...]).astype(BF16)
        block = whole.at[rows, :]
        back = {e: sems.copy(block, block, at(zl_=zl_by(e))) for e in (2, 1, 3)}
        spread_x(0, g)
        return back

    def sum_rope_zl(made):
        for m in made:
            m.wait_recv()
        grad = rope_z[0].astype(F32)
        for i in range(1, ZL):
            grad += rope_z[i].astype(F32)
        rope_a[x] = grad.astype(BF16)
        block = rope_a.at[x]
        for d in (2, 1, 3):
            rope_far.append(sems.copy(block, block, at(x_=x_by(d))))

    def gather_x(back, g):
        done = 0
        for e in (1, 3, 2):
            back[e].wait_recv()
            spread_x(e, g)
            forward_x(done, g)
            done = e

    def finish(d):
        b = x_by(-d)
        cols = pl.ds(pl.multiple_of(b * TILE, TILE), TILE)
        lat = whole[cols, :ROWS]
        key_up_out[b] = dot_nt(qn_exp_t[...], lat)
        return dot(ku_ref[:, cols], lat)

    core_sums, y_sums, zh_sums = {}, {}, {}

    def key_grads(dz):
        part = zh_by(-dz)
        p = score[part] * (jnp.exp((peaks[dz] - top) * SCALE) * inverse)
        sg = (p * (pgrad[part] - row_delta) * SCALE).astype(BF16)
        grad = dot(sg, qry[...])
        value = dot(p.astype(BF16), lgr[...])
        kgrad[part, :, :, :LATENT] = (grad[:, :LATENT] + value).reshape(CORE, Y * BLOCK, LATENT)
        kgrad[part, :, :, LATENT:] = grad[:, LATENT:].reshape(CORE, Y * BLOCK, ROPE)
        c1s[part] = kgrad[part, 1 - core].astype(BF16)
        core_sums[dz] = sems.copy(c1s.at[part], c1r.at[part], sibling)

    def add_cores(dz):
        part = zh_by(-dz)
        core_sums[dz].wait_recv()
        both = kgrad[part, core] + c1r[part].astype(F32)
        kgrad[part, core] = both
        c2s[dz] = both.reshape(Y, BLOCK, WIDTH).astype(BF16)
        y_sums[dz] = [
            sems.copy(c2s.at[dz, y_by(d)], c2r.at[dz, d - 1], at(y_=y_by(d))) for d in (2, 1, 3)
        ]

    def add_ys(dz):
        for made in y_sums[dz]:
            made.wait_recv()
        rows = pl.ds(pl.multiple_of(y * BLOCK, BLOCK), BLOCK)
        mine = kgrad[zh_by(-dz), core, rows, :]
        for i in range(Y - 1):
            mine += c2r[dz, i].astype(F32)
        return mine

    def send_far(mine):
        c3s[2] = mine.astype(BF16)
        return [
            sems.copy(c3s.at[2, pl.ds(0, half)], c3h.at[0], at(zh_=zh_by(1))),
            sems.copy(c3s.at[2, pl.ds(half, half)], c3h.at[1], at(zh_=zh_by(-1))),
        ]

    def send_near(halves, up, down):
        for made in halves:
            made.wait_recv()
        c3s[0, :half] = (up[:half] + c3h[0].astype(F32)).astype(BF16)
        c3s[0, half:] = up[half:].astype(BF16)
        c3s[1, :half] = down[:half].astype(BF16)
        c3s[1, half:] = (down[half:] + c3h[1].astype(F32)).astype(BF16)
        return [
            sems.copy(c3s.at[0], c3r.at[0], at(zh_=zh_by(1))),
            sems.copy(c3s.at[1], c3r.at[1], at(zh_=zh_by(-1))),
        ]

    for g in range(2):
        for e in ORDER:
            send_near_x(e, g)
    key_grads(2)
    for e in ORDER:
        sum_x(e, 0)
    key_grads(1)
    add_cores(2)
    for e in ORDER:
        sum_x(e, 1)
    rope_zl = sum_rope_x()
    key_grads(3)
    add_cores(1)
    key_grads(0)
    add_cores(3)
    back_0 = sum_zl(0)
    add_cores(0)
    halves = send_far(add_ys(2))
    back_1 = sum_zl(1)
    sum_rope_zl(rope_zl)
    gather_x(back_0, 0)
    up, down, final = add_ys(3), add_ys(1), add_ys(0)
    near = send_near(halves, up, down)
    gather_x(back_1, 1)
    forward_x(2, 0)
    forward_x(2, 1)

    spread = finish(0) + finish(1) + finish(3)
    for made in to_far:
        made.wait_recv()
    spread += finish(2)
    for made in rope_far:
        made.wait_recv()
    for b in range(X):
        query_out[NOPE + b * RCOLS : NOPE + (b + 1) * RCOLS, :] = rope_a[b].astype(F32)
    head_of = lane & (HEADS - 1)
    nope = spread[:NOPE, :]
    for h in range(1, HEADS):
        nope = jnp.where(head_of == h, spread[h * NOPE : (h + 1) * NOPE, :], nope)
    query_out[:NOPE, :] = nope
    value_out[...] = whole[:, ROWS:]
    for made in near:
        made.wait_recv()
    keys_out[...] = final + c3r[0].astype(F32) + c3r[1].astype(F32)
    for made in sems.started:
        made.wait_send()


def unpack(
    keys_ref, value_ref, key_up_ref, query_ref,
    prompt_out, suffix_out, query_out, key_up_out, value_up_out,
):
    prompt_out[0] = keys_ref[:PKEYS, :]
    prompt_out[1] = keys_ref[PKEYS : 2 * PKEYS, :]
    suffix_out[0] = keys_ref[2 * PKEYS :, :]
    for h in range(HEADS):
        value_up_out[h * LATENT : (h + 1) * LATENT, :] = value_ref[
            :, h * VHEAD : (h + 1) * VHEAD
        ].astype(F32)
    for b in range(X):
        key_up_out[:, b * TILE : (b + 1) * TILE] = key_up_ref[b]
    steps = TILE // HEADS
    for t in range(TILES):
        part = query_ref[:, t * TILE : (t + 1) * TILE].T
        query_out[t * steps : (t + 1) * steps] = part.reshape(steps, HEADS, QUERY)


def shards(prompt, suffix, queries, key_up, value_up, out_grad, fork_prompt, suffix_length):
    vmem = pl.BlockSpec(memory_space=pltpu.VMEM)
    copies = 184
    hbm = pl.BlockSpec(memory_space=pltpu.HBM)

    def in_hbm(v):
        return pltpu.with_memory_space_constraint(v, pltpu.HBM)

    steps = FORKS * RECOMP
    sums = pl.pallas_call(
        kernel,
        out_shape=(
            jax.ShapeDtypeStruct((BLOCK, WIDTH), F32),
            jax.ShapeDtypeStruct((LATENT, HEADS * VHEAD), BF16),
            jax.ShapeDtypeStruct((X, HEADS * NOPE, TILE), F32),
            jax.ShapeDtypeStruct((QUERY, ROWS), F32),
        ),
        in_specs=[hbm] * 8,
        out_specs=(vmem,) * 4,
        scratch_shapes=[
            pltpu.VMEM((ZH, CORE, Y, BLOCK, WIDTH), BF16),
            pltpu.VMEM((ROWS, WIDTH), BF16),
            pltpu.VMEM((WIDTH, ROWS), BF16),
            pltpu.VMEM((ROWS, LATENT), BF16),
            pltpu.VMEM((LATENT, ROWS), BF16),
            pltpu.VMEM((ROWS, HEADS * VHEAD), BF16),
            pltpu.VMEM((HEADS * NOPE, ROWS), BF16),
            pltpu.VMEM((ZH, KEYS, ROWS), F32),
            pltpu.VMEM((ZH, KEYS, ROWS), F32),
            pltpu.VMEM((ZH, KEYS, ROWS), F32),
            pltpu.VMEM((ZH, 1, ROWS), F32),
            pltpu.VMEM((WIDTH, ROWS), F32),
            pltpu.VMEM((WIDTH, ROWS), F32),
            pltpu.VMEM((ZH, CORE, Y * BLOCK, WIDTH), F32),
            pltpu.VMEM((16, TILE), F32),
            pltpu.VMEM((ZL * X, 16, TILE), F32),
            pltpu.VMEM((ZH, Y * BLOCK, WIDTH), BF16),
            pltpu.VMEM((ZH, Y * BLOCK, WIDTH), BF16),
            pltpu.VMEM((ZH, Y, BLOCK, WIDTH), BF16),
            pltpu.VMEM((ZH, Y - 1, BLOCK, WIDTH), BF16),
            pltpu.VMEM((ZH - 1, BLOCK, WIDTH), BF16),
            pltpu.VMEM((2, BLOCK // 2, WIDTH), BF16),
            pltpu.VMEM((2, BLOCK, WIDTH), BF16),
            pltpu.VMEM((ZL, 2, 2, GROUP, ROWS), BF16),
            pltpu.VMEM((ZL, 2, 2, GROUP, ROWS), BF16),
            pltpu.VMEM((2, ZL, 2, 2, GROUP, ROWS), BF16),
            pltpu.VMEM((2, ZL, 2, 2, GROUP, ROWS), BF16),
            pltpu.VMEM((ZL, 2, 2, GROUP, ROWS), BF16),
            pltpu.VMEM((ZL - 1, 2, 2, GROUP, ROWS), BF16),
            pltpu.VMEM((X, 2, RCOLS, ROWS), BF16),
            pltpu.VMEM((X - 1, 2, RCOLS, ROWS), BF16),
            pltpu.VMEM((ZL, RCOLS, ROWS), BF16),
            pltpu.VMEM((LATENT, ROWS + HEADS * VHEAD), BF16),
            pltpu.VMEM((X, RCOLS, ROWS), BF16),
            pltpu.VMEM((2, PKEYS, WIDTH), BF16),
            pltpu.VMEM((1, SKEYS, WIDTH), BF16),
            pltpu.VMEM((steps, HEADS, QUERY), BF16),
            pltpu.VMEM((HEADS * NOPE, LATENT), BF16),
            pltpu.VMEM((HEADS * LATENT, VHEAD), BF16),
            pltpu.VMEM((steps, HEADS, VHEAD), BF16),
            pltpu.SMEM((FORKS,), jnp.int32),
            pltpu.SMEM((FORKS,), jnp.int32),
            pltpu.SemaphoreType.DMA((copies,)),
            pltpu.SemaphoreType.DMA((copies,)),
            pltpu.SemaphoreType.DMA((8,)),
        ],
        compiler_params=pltpu.CompilerParams(
            collective_id=0, has_side_effects=True, vmem_limit_bytes=42 << 20
        ),
        cost_estimate=pl.CostEstimate(
            flops=8_000_000_000, bytes_accessed=6_000_000, transcendentals=700_000
        ),
        name="latent_backward",
    )(
        in_hbm(prompt),
        in_hbm(suffix),
        in_hbm(queries.reshape(steps, HEADS, QUERY)),
        in_hbm(key_up.reshape(HEADS * NOPE, LATENT)),
        in_hbm(value_up.reshape(HEADS * LATENT, VHEAD)),
        in_hbm(out_grad.reshape(steps, HEADS, VHEAD)),
        in_hbm(fork_prompt),
        in_hbm(suffix_length),
    )
    prompt_grad, suffix_grad, query_grad, key_up_grad, value_up_grad = pl.pallas_call(
        unpack,
        out_shape=(
            jax.ShapeDtypeStruct((2, PKEYS, WIDTH), F32),
            jax.ShapeDtypeStruct((1, SKEYS, WIDTH), F32),
            jax.ShapeDtypeStruct((steps, HEADS, QUERY), F32),
            jax.ShapeDtypeStruct((HEADS * NOPE, LATENT), F32),
            jax.ShapeDtypeStruct((HEADS * LATENT, VHEAD), F32),
        ),
        in_specs=[vmem] * 4,
        out_specs=(vmem,) * 5,
        compiler_params=pltpu.CompilerParams(vmem_limit_bytes=16 << 20),
        name="unpack_grads",
    )(*sums)
    return (
        prompt_grad,
        suffix_grad,
        query_grad.reshape(FORKS, RECOMP, HEADS, QUERY),
        key_up_grad.reshape(HEADS, NOPE, LATENT),
        value_up_grad.reshape(HEADS, LATENT, VHEAD),
    )


def solution(mesh):
    return jax.shard_map(
        shards,
        mesh=mesh,
        in_specs=(
            P(None, ("ctx", "sample"), None),
            P("sample", "ctx", None),
            P(None, None, "sample", None),
            P("sample", None, None),
            P("sample", None, None),
            P(None, None, "sample", None),
            P(),
            P(),
        ),
        out_specs=(
            P(None, ("ctx", "sample"), None),
            P("sample", "ctx", None),
            P(None, None, "sample", None),
            P("sample", None, None),
            P("sample", None, None),
        ),
        check_vma=False,
    )
```

```python
import functools

import jax
import jax.numpy as jnp
from jax import lax
from jax.experimental import pallas as pl
from jax.experimental.pallas import tpu as pltpu
from jax.sharding import PartitionSpec as P

MESH = pl.DeviceIdType.MESH
F32 = jnp.float32
BF16 = jnp.bfloat16
HIDDEN = -1e30

ZL, X, ZH, Y, CORE = 4, 4, 4, 4, 2
FORKS, RECOMP, HEADS = 32, 5, 4
NOPE, ROPE, LATENT, VHEAD = 128, 64, 512, 128
WIDTH = LATENT + ROPE
QUERY = NOPE + ROPE
ROWS = FORKS * RECOMP * HEADS
TILE = 128
TILES = ROWS // TILE
PKEYS, SKEYS = 8, 16
BLOCK = 2 * PKEYS + SKEYS
KEYS = CORE * Y * BLOCK
SCALE = QUERY**-0.5
COLS = LATENT // (X * ZL)
GROUP = COLS // 2
RCOLS = ROPE // X


def dot(a, b):
    return jnp.dot(a, b, preferred_element_type=F32)


def dot_nt(a, b):
    return lax.dot_general(a, b, (((1,), (1,)), ((), ())), preferred_element_type=F32)


class Sems:
    def __init__(self, send, recv):
        self.send, self.recv, self.used, self.started = send, recv, 0, []

    def drain(self, kept):
        while len(self.started) > kept:
            self.started.pop(0).wait_send()

    def copy(self, src, dst, device):
        k = self.used
        self.used += 1
        made = pltpu.make_async_remote_copy(
            src_ref=src,
            dst_ref=dst,
            send_sem=self.send.at[k],
            recv_sem=self.recv.at[k],
            device_id=device,
            device_id_type=MESH,
        )
        made.start()
        self.started.append(made)
        return made


def kernel(
    prompt_any, suffix_any, q_any, ku_any, vu_any, og_any, fork_any, length_any,
    keys_out, value_out, key_up_out, query_out,
    keys, qry, qry_t, lgr, lgr_t, og_exp, qn_exp_t, bias, score, pgrad, peaks,
    acc_t, dif_t, kgrad, stat, stat_all, c1s, c1r, c2s, c2r, c3s, c3h, c3r,
    far_s, far_r, near_s, near_r, lat_m, lat_z, rope_s, rope_r, rope_z, whole, rope_a,
    prompt_ref, suffix_ref, q_ref, ku_ref, vu_ref, og_ref, fork_ref, length_ref,
    send_sem, recv_sem, load_sem,
):
    ctx, sample = lax.axis_index("ctx"), lax.axis_index("sample")
    zl, x = ctx // X, ctx % X
    zh, y, core = sample // (Y * CORE), (sample // CORE) % Y, sample % CORE

    def at(zl_=zl, x_=x, zh_=zh, y_=y, core_=core):
        return (zl_ * X + x_, zh_ * (Y * CORE) + y_ * CORE + core_)

    sibling = at(core_=1 - core)

    def zh_by(d):
        return (zh + d + ZH) % ZH

    def y_by(d):
        return (y + d + Y) % Y

    def x_by(d):
        return (x + d + X) % X

    def zl_by(d):
        return (zl + d + ZL) % ZL

    sems = Sems(send_sem, recv_sem)
    pairs = (
        (prompt_any, prompt_ref), (suffix_any, suffix_ref), (q_any, q_ref), (ku_any, ku_ref),
        (og_any, og_ref), (vu_any, vu_ref), (fork_any, fork_ref), (length_any, length_ref),
    )
    loads = [pltpu.make_async_copy(*pair, load_sem.at[k]) for k, pair in enumerate(pairs)]
    for made in loads[:2]:
        made.start()

    partners = [at(zh_=zh_by(d)) for d in (1, -1)]
    partners += [at(zl_=zl_by(a), x_=x_by(b)) for a in (2, 1, 3, 0) for b in (2, 1, 3, 0) if a + b]
    partners += [at(y_=y_by(d)) for d in (2, 1, 3)]
    partners += [at(y_=y_by(d), core_=1 - core) for d in (2, 1, 3)]
    partners += [sibling]
    barrier = pltpu.get_barrier_semaphore()
    for device in partners:
        pl.semaphore_signal(barrier, inc=1, device_id=device, device_id_type=MESH)
    for made in loads[2:]:
        made.start()
    for made in loads[:2]:
        made.wait()
    own = jnp.concatenate(
        [prompt_ref[0].astype(F32), prompt_ref[1].astype(F32), suffix_ref[0].astype(F32)], 0
    ).astype(BF16)
    keys[zh, core, y] = own
    pl.semaphore_wait(barrier, len(partners))

    from_zh = {}
    from_y = {}
    from_core = {}
    for d in (1, 3):
        block = keys.at[zh, core, y]
        from_zh[d] = [sems.copy(block, block, at(zh_=zh_by(d)))]
    half = BLOCK // 2

    def relay(d, rows):
        from_zh[d][0].wait_recv()
        part = keys.at[zh_by(-d), core, y, rows]
        from_zh.setdefault(2, []).append(sems.copy(part, part, at(zh_=zh_by(d))))

    def spread_y(dz):
        if dz == 2:
            for made in from_zh[dz]:
                made.wait_recv()
        block = keys.at[zh_by(-dz), core, y]
        from_y[dz] = [sems.copy(block, block, at(y_=y_by(d))) for d in (2, 1, 3)]
        if dz == 2:
            from_core[dz] = [
                sems.copy(block, block, at(y_=y_by(d), core_=1 - core)) for d in (2, 1, 3, 0)
            ]

    def to_core(dz):
        for made in from_y[dz]:
            made.wait_recv()
        part = keys.at[zh_by(-dz), core]
        from_core[dz] = [sems.copy(part, part, sibling)]

    spread_y(0)

    lane = lax.broadcasted_iota(jnp.int32, (1, ROWS), 1)
    row_fork = (lane * 3277) >> 16
    row_step = (lane - row_fork * (RECOMP * HEADS)) >> 2

    def project(t, carry):
        rows = pl.ds(pl.multiple_of(t * TILE, TILE), TILE)
        steps = pl.ds(t * (TILE // HEADS), TILE // HEADS)
        q = q_ref[steps].reshape(TILE, QUERY)
        og = og_ref[steps].reshape(TILE, VHEAD)
        head = lax.broadcasted_iota(jnp.int32, (TILE, NOPE), 0) & (HEADS - 1)
        q_nope = q[:, :NOPE]
        zero = jnp.zeros_like(q_nope)
        q_exp = jnp.concatenate([jnp.where(head == h, q_nope, zero) for h in range(HEADS)], 1)
        o_exp = jnp.concatenate([jnp.where(head == h, og, zero) for h in range(HEADS)], 1)
        og_exp[rows, :] = o_exp
        q_t = q_nope.T
        head_t = lax.broadcasted_iota(jnp.int32, (NOPE, TILE), 1) & (HEADS - 1)
        qn_exp_t[:, rows] = jnp.concatenate(
            [jnp.where(head_t == h, q_t, zero) for h in range(HEADS)], 0
        )
        whole = jnp.concatenate([dot(q_exp, ku_ref[...]).astype(BF16), q[:, NOPE:]], 1)
        qry[rows, :] = whole
        qry_t[:, rows] = whole.T
        grad = dot_nt(o_exp[:, :VHEAD], vu_ref[pl.ds(0, LATENT), :])
        for h in range(1, HEADS):
            grad += dot_nt(
                o_exp[:, h * VHEAD : (h + 1) * VHEAD], vu_ref[pl.ds(h * LATENT, LATENT), :]
            )
        grad = grad.astype(BF16)
        lgr[rows, :] = grad
        lgr_t[:, rows] = grad.T
        return carry

    for made in loads[2:]:
        made.wait()
    lax.fori_loop(0, 2, project, 0)
    relay(1, pl.ds(0, half))
    relay(3, pl.ds(half, half))
    spread_y(1)
    spread_y(3)
    lax.fori_loop(2, TILES, project, 0)

    def gather_rows(f, carry):
        limit, prompt = carry
        mine = row_fork == f
        return jnp.where(mine, length_ref[f], limit), jnp.where(mine, fork_ref[f], prompt)

    none = jnp.zeros((1, ROWS), jnp.int32)
    row_limit, row_prompt = lax.fori_loop(0, FORKS, gather_rows, (none, none))
    row_limit = row_limit - RECOMP + row_step
    first = jnp.broadcast_to(jnp.where(row_prompt == 0, 0.0, HIDDEN), (PKEYS, ROWS))
    second = jnp.broadcast_to(jnp.where(row_prompt == 1, 0.0, HIDDEN), (PKEYS, ROWS))
    position = ctx * SKEYS + lax.broadcasted_iota(jnp.int32, (SKEYS, ROWS), 0)

    def make_bias(b, carry):
        bz, bc, by = b // (CORE * Y), (b // Y) % CORE, b % Y
        fork = bz * (Y * CORE) + by * CORE + bc
        last = jnp.where(row_fork == fork, row_limit, -1)
        seen = jnp.where(position <= last, 0.0, HIDDEN)
        bias[bz, pl.ds(pl.multiple_of((bc * Y + by) * BLOCK, BLOCK), BLOCK), :] = (
            jnp.concatenate([first, second, seen], 0)
        )
        return carry

    to_core(0)
    lax.fori_loop(0, Y * CORE * ZH, make_bias, 0)

    def scores_of(dz):
        for made in from_core[dz]:
            made.wait_recv()
        part = zh_by(-dz)
        tile = keys[part].reshape(KEYS, WIDTH)
        s = dot(tile, qry_t[...]) + bias[part]
        peak = jnp.max(s, 0, keepdims=True)
        p = jnp.exp((s - peak) * SCALE)
        score[part] = p
        grad = dot(tile[:, :LATENT], lgr_t[...])
        pgrad[part] = grad
        total = jnp.sum(p, 0, keepdims=True)
        mean = jnp.sum(p * grad, 0, keepdims=True) / total
        peaks[dz] = peak
        return part, peak, total, mean

    def merged(left, right):
        top = jnp.maximum(left[0], right[0])
        shrink_left = jnp.exp((left[0] - top) * SCALE)
        shrink_right = jnp.exp((right[0] - top) * SCALE)
        total_left, total_right = left[1] * shrink_left, right[1] * shrink_right
        total = total_left + total_right
        mean = (total_left * left[2] + total_right * right[2]) / total
        return (top, total, mean), shrink_left, shrink_right

    def sums_of(part, mean):
        tile_t = keys[part].reshape(KEYS, WIDTH).T
        p = score[part]
        return dot(tile_t, p.astype(BF16)), dot(
            tile_t, (p * (pgrad[part] - mean)).astype(BF16)
        )

    def add_sums(state, new, part):
        both, shrink_left, shrink_right = merged(state, new)
        acc, grad = sums_of(part, new[2])
        old = acc_t[...]
        acc_t[...] = shrink_left * old + shrink_right * acc
        dif_t[...] = shrink_left * (dif_t[...] + (state[2] - both[2]) * old) + shrink_right * (
            grad + (new[2] - both[2]) * acc
        )
        return both

    part, *state = scores_of(0)
    acc_t[...], dif_t[...] = sums_of(part, state[2])
    to_core(1)
    to_core(3)
    spread_y(2)
    part, *new = scores_of(1)
    state = add_sums(state, new, part)
    part, *new = scores_of(3)
    state = add_sums(state, new, part)
    for made in from_y[2]:
        made.wait_recv()
    part, *new = scores_of(2)
    (peak, total, mean), _, _ = merged(state, new)

    delta = mean * total
    for t in range(TILES):
        cols = slice(t * TILE, (t + 1) * TILE)
        stat[t : t + 1, :] = peak[:, cols]
        stat[TILES + t : TILES + t + 1, :] = total[:, cols]
        stat[2 * TILES + t : 2 * TILES + t + 1, :] = delta[:, cols]
    stat[3 * TILES : 3 * TILES + 1, :] = jnp.zeros((1, TILE), F32)
    stat_copies = []
    for a in range(ZL):
        for b in range(X):
            if a + b:
                stat_copies.append(
                    sems.copy(stat, stat_all.at[ctx], at(zl_=zl_by(a), x_=x_by(b)))
                )
    stat_all[ctx] = stat[...]

    add_sums(state, new, part)
    ORDER = (2, 1, 3, 0)
    FAR_LANES = (slice(0, 3 * TILE), slice(3 * TILE, ROWS))
    OUT_LANES = (slice(0, ROWS), slice(ROWS, ROWS + HEADS * VHEAD))

    def block_of(to_x, to_zl, g):
        return pl.ds(pl.multiple_of((to_x * ZL + to_zl) * COLS + g * GROUP, GROUP), GROUP)

    far_x = {}
    for g in range(2):
        for e in ORDER:
            to = zl_by(e)
            rows = block_of(x_by(2), to, g)
            far_s[to, g, 0] = acc_t[rows, :].astype(BF16)
            far_s[to, g, 1] = dif_t[rows, :].astype(BF16)
            far_x[e, g] = [
                sems.copy(
                    far_s.at[to, g, :, :, FAR_LANES[k]],
                    far_r.at[to, g, :, :, FAR_LANES[k]],
                    at(x_=x_by(1 - 2 * k)),
                )
                for k in range(2)
            ]
    for b in range(X):
        rows = slice(LATENT + b * RCOLS, LATENT + (b + 1) * RCOLS)
        rope_s[b, 0] = acc_t[rows, :].astype(BF16)
        rope_s[b, 1] = dif_t[rows, :].astype(BF16)
    rope_x = [
        sems.copy(rope_s.at[x_by(d)], rope_r.at[d - 1], at(x_=x_by(d))) for d in (2, 1, 3)
    ]

    for made in stat_copies:
        made.wait_recv()
    all_peak = stat_all[:, 0:TILES, :]
    top = jnp.max(all_peak, 0)
    shrink = jnp.exp((all_peak - top[None]) * SCALE)
    whole_total = jnp.sum(stat_all[:, TILES : 2 * TILES, :] * shrink, 0)
    whole_delta = jnp.sum(stat_all[:, 2 * TILES : 3 * TILES, :] * shrink, 0)
    inverse = 1.0 / whole_total

    def as_row(v):
        return jnp.concatenate([v[t : t + 1, :] for t in range(TILES)], 1)

    def weigh(d):
        if d == 0:
            one = stat
        else:
            one = stat_all.at[zl * X + x_by(-d)]
        factor = jnp.exp((one[0:TILES, :] - top) * SCALE) * inverse
        shift = whole_delta * inverse - one[2 * TILES : 3 * TILES, :] / one[TILES : 2 * TILES, :]
        return as_row(factor), as_row(shift)

    weights = [weigh(d) for d in range(X)]
    top, inverse, row_delta = as_row(top), as_row(inverse), as_row(whole_delta * inverse)

    def weighted(d, acc, dif, lanes=slice(0, ROWS)):
        factor, shift = weights[d][0][:, lanes], weights[d][1][:, lanes]
        return factor * acc, (factor * SCALE) * (dif - shift * acc)

    near_x = {}

    def send_near_x(e, g):
        to = zl_by(e)
        near_x[e, g] = []
        for k in range(2):
            far_x[e, g][k].wait_recv()
            rows = block_of(x_by(1 - 2 * k), to, g)
            own = weighted(0, acc_t[rows, :], dif_t[rows, :])
            added, other = FAR_LANES[k], FAR_LANES[1 - k]
            came = weighted(
                1 + 2 * k,
                far_r[to, g, 0, :, added].astype(F32),
                far_r[to, g, 1, :, added].astype(F32),
                added,
            )
            for i in range(2):
                near_s[k, to, g, i, :, added] = (own[i][:, added] + came[i]).astype(BF16)
                near_s[k, to, g, i, :, other] = own[i][:, other].astype(BF16)
            near_x[e, g].append(
                sems.copy(near_s.at[k, to, g], near_r.at[k, to, g], at(x_=x_by(1 - 2 * k)))
            )

    lat_zl = [[], []]

    def sum_x(e, g):
        for made in near_x[e, g]:
            made.wait_recv()
        to = zl_by(e)
        rows = block_of(x, to, g)
        own = weighted(0, acc_t[rows, :], dif_t[rows, :])
        for i in range(2):
            add = own[i] + near_r[0, to, g, i].astype(F32) + near_r[1, to, g, i].astype(F32)
            lat_m[to, g, i] = add.astype(BF16)
        if e:
            lat_zl[g].append(sems.copy(lat_m.at[to, g], lat_z.at[e - 1, g], at(zl_=to)))

    def sum_rope_x():
        for made in rope_x:
            made.wait_recv()
        rows = pl.ds(pl.multiple_of(LATENT + x * RCOLS, RCOLS), RCOLS)

        grad = weighted(0, acc_t[rows, :], dif_t[rows, :])[1]
        for d in (1, 2, 3):
            grad += weighted(d, rope_r[d - 1, 0].astype(F32), rope_r[d - 1, 1].astype(F32))[1]
        rope_z[zl] = grad.astype(BF16)
        block = rope_z.at[zl]
        return [sems.copy(block, block, at(zl_=zl_by(e))) for e in (2, 1, 3)]

    to_near = {}
    to_far = []

    def spread_x(e, g):
        block = whole.at[block_of(x, zl_by(-e), g), :]
        to_near[e, g] = [sems.copy(block, block, at(x_=x_by(1 - 2 * k))) for k in range(2)]

    def forward_x(e, g):
        for k in range(2):
            to_near[e, g][k].wait_recv()
            block = whole.at[block_of(x_by(2 * k - 1), zl_by(-e), g), OUT_LANES[k]]
            to_far.append(sems.copy(block, block, at(x_=x_by(1 - 2 * k))))

    rope_far = []

    def sum_zl(g):
        for made in lat_zl[g]:
            made.wait_recv()
        out = lat_m[zl, g, 0].astype(F32)
        grad = lat_m[zl, g, 1].astype(F32)
        for i in range(ZL - 1):
            out += lat_z[i, g, 0].astype(F32)
            grad += lat_z[i, g, 1].astype(F32)
        rows = block_of(x, zl, g)
        whole[rows, :ROWS] = grad.astype(BF16)
        whole[rows, ROWS:] = dot(out.astype(BF16), og_exp[...]).astype(BF16)
        block = whole.at[rows, :]
        back = {e: sems.copy(block, block, at(zl_=zl_by(e))) for e in (2, 1, 3)}
        spread_x(0, g)
        return back

    def sum_rope_zl(made):
        for m in made:
            m.wait_recv()
        grad = rope_z[0].astype(F32)
        for i in range(1, ZL):
            grad += rope_z[i].astype(F32)
        rope_a[x] = grad.astype(BF16)
        block = rope_a.at[x]
        for d in (2, 1, 3):
            rope_far.append(sems.copy(block, block, at(x_=x_by(d))))

    def gather_x(back, g):
        done = 0
        for e in (1, 3, 2):
            back[e].wait_recv()
            spread_x(e, g)
            forward_x(done, g)
            done = e

    head_of = lane & (HEADS - 1)

    def finish(d):
        b = x_by(-d)
        cols = pl.ds(pl.multiple_of(b * TILE, TILE), TILE)
        lat = whole[cols, :ROWS]
        key_up_out[b] = dot_nt(qn_exp_t[...], lat)
        value_out[cols, :] = whole[cols, ROWS:]
        spread = dot(ku_ref[:, cols], lat)
        nope = spread[:NOPE, :]
        for h in range(1, HEADS):
            nope = jnp.where(head_of == h, spread[h * NOPE : (h + 1) * NOPE, :], nope)
        return nope

    core_sums, y_sums, zh_sums = {}, {}, {}

    def key_grads(dz):
        part = zh_by(-dz)
        p = score[part] * (jnp.exp((peaks[dz] - top) * SCALE) * inverse)
        sg = (p * (pgrad[part] - row_delta) * SCALE).astype(BF16)
        grad = dot(sg, qry[...])
        value = dot(p.astype(BF16), lgr[...])
        kgrad[part, :, :, :LATENT] = (grad[:, :LATENT] + value).reshape(CORE, Y * BLOCK, LATENT)
        kgrad[part, :, :, LATENT:] = grad[:, LATENT:].reshape(CORE, Y * BLOCK, ROPE)
        c1s[part] = kgrad[part, 1 - core].astype(BF16)
        core_sums[dz] = sems.copy(c1s.at[part], c1r.at[part], sibling)

    def add_cores(dz):
        part = zh_by(-dz)
        core_sums[dz].wait_recv()
        both = kgrad[part, core] + c1r[part].astype(F32)
        kgrad[part, core] = both
        c2s[dz] = both.reshape(Y, BLOCK, WIDTH).astype(BF16)
        y_sums[dz] = [
            sems.copy(c2s.at[dz, y_by(d)], c2r.at[dz, d - 1], at(y_=y_by(d))) for d in (2, 1, 3)
        ]

    def add_ys(dz):
        for made in y_sums[dz]:
            made.wait_recv()
        rows = pl.ds(pl.multiple_of(y * BLOCK, BLOCK), BLOCK)
        mine = kgrad[zh_by(-dz), core, rows, :]
        for i in range(Y - 1):
            mine += c2r[dz, i].astype(F32)
        return mine

    def send_far(mine):
        c3s[2] = mine.astype(BF16)
        return [
            sems.copy(c3s.at[2, pl.ds(0, half)], c3h.at[0], at(zh_=zh_by(1))),
            sems.copy(c3s.at[2, pl.ds(half, half)], c3h.at[1], at(zh_=zh_by(-1))),
        ]

    def send_near(halves, up, down):
        for made in halves:
            made.wait_recv()
        c3s[0, :half] = (up[:half] + c3h[0].astype(F32)).astype(BF16)
        c3s[0, half:] = up[half:].astype(BF16)
        c3s[1, :half] = down[:half].astype(BF16)
        c3s[1, half:] = (down[half:] + c3h[1].astype(F32)).astype(BF16)
        return [
            sems.copy(c3s.at[0], c3r.at[0], at(zh_=zh_by(1))),
            sems.copy(c3s.at[1], c3r.at[1], at(zh_=zh_by(-1))),
        ]

    early = sems.used
    for g in range(2):
        for e in ORDER:
            send_near_x(e, g)
    key_grads(2)
    for e in ORDER:
        sum_x(e, 0)
    key_grads(1)
    add_cores(2)
    for e in ORDER:
        sum_x(e, 1)
    rope_zl = sum_rope_x()
    key_grads(3)
    add_cores(1)
    key_grads(0)
    add_cores(3)
    back_0 = sum_zl(0)
    add_cores(0)
    halves = send_far(add_ys(2))
    sems.drain(sems.used - early)
    back_1 = sum_zl(1)
    middle = sems.used
    sum_rope_zl(rope_zl)
    gather_x(back_0, 0)
    up, down, final = add_ys(3), add_ys(1), add_ys(0)
    near = send_near(halves, up, down)
    gather_x(back_1, 1)
    forward_x(2, 0)
    forward_x(2, 1)
    sems.drain(sems.used - middle)

    nope = finish(0) + finish(1) + finish(3)
    for made in rope_far:
        made.wait_recv()
    for b in range(X):
        query_out[NOPE + b * RCOLS : NOPE + (b + 1) * RCOLS, :] = rope_a[b].astype(F32)
    for made in to_far:
        made.wait_recv()
    query_out[:NOPE, :] = nope + finish(2)
    for made in near:
        made.wait_recv()
    keys_out[...] = final + c3r[0].astype(F32) + c3r[1].astype(F32)
    sems.drain(0)


def unpack(
    keys_ref, value_ref, key_up_ref, query_ref,
    prompt_out, suffix_out, query_out, key_up_out, value_up_out,
    value_f, query_f, sem,
):
    copies = []

    def put(src, dst):
        made = pltpu.make_async_copy(src, dst, sem.at[len(copies)])
        made.start()
        copies.append(made)

    for b in range(X):
        put(key_up_ref.at[b], key_up_out.at[:, pl.ds(b * TILE, TILE)])
    for h in range(HEADS):
        value_f[h] = value_ref[:, h * VHEAD : (h + 1) * VHEAD].astype(F32)
        put(value_f.at[h], value_up_out.at[pl.ds(h * LATENT, LATENT), :])
    prompt_out[0] = keys_ref[:PKEYS, :]
    prompt_out[1] = keys_ref[PKEYS : 2 * PKEYS, :]
    suffix_out[0] = keys_ref[2 * PKEYS :, :]
    steps = TILE // HEADS
    for t in range(TILES):
        part = query_ref[:, t * TILE : (t + 1) * TILE].T
        query_f[t] = part.reshape(steps, HEADS, QUERY)
        put(query_f.at[t], query_out.at[pl.ds(t * steps, steps)])
    for made in copies:
        made.wait()


def shards(prompt, suffix, queries, key_up, value_up, out_grad, fork_prompt, suffix_length):
    vmem = pl.BlockSpec(memory_space=pltpu.VMEM)
    copies = 184
    hbm = pl.BlockSpec(memory_space=pltpu.HBM)

    def in_hbm(v):
        return pltpu.with_memory_space_constraint(v, pltpu.HBM)

    steps = FORKS * RECOMP
    sums = pl.pallas_call(
        kernel,
        out_shape=(
            jax.ShapeDtypeStruct((BLOCK, WIDTH), F32),
            jax.ShapeDtypeStruct((LATENT, HEADS * VHEAD), BF16),
            jax.ShapeDtypeStruct((X, HEADS * NOPE, TILE), F32),
            jax.ShapeDtypeStruct((QUERY, ROWS), F32),
        ),
        in_specs=[hbm] * 8,
        out_specs=(vmem,) * 4,
        scratch_shapes=[
            pltpu.VMEM((ZH, CORE, Y, BLOCK, WIDTH), BF16),
            pltpu.VMEM((ROWS, WIDTH), BF16),
            pltpu.VMEM((WIDTH, ROWS), BF16),
            pltpu.VMEM((ROWS, LATENT), BF16),
            pltpu.VMEM((LATENT, ROWS), BF16),
            pltpu.VMEM((ROWS, HEADS * VHEAD), BF16),
            pltpu.VMEM((HEADS * NOPE, ROWS), BF16),
            pltpu.VMEM((ZH, KEYS, ROWS), F32),
            pltpu.VMEM((ZH, KEYS, ROWS), F32),
            pltpu.VMEM((ZH, KEYS, ROWS), F32),
            pltpu.VMEM((ZH, 1, ROWS), F32),
            pltpu.VMEM((WIDTH, ROWS), F32),
            pltpu.VMEM((WIDTH, ROWS), F32),
            pltpu.VMEM((ZH, CORE, Y * BLOCK, WIDTH), F32),
            pltpu.VMEM((16, TILE), F32),
            pltpu.VMEM((ZL * X, 16, TILE), F32),
            pltpu.VMEM((ZH, Y * BLOCK, WIDTH), BF16),
            pltpu.VMEM((ZH, Y * BLOCK, WIDTH), BF16),
            pltpu.VMEM((ZH, Y, BLOCK, WIDTH), BF16),
            pltpu.VMEM((ZH, Y - 1, BLOCK, WIDTH), BF16),
            pltpu.VMEM((ZH - 1, BLOCK, WIDTH), BF16),
            pltpu.VMEM((2, BLOCK // 2, WIDTH), BF16),
            pltpu.VMEM((2, BLOCK, WIDTH), BF16),
            pltpu.VMEM((ZL, 2, 2, GROUP, ROWS), BF16),
            pltpu.VMEM((ZL, 2, 2, GROUP, ROWS), BF16),
            pltpu.VMEM((2, ZL, 2, 2, GROUP, ROWS), BF16),
            pltpu.VMEM((2, ZL, 2, 2, GROUP, ROWS), BF16),
            pltpu.VMEM((ZL, 2, 2, GROUP, ROWS), BF16),
            pltpu.VMEM((ZL - 1, 2, 2, GROUP, ROWS), BF16),
            pltpu.VMEM((X, 2, RCOLS, ROWS), BF16),
            pltpu.VMEM((X - 1, 2, RCOLS, ROWS), BF16),
            pltpu.VMEM((ZL, RCOLS, ROWS), BF16),
            pltpu.VMEM((LATENT, ROWS + HEADS * VHEAD), BF16),
            pltpu.VMEM((X, RCOLS, ROWS), BF16),
            pltpu.VMEM((2, PKEYS, WIDTH), BF16),
            pltpu.VMEM((1, SKEYS, WIDTH), BF16),
            pltpu.VMEM((steps, HEADS, QUERY), BF16),
            pltpu.VMEM((HEADS * NOPE, LATENT), BF16),
            pltpu.VMEM((HEADS * LATENT, VHEAD), BF16),
            pltpu.VMEM((steps, HEADS, VHEAD), BF16),
            pltpu.SMEM((FORKS,), jnp.int32),
            pltpu.SMEM((FORKS,), jnp.int32),
            pltpu.SemaphoreType.DMA((copies,)),
            pltpu.SemaphoreType.DMA((copies,)),
            pltpu.SemaphoreType.DMA((8,)),
        ],
        compiler_params=pltpu.CompilerParams(
            collective_id=0, has_side_effects=True, vmem_limit_bytes=42 << 20
        ),
        cost_estimate=pl.CostEstimate(
            flops=8_000_000_000, bytes_accessed=6_000_000, transcendentals=700_000
        ),
        name="latent_backward",
    )(
        in_hbm(prompt),
        in_hbm(suffix),
        in_hbm(queries.reshape(steps, HEADS, QUERY)),
        in_hbm(key_up.reshape(HEADS * NOPE, LATENT)),
        in_hbm(value_up.reshape(HEADS * LATENT, VHEAD)),
        in_hbm(out_grad.reshape(steps, HEADS, VHEAD)),
        in_hbm(fork_prompt),
        in_hbm(suffix_length),
    )
    prompt_grad, suffix_grad, query_grad, key_up_grad, value_up_grad = pl.pallas_call(
        unpack,
        out_shape=(
            jax.ShapeDtypeStruct((2, PKEYS, WIDTH), F32),
            jax.ShapeDtypeStruct((1, SKEYS, WIDTH), F32),
            jax.ShapeDtypeStruct((steps, HEADS, QUERY), F32),
            jax.ShapeDtypeStruct((HEADS * NOPE, LATENT), F32),
            jax.ShapeDtypeStruct((HEADS * LATENT, VHEAD), F32),
        ),
        in_specs=[vmem] * 4,
        out_specs=(vmem, vmem, hbm, hbm, hbm),
        scratch_shapes=[
            pltpu.VMEM((HEADS, LATENT, VHEAD), F32),
            pltpu.VMEM((TILES, TILE // HEADS, HEADS, QUERY), F32),
            pltpu.SemaphoreType.DMA((X + HEADS + TILES,)),
        ],
        compiler_params=pltpu.CompilerParams(vmem_limit_bytes=16 << 20),
        name="unpack_grads",
    )(*sums)
    return (
        prompt_grad,
        suffix_grad,
        query_grad.reshape(FORKS, RECOMP, HEADS, QUERY),
        key_up_grad.reshape(HEADS, NOPE, LATENT),
        value_up_grad.reshape(HEADS, LATENT, VHEAD),
    )


def solution(mesh):
    return jax.shard_map(
        shards,
        mesh=mesh,
        in_specs=(
            P(None, ("ctx", "sample"), None),
            P("sample", "ctx", None),
            P(None, None, "sample", None),
            P("sample", None, None),
            P("sample", None, None),
            P(None, None, "sample", None),
            P(),
            P(),
        ),
        out_specs=(
            P(None, ("ctx", "sample"), None),
            P("sample", "ctx", None),
            P(None, None, "sample", None),
            P("sample", None, None),
            P("sample", None, None),
        ),
        check_vma=False,
    )
```

```python
import functools

import jax
import jax.numpy as jnp
from jax import lax
from jax.experimental import pallas as pl
from jax.experimental.pallas import tpu as pltpu
from jax.sharding import PartitionSpec as P

MESH = pl.DeviceIdType.MESH
F32 = jnp.float32
BF16 = jnp.bfloat16
HIDDEN = -1e30

ZL, X, ZH, Y, CORE = 4, 4, 4, 4, 2
FORKS, RECOMP, HEADS = 32, 5, 4
NOPE, ROPE, LATENT, VHEAD = 128, 64, 512, 128
WIDTH = LATENT + ROPE
QUERY = NOPE + ROPE
ROWS = FORKS * RECOMP * HEADS
TILE = 128
TILES = ROWS // TILE
PKEYS, SKEYS = 8, 16
BLOCK = 2 * PKEYS + SKEYS
KEYS = CORE * Y * BLOCK
SCALE = QUERY**-0.5
COLS = LATENT // (X * ZL)
GROUP = COLS // 2
RCOLS = ROPE // X


def dot(a, b):
    return jnp.dot(a, b, preferred_element_type=F32)


def dot_nt(a, b):
    return lax.dot_general(a, b, (((1,), (1,)), ((), ())), preferred_element_type=F32)


class Sems:
    def __init__(self, send, recv):
        self.send, self.recv, self.used, self.started = send, recv, 0, []

    def drain(self, kept):
        while len(self.started) > kept:
            self.started.pop(0).wait_send()

    def copy(self, src, dst, device):
        k = self.used
        self.used += 1
        made = pltpu.make_async_remote_copy(
            src_ref=src,
            dst_ref=dst,
            send_sem=self.send.at[k],
            recv_sem=self.recv.at[k],
            device_id=device,
            device_id_type=MESH,
        )
        made.start()
        self.started.append(made)
        return made


def kernel(
    prompt_any, suffix_any, q_any, ku_any, vu_any, og_any, fork_any, length_any,
    keys_out, value_out, key_up_out, query_out,
    keys, qry, qry_t, lgr, lgr_t, og_exp, qn_exp_t, bias, score, pgrad, peaks,
    acc_t, dif_t, kgrad, stat, stat_all, c1s, c1r, c2s, c2r, c3s, c3h, c3r,
    far_s, far_r, near_s, near_r, lat_m, lat_z, rope_s, rope_r, rope_z, whole, rope_a,
    prompt_ref, suffix_ref, q_ref, ku_ref, vu_ref, og_ref, fork_ref, length_ref,
    send_sem, recv_sem, load_sem,
):
    ctx, sample = lax.axis_index("ctx"), lax.axis_index("sample")
    zl, x = ctx // X, ctx % X
    zh, y, core = sample // (Y * CORE), (sample // CORE) % Y, sample % CORE

    def at(zl_=zl, x_=x, zh_=zh, y_=y, core_=core):
        return (zl_ * X + x_, zh_ * (Y * CORE) + y_ * CORE + core_)

    sibling = at(core_=1 - core)

    def zh_by(d):
        return (zh + d + ZH) % ZH

    def y_by(d):
        return (y + d + Y) % Y

    def x_by(d):
        return (x + d + X) % X

    def zl_by(d):
        return (zl + d + ZL) % ZL

    sems = Sems(send_sem, recv_sem)
    pairs = (
        (prompt_any, prompt_ref), (suffix_any, suffix_ref), (q_any, q_ref), (ku_any, ku_ref),
        (og_any, og_ref), (vu_any, vu_ref), (fork_any, fork_ref), (length_any, length_ref),
    )
    loads = [pltpu.make_async_copy(*pair, load_sem.at[k]) for k, pair in enumerate(pairs)]
    for made in loads[:2]:
        made.start()

    partners = [at(zh_=zh_by(d)) for d in (1, -1)]
    partners += [at(zl_=zl_by(a), x_=x_by(b)) for a in (2, 1, 3, 0) for b in (2, 1, 3, 0) if a + b]
    partners += [at(y_=y_by(d)) for d in (2, 1, 3)]
    partners += [at(y_=y_by(d), core_=1 - core) for d in (2, 1, 3)]
    partners += [sibling]
    barrier = pltpu.get_barrier_semaphore()
    for device in partners:
        pl.semaphore_signal(barrier, inc=1, device_id=device, device_id_type=MESH)
    for made in loads[2:]:
        made.start()
    for made in loads[:2]:
        made.wait()
    own = jnp.concatenate(
        [prompt_ref[0].astype(F32), prompt_ref[1].astype(F32), suffix_ref[0].astype(F32)], 0
    ).astype(BF16)
    keys[zh, core, y] = own
    pl.semaphore_wait(barrier, len(partners))

    from_zh = {}
    from_y = {}
    from_core = {}
    for d in (1, 3):
        block = keys.at[zh, core, y]
        from_zh[d] = [sems.copy(block, block, at(zh_=zh_by(d)))]
    half = BLOCK // 2

    def relay(d, rows):
        from_zh[d][0].wait_recv()
        part = keys.at[zh_by(-d), core, y, rows]
        from_zh.setdefault(2, []).append(sems.copy(part, part, at(zh_=zh_by(d))))

    def spread_y(dz):
        if dz == 2:
            for made in from_zh[dz]:
                made.wait_recv()
        block = keys.at[zh_by(-dz), core, y]
        from_y[dz] = [sems.copy(block, block, at(y_=y_by(d))) for d in (2, 1, 3)]
        if dz == 2:
            from_core[dz] = [
                sems.copy(block, block, at(y_=y_by(d), core_=1 - core)) for d in (2, 1, 3, 0)
            ]

    def to_core(dz):
        for made in from_y[dz]:
            made.wait_recv()
        part = keys.at[zh_by(-dz), core]
        from_core[dz] = [sems.copy(part, part, sibling)]

    spread_y(0)

    lane = lax.broadcasted_iota(jnp.int32, (1, ROWS), 1)
    row_fork = (lane * 3277) >> 16
    row_step = (lane - row_fork * (RECOMP * HEADS)) >> 2

    def project(t, carry):
        rows = pl.ds(pl.multiple_of(t * TILE, TILE), TILE)
        steps = pl.ds(t * (TILE // HEADS), TILE // HEADS)
        q = q_ref[steps].reshape(TILE, QUERY)
        og = og_ref[steps].reshape(TILE, VHEAD)
        head = lax.broadcasted_iota(jnp.int32, (TILE, NOPE), 0) & (HEADS - 1)
        q_nope = q[:, :NOPE]
        zero = jnp.zeros_like(q_nope)
        q_exp = jnp.concatenate([jnp.where(head == h, q_nope, zero) for h in range(HEADS)], 1)
        o_exp = jnp.concatenate([jnp.where(head == h, og, zero) for h in range(HEADS)], 1)
        og_exp[rows, :] = o_exp
        q_t = q_nope.T
        head_t = lax.broadcasted_iota(jnp.int32, (NOPE, TILE), 1) & (HEADS - 1)
        qn_exp_t[:, rows] = jnp.concatenate(
            [jnp.where(head_t == h, q_t, zero) for h in range(HEADS)], 0
        )
        whole = jnp.concatenate([dot(q_exp, ku_ref[...]).astype(BF16), q[:, NOPE:]], 1)
        qry[rows, :] = whole
        qry_t[:, rows] = whole.T
        grad = dot_nt(o_exp[:, :VHEAD], vu_ref[pl.ds(0, LATENT), :])
        for h in range(1, HEADS):
            grad += dot_nt(
                o_exp[:, h * VHEAD : (h + 1) * VHEAD], vu_ref[pl.ds(h * LATENT, LATENT), :]
            )
        grad = grad.astype(BF16)
        lgr[rows, :] = grad
        lgr_t[:, rows] = grad.T
        return carry

    relay(1, pl.ds(0, half))
    relay(3, pl.ds(half, half))
    spread_y(1)
    spread_y(3)
    for made in loads[2:]:
        made.wait()
    lax.fori_loop(0, TILES, project, 0)

    def gather_rows(f, carry):
        limit, prompt = carry
        mine = row_fork == f
        return jnp.where(mine, length_ref[f], limit), jnp.where(mine, fork_ref[f], prompt)

    none = jnp.zeros((1, ROWS), jnp.int32)
    row_limit, row_prompt = lax.fori_loop(0, FORKS, gather_rows, (none, none))
    row_limit = row_limit - RECOMP + row_step
    first = jnp.broadcast_to(jnp.where(row_prompt == 0, 0.0, HIDDEN), (PKEYS, ROWS))
    second = jnp.broadcast_to(jnp.where(row_prompt == 1, 0.0, HIDDEN), (PKEYS, ROWS))
    position = ctx * SKEYS + lax.broadcasted_iota(jnp.int32, (SKEYS, ROWS), 0)

    def make_bias(b, carry):
        bz, bc, by = b // (CORE * Y), (b // Y) % CORE, b % Y
        fork = bz * (Y * CORE) + by * CORE + bc
        last = jnp.where(row_fork == fork, row_limit, -1)
        seen = jnp.where(position <= last, 0.0, HIDDEN)
        bias[bz, pl.ds(pl.multiple_of((bc * Y + by) * BLOCK, BLOCK), BLOCK), :] = (
            jnp.concatenate([first, second, seen], 0)
        )
        return carry

    to_core(0)
    lax.fori_loop(0, Y * CORE * ZH, make_bias, 0)

    def scores_of(dz):
        for made in from_core[dz]:
            made.wait_recv()
        part = zh_by(-dz)
        tile = keys[part].reshape(KEYS, WIDTH)
        s = dot(tile, qry_t[...]) + bias[part]
        peak = jnp.max(s, 0, keepdims=True)
        p = jnp.exp((s - peak) * SCALE)
        score[part] = p
        grad = dot(tile[:, :LATENT], lgr_t[...])
        pgrad[part] = grad
        total = jnp.sum(p, 0, keepdims=True)
        mean = jnp.sum(p * grad, 0, keepdims=True) / total
        peaks[dz] = peak
        return part, peak, total, mean

    def merged(left, right):
        top = jnp.maximum(left[0], right[0])
        shrink_left = jnp.exp((left[0] - top) * SCALE)
        shrink_right = jnp.exp((right[0] - top) * SCALE)
        total_left, total_right = left[1] * shrink_left, right[1] * shrink_right
        total = total_left + total_right
        mean = (total_left * left[2] + total_right * right[2]) / total
        return (top, total, mean), shrink_left, shrink_right

    def sums_of(part, mean):
        tile_t = keys[part].reshape(KEYS, WIDTH).T
        p = score[part]
        return dot(tile_t, p.astype(BF16)), dot(
            tile_t, (p * (pgrad[part] - mean)).astype(BF16)
        )

    def add_sums(state, new, part):
        both, shrink_left, shrink_right = merged(state, new)
        acc, grad = sums_of(part, new[2])
        old = acc_t[...]
        acc_t[...] = shrink_left * old + shrink_right * acc
        dif_t[...] = shrink_left * (dif_t[...] + (state[2] - both[2]) * old) + shrink_right * (
            grad + (new[2] - both[2]) * acc
        )
        return both

    part, *state = scores_of(0)
    acc_t[...], dif_t[...] = sums_of(part, state[2])
    to_core(1)
    to_core(3)
    spread_y(2)
    part, *new = scores_of(1)
    state = add_sums(state, new, part)
    part, *new = scores_of(3)
    state = add_sums(state, new, part)
    for made in from_y[2]:
        made.wait_recv()
    part, *new = scores_of(2)
    (peak, total, mean), _, _ = merged(state, new)

    delta = mean * total
    for t in range(TILES):
        cols = slice(t * TILE, (t + 1) * TILE)
        stat[t : t + 1, :] = peak[:, cols]
        stat[TILES + t : TILES + t + 1, :] = total[:, cols]
        stat[2 * TILES + t : 2 * TILES + t + 1, :] = delta[:, cols]
    stat[3 * TILES : 3 * TILES + 1, :] = jnp.zeros((1, TILE), F32)
    stat_copies = []
    for a in range(ZL):
        for b in range(X):
            if a + b:
                stat_copies.append(
                    sems.copy(stat, stat_all.at[ctx], at(zl_=zl_by(a), x_=x_by(b)))
                )
    stat_all[ctx] = stat[...]

    add_sums(state, new, part)
    ORDER = (2, 1, 3, 0)
    FAR_LANES = (slice(0, 3 * TILE), slice(3 * TILE, ROWS))
    OUT_LANES = (slice(0, ROWS), slice(ROWS, ROWS + HEADS * VHEAD))

    def block_of(to_x, to_zl, g):
        return pl.ds(pl.multiple_of((to_x * ZL + to_zl) * COLS + g * GROUP, GROUP), GROUP)

    far_x = {}
    for g in range(2):
        for e in ORDER:
            to = zl_by(e)
            rows = block_of(x_by(2), to, g)
            far_s[to, g, 0] = acc_t[rows, :].astype(BF16)
            far_s[to, g, 1] = dif_t[rows, :].astype(BF16)
            far_x[e, g] = [
                sems.copy(
                    far_s.at[to, g, :, :, FAR_LANES[k]],
                    far_r.at[to, g, :, :, FAR_LANES[k]],
                    at(x_=x_by(1 - 2 * k)),
                )
                for k in range(2)
            ]
    for b in range(X):
        rows = slice(LATENT + b * RCOLS, LATENT + (b + 1) * RCOLS)
        rope_s[b, 0] = acc_t[rows, :].astype(BF16)
        rope_s[b, 1] = dif_t[rows, :].astype(BF16)
    rope_x = [
        sems.copy(rope_s.at[x_by(d)], rope_r.at[d - 1], at(x_=x_by(d))) for d in (2, 1, 3)
    ]

    for made in stat_copies:
        made.wait_recv()
    all_peak = stat_all[:, 0:TILES, :]
    top = jnp.max(all_peak, 0)
    shrink = jnp.exp((all_peak - top[None]) * SCALE)
    whole_total = jnp.sum(stat_all[:, TILES : 2 * TILES, :] * shrink, 0)
    whole_delta = jnp.sum(stat_all[:, 2 * TILES : 3 * TILES, :] * shrink, 0)
    inverse = 1.0 / whole_total

    def as_row(v):
        return jnp.concatenate([v[t : t + 1, :] for t in range(TILES)], 1)

    def weigh(d):
        if d == 0:
            one = stat
        else:
            one = stat_all.at[zl * X + x_by(-d)]
        factor = jnp.exp((one[0:TILES, :] - top) * SCALE) * inverse
        shift = whole_delta * inverse - one[2 * TILES : 3 * TILES, :] / one[TILES : 2 * TILES, :]
        return as_row(factor), as_row(shift)

    weights = [weigh(d) for d in range(X)]
    top, inverse, row_delta = as_row(top), as_row(inverse), as_row(whole_delta * inverse)

    def weighted(d, acc, dif, lanes=slice(0, ROWS)):
        factor, shift = weights[d][0][:, lanes], weights[d][1][:, lanes]
        return factor * acc, (factor * SCALE) * (dif - shift * acc)

    near_x = {}

    def send_near_x(e, g):
        to = zl_by(e)
        near_x[e, g] = []
        for k in range(2):
            far_x[e, g][k].wait_recv()
            rows = block_of(x_by(1 - 2 * k), to, g)
            own = weighted(0, acc_t[rows, :], dif_t[rows, :])
            added, other = FAR_LANES[k], FAR_LANES[1 - k]
            came = weighted(
                1 + 2 * k,
                far_r[to, g, 0, :, added].astype(F32),
                far_r[to, g, 1, :, added].astype(F32),
                added,
            )
            for i in range(2):
                near_s[k, to, g, i, :, added] = (own[i][:, added] + came[i]).astype(BF16)
                near_s[k, to, g, i, :, other] = own[i][:, other].astype(BF16)
            near_x[e, g].append(
                sems.copy(near_s.at[k, to, g], near_r.at[k, to, g], at(x_=x_by(1 - 2 * k)))
            )

    lat_zl = [[], []]

    def sum_x(e, g):
        for made in near_x[e, g]:
            made.wait_recv()
        to = zl_by(e)
        rows = block_of(x, to, g)
        own = weighted(0, acc_t[rows, :], dif_t[rows, :])
        for i in range(2):
            add = own[i] + near_r[0, to, g, i].astype(F32) + near_r[1, to, g, i].astype(F32)
            lat_m[to, g, i] = add.astype(BF16)
        if e:
            lat_zl[g].append(sems.copy(lat_m.at[to, g], lat_z.at[e - 1, g], at(zl_=to)))

    def sum_rope_x():
        for made in rope_x:
            made.wait_recv()
        rows = pl.ds(pl.multiple_of(LATENT + x * RCOLS, RCOLS), RCOLS)

        grad = weighted(0, acc_t[rows, :], dif_t[rows, :])[1]
        for d in (1, 2, 3):
            grad += weighted(d, rope_r[d - 1, 0].astype(F32), rope_r[d - 1, 1].astype(F32))[1]
        rope_z[zl] = grad.astype(BF16)
        block = rope_z.at[zl]
        return [sems.copy(block, block, at(zl_=zl_by(e))) for e in (2, 1, 3)]

    to_near = {}
    to_far = []

    def spread_x(e, g):
        block = whole.at[block_of(x, zl_by(-e), g), :]
        to_near[e, g] = [sems.copy(block, block, at(x_=x_by(1 - 2 * k))) for k in range(2)]

    def forward_x(e, g):
        for k in range(2):
            to_near[e, g][k].wait_recv()
            block = whole.at[block_of(x_by(2 * k - 1), zl_by(-e), g), OUT_LANES[k]]
            to_far.append(sems.copy(block, block, at(x_=x_by(1 - 2 * k))))

    rope_far = []

    def sum_zl(g):
        for made in lat_zl[g]:
            made.wait_recv()
        out = lat_m[zl, g, 0].astype(F32)
        grad = lat_m[zl, g, 1].astype(F32)
        for i in range(ZL - 1):
            out += lat_z[i, g, 0].astype(F32)
            grad += lat_z[i, g, 1].astype(F32)
        rows = block_of(x, zl, g)
        whole[rows, :ROWS] = grad.astype(BF16)
        whole[rows, ROWS:] = dot(out.astype(BF16), og_exp[...]).astype(BF16)
        block = whole.at[rows, :]
        back = {e: sems.copy(block, block, at(zl_=zl_by(e))) for e in (2, 1, 3)}
        spread_x(0, g)
        return back

    def sum_rope_zl(made):
        for m in made:
            m.wait_recv()
        grad = rope_z[0].astype(F32)
        for i in range(1, ZL):
            grad += rope_z[i].astype(F32)
        rope_a[x] = grad.astype(BF16)
        block = rope_a.at[x]
        for d in (2, 1, 3):
            rope_far.append(sems.copy(block, block, at(x_=x_by(d))))

    def gather_x(back, g):
        done = 0
        for e in (1, 3, 2):
            back[e].wait_recv()
            spread_x(e, g)
            forward_x(done, g)
            done = e

    head_of = lane & (HEADS - 1)

    def finish(d):
        b = x_by(-d)
        cols = pl.ds(pl.multiple_of(b * TILE, TILE), TILE)
        lat = whole[cols, :ROWS]
        key_up_out[b] = dot_nt(qn_exp_t[...], lat)
        value_out[cols, :] = whole[cols, ROWS:]
        spread = dot(ku_ref[:, cols], lat)
        nope = spread[:NOPE, :]
        for h in range(1, HEADS):
            nope = jnp.where(head_of == h, spread[h * NOPE : (h + 1) * NOPE, :], nope)
        return nope

    core_sums, y_sums, zh_sums = {}, {}, {}

    def key_grads(dz):
        part = zh_by(-dz)
        p = score[part] * (jnp.exp((peaks[dz] - top) * SCALE) * inverse)
        sg = (p * (pgrad[part] - row_delta) * SCALE).astype(BF16)
        grad = dot(sg, qry[...])
        value = dot(p.astype(BF16), lgr[...])
        kgrad[part, :, :, :LATENT] = (grad[:, :LATENT] + value).reshape(CORE, Y * BLOCK, LATENT)
        kgrad[part, :, :, LATENT:] = grad[:, LATENT:].reshape(CORE, Y * BLOCK, ROPE)
        c1s[part] = kgrad[part, 1 - core].astype(BF16)
        core_sums[dz] = sems.copy(c1s.at[part], c1r.at[part], sibling)

    def add_cores(dz):
        part = zh_by(-dz)
        core_sums[dz].wait_recv()
        both = kgrad[part, core] + c1r[part].astype(F32)
        kgrad[part, core] = both
        c2s[dz] = both.reshape(Y, BLOCK, WIDTH).astype(BF16)
        y_sums[dz] = [
            sems.copy(c2s.at[dz, y_by(d)], c2r.at[dz, d - 1], at(y_=y_by(d))) for d in (2, 1, 3)
        ]

    def add_ys(dz):
        for made in y_sums[dz]:
            made.wait_recv()
        rows = pl.ds(pl.multiple_of(y * BLOCK, BLOCK), BLOCK)
        mine = kgrad[zh_by(-dz), core, rows, :]
        for i in range(Y - 1):
            mine += c2r[dz, i].astype(F32)
        return mine

    def send_far(mine):
        c3s[2] = mine.astype(BF16)
        return [
            sems.copy(c3s.at[2, pl.ds(0, half)], c3h.at[0], at(zh_=zh_by(1))),
            sems.copy(c3s.at[2, pl.ds(half, half)], c3h.at[1], at(zh_=zh_by(-1))),
        ]

    def send_near(halves, up, down):
        for made in halves:
            made.wait_recv()
        c3s[0, :half] = (up[:half] + c3h[0].astype(F32)).astype(BF16)
        c3s[0, half:] = up[half:].astype(BF16)
        c3s[1, :half] = down[:half].astype(BF16)
        c3s[1, half:] = (down[half:] + c3h[1].astype(F32)).astype(BF16)
        return [
            sems.copy(c3s.at[0], c3r.at[0], at(zh_=zh_by(1))),
            sems.copy(c3s.at[1], c3r.at[1], at(zh_=zh_by(-1))),
        ]

    early = sems.used
    for g in range(2):
        for e in ORDER:
            send_near_x(e, g)
    key_grads(2)
    for e in ORDER:
        sum_x(e, 0)
    key_grads(1)
    add_cores(2)
    for e in ORDER:
        sum_x(e, 1)
    rope_zl = sum_rope_x()
    key_grads(3)
    add_cores(1)
    key_grads(0)
    add_cores(3)
    back_0 = sum_zl(0)
    add_cores(0)
    halves = send_far(add_ys(2))
    sems.drain(sems.used - early)
    back_1 = sum_zl(1)
    middle = sems.used
    sum_rope_zl(rope_zl)
    gather_x(back_0, 0)
    up, down, final = add_ys(3), add_ys(1), add_ys(0)
    near = send_near(halves, up, down)
    gather_x(back_1, 1)
    forward_x(2, 0)
    forward_x(2, 1)
    sems.drain(sems.used - middle)

    nope = finish(0) + finish(1) + finish(3)
    for made in rope_far:
        made.wait_recv()
    for b in range(X):
        query_out[NOPE + b * RCOLS : NOPE + (b + 1) * RCOLS, :] = rope_a[b].astype(F32)
    for made in to_far:
        made.wait_recv()
    query_out[:NOPE, :] = nope + finish(2)
    for made in near:
        made.wait_recv()
    keys_out[...] = final + c3r[0].astype(F32) + c3r[1].astype(F32)
    sems.drain(0)


def unpack(
    keys_ref, value_ref, key_up_ref, query_ref,
    prompt_out, suffix_out, query_out, key_up_out, value_up_out,
):
    prompt_out[0] = keys_ref[:PKEYS, :]
    prompt_out[1] = keys_ref[PKEYS : 2 * PKEYS, :]
    suffix_out[0] = keys_ref[2 * PKEYS :, :]
    for h in range(HEADS):
        value_up_out[h * LATENT : (h + 1) * LATENT, :] = value_ref[
            :, h * VHEAD : (h + 1) * VHEAD
        ].astype(F32)
    for b in range(X):
        key_up_out[:, b * TILE : (b + 1) * TILE] = key_up_ref[b]
    steps = TILE // HEADS
    for t in range(TILES):
        part = query_ref[:, t * TILE : (t + 1) * TILE].T
        query_out[t * steps : (t + 1) * steps] = part.reshape(steps, HEADS, QUERY)


def shards(prompt, suffix, queries, key_up, value_up, out_grad, fork_prompt, suffix_length):
    vmem = pl.BlockSpec(memory_space=pltpu.VMEM)
    copies = 184
    hbm = pl.BlockSpec(memory_space=pltpu.HBM)

    def in_hbm(v):
        return pltpu.with_memory_space_constraint(v, pltpu.HBM)

    steps = FORKS * RECOMP
    sums = pl.pallas_call(
        kernel,
        out_shape=(
            jax.ShapeDtypeStruct((BLOCK, WIDTH), F32),
            jax.ShapeDtypeStruct((LATENT, HEADS * VHEAD), BF16),
            jax.ShapeDtypeStruct((X, HEADS * NOPE, TILE), F32),
            jax.ShapeDtypeStruct((QUERY, ROWS), F32),
        ),
        in_specs=[hbm] * 8,
        out_specs=(vmem,) * 4,
        scratch_shapes=[
            pltpu.VMEM((ZH, CORE, Y, BLOCK, WIDTH), BF16),
            pltpu.VMEM((ROWS, WIDTH), BF16),
            pltpu.VMEM((WIDTH, ROWS), BF16),
            pltpu.VMEM((ROWS, LATENT), BF16),
            pltpu.VMEM((LATENT, ROWS), BF16),
            pltpu.VMEM((ROWS, HEADS * VHEAD), BF16),
            pltpu.VMEM((HEADS * NOPE, ROWS), BF16),
            pltpu.VMEM((ZH, KEYS, ROWS), F32),
            pltpu.VMEM((ZH, KEYS, ROWS), F32),
            pltpu.VMEM((ZH, KEYS, ROWS), F32),
            pltpu.VMEM((ZH, 1, ROWS), F32),
            pltpu.VMEM((WIDTH, ROWS), F32),
            pltpu.VMEM((WIDTH, ROWS), F32),
            pltpu.VMEM((ZH, CORE, Y * BLOCK, WIDTH), F32),
            pltpu.VMEM((16, TILE), F32),
            pltpu.VMEM((ZL * X, 16, TILE), F32),
            pltpu.VMEM((ZH, Y * BLOCK, WIDTH), BF16),
            pltpu.VMEM((ZH, Y * BLOCK, WIDTH), BF16),
            pltpu.VMEM((ZH, Y, BLOCK, WIDTH), BF16),
            pltpu.VMEM((ZH, Y - 1, BLOCK, WIDTH), BF16),
            pltpu.VMEM((ZH - 1, BLOCK, WIDTH), BF16),
            pltpu.VMEM((2, BLOCK // 2, WIDTH), BF16),
            pltpu.VMEM((2, BLOCK, WIDTH), BF16),
            pltpu.VMEM((ZL, 2, 2, GROUP, ROWS), BF16),
            pltpu.VMEM((ZL, 2, 2, GROUP, ROWS), BF16),
            pltpu.VMEM((2, ZL, 2, 2, GROUP, ROWS), BF16),
            pltpu.VMEM((2, ZL, 2, 2, GROUP, ROWS), BF16),
            pltpu.VMEM((ZL, 2, 2, GROUP, ROWS), BF16),
            pltpu.VMEM((ZL - 1, 2, 2, GROUP, ROWS), BF16),
            pltpu.VMEM((X, 2, RCOLS, ROWS), BF16),
            pltpu.VMEM((X - 1, 2, RCOLS, ROWS), BF16),
            pltpu.VMEM((ZL, RCOLS, ROWS), BF16),
            pltpu.VMEM((LATENT, ROWS + HEADS * VHEAD), BF16),
            pltpu.VMEM((X, RCOLS, ROWS), BF16),
            pltpu.VMEM((2, PKEYS, WIDTH), BF16),
            pltpu.VMEM((1, SKEYS, WIDTH), BF16),
            pltpu.VMEM((steps, HEADS, QUERY), BF16),
            pltpu.VMEM((HEADS * NOPE, LATENT), BF16),
            pltpu.VMEM((HEADS * LATENT, VHEAD), BF16),
            pltpu.VMEM((steps, HEADS, VHEAD), BF16),
            pltpu.SMEM((FORKS,), jnp.int32),
            pltpu.SMEM((FORKS,), jnp.int32),
            pltpu.SemaphoreType.DMA((copies,)),
            pltpu.SemaphoreType.DMA((copies,)),
            pltpu.SemaphoreType.DMA((8,)),
        ],
        compiler_params=pltpu.CompilerParams(
            collective_id=0, has_side_effects=True, vmem_limit_bytes=42 << 20
        ),
        cost_estimate=pl.CostEstimate(
            flops=8_000_000_000, bytes_accessed=6_000_000, transcendentals=700_000
        ),
        name="latent_backward",
    )(
        in_hbm(prompt),
        in_hbm(suffix),
        in_hbm(queries.reshape(steps, HEADS, QUERY)),
        in_hbm(key_up.reshape(HEADS * NOPE, LATENT)),
        in_hbm(value_up.reshape(HEADS * LATENT, VHEAD)),
        in_hbm(out_grad.reshape(steps, HEADS, VHEAD)),
        in_hbm(fork_prompt),
        in_hbm(suffix_length),
    )
    prompt_grad, suffix_grad, query_grad, key_up_grad, value_up_grad = pl.pallas_call(
        unpack,
        out_shape=(
            jax.ShapeDtypeStruct((2, PKEYS, WIDTH), F32),
            jax.ShapeDtypeStruct((1, SKEYS, WIDTH), F32),
            jax.ShapeDtypeStruct((steps, HEADS, QUERY), F32),
            jax.ShapeDtypeStruct((HEADS * NOPE, LATENT), F32),
            jax.ShapeDtypeStruct((HEADS * LATENT, VHEAD), F32),
        ),
        in_specs=[vmem] * 4,
        out_specs=(vmem,) * 5,
        compiler_params=pltpu.CompilerParams(vmem_limit_bytes=16 << 20),
        name="unpack_grads",
    )(*sums)
    return (
        prompt_grad,
        suffix_grad,
        query_grad.reshape(FORKS, RECOMP, HEADS, QUERY),
        key_up_grad.reshape(HEADS, NOPE, LATENT),
        value_up_grad.reshape(HEADS, LATENT, VHEAD),
    )


def solution(mesh):
    return jax.shard_map(
        shards,
        mesh=mesh,
        in_specs=(
            P(None, ("ctx", "sample"), None),
            P("sample", "ctx", None),
            P(None, None, "sample", None),
            P("sample", None, None),
            P("sample", None, None),
            P(None, None, "sample", None),
            P(),
            P(),
        ),
        out_specs=(
            P(None, ("ctx", "sample"), None),
            P("sample", "ctx", None),
            P(None, None, "sample", None),
            P("sample", None, None),
            P("sample", None, None),
        ),
        check_vma=False,
    )
```
